32 devices in a mesh: items: 8 (over z, x), frames: 4 (over y, core).
Axes of the slice: x: 2, y: 2, z: 4, core: 2. Of those that a mesh axis runs over, the one named last changes fastest.
Arguments:
- frames_in: bfloat16 [64, 1024, 768], P('items', 'frames'), may hold values from -6 to 6
- cond: bfloat16 [64, 768], P('items'), may hold values from -6 to 6
- text: bfloat16 [64, 256, 768], P('items', 'frames'), may hold values from -6 to 6
- item_lengths: int32 [64], P('items'), may hold values from 256 to 1024, as said below
- text_lengths: int32 [64], P('items'), may hold values from 64 to 256, as said below
- ada_weight: bfloat16 [768, 6912], replicated, may hold values from -0.21875 to 0.21875
- qkv_weight: bfloat16 [768, 2304], replicated, may hold values from -0.21875 to 0.21875
- out_weight: bfloat16 [768, 768], replicated, may hold values from -0.875 to 0.875
- cross_q_weight: bfloat16 [768, 768], replicated, may hold values from -0.21875 to 0.21875
- cross_kv_weight: bfloat16 [768, 1536], replicated, may hold values from -0.21875 to 0.21875
- cross_out_weight: bfloat16 [768, 768], replicated, may hold values from -0.625 to 0.625
- up_weight: bfloat16 [768, 3072], replicated, may hold values from -0.21875 to 0.21875
- down_weight: bfloat16 [3072, 768], replicated, may hold values from -0.109375 to 0.109375
- cotangent: bfloat16 [64, 1024, 768], P('items', 'frames'), may hold values from -6 to 6
Outputs:
- layer_out: bfloat16 [64, 1024, 768], P('items', 'frames')
- input_grad: float32 [64, 1024, 768], P('items', 'frames')
- text_grad: float32 [64, 256, 768], P('items', 'frames')
- cond_grad: float32 [64, 768], P('items', 'frames')
- grad_ada: float32 [768, 6912], P('items', 'frames')
- grad_qkv: float32 [768, 2304], P('items', 'frames')
- grad_out: float32 [768, 768], P('items', 'frames')
- grad_cross_q: float32 [768, 768], P('items', 'frames')
- grad_cross_kv: float32 [768, 1536], P('items', 'frames')
- grad_cross_out: float32 [768, 768], P('items', 'frames')
- grad_up: float32 [768, 3072], P('items', 'frames')
- grad_down: float32 [3072, 768], P('items', 'frames')
The draws below stay inside these ranges and needn't reach their ends.
Inputs may be any that keep to these rules, and one draw needn't show every extreme that they name: `item_lengths`: each item has 1024, 512 or 256 frames; of every 8 consecutive items one has all 1024. `text_lengths`: of every 8 consecutive items one has all 256 text tokens.
All inputs are finite; a program needn't handle non-finite values.
Results may differ from the reference program's by a relative error of at most 0.025.
Values may be sent and summed in bfloat16 or wider, within the bound.
No kernel may reach another device: no remote copies, remote signals or barrier semaphores. Data moves between devices by JAX's collectives and lax.ppermute only.
A program may use at most 640 MiB of HBM per device.

```python
import jax
import jax.numpy as jnp
from jax import lax

D = 768
H = 12
HD = 64
FF = 3072
LT = 256
LEN = 1024
ITEMS_DEV = 8
ITEMS = 64


def draw_item_lengths(key, part):
    key = jax.random.fold_in(key, 11)
    buckets = jax.random.randint(key, (ITEMS,), 0, 3)
    chosen = jax.random.randint(jax.random.fold_in(key, 5), (ITEMS // ITEMS_DEV,), 0, ITEMS_DEV)
    places = jnp.arange(ITEMS // ITEMS_DEV, dtype=jnp.int32) * ITEMS_DEV + chosen
    buckets = buckets.at[places].set(0)
    return jnp.where(buckets == 0, LEN, jnp.where(buckets == 1, LEN // 2, LEN // 4)).astype(jnp.int32)


def draw_text_lengths(key, part):
    key = jax.random.fold_in(key, 23)
    lengths = jax.random.randint(key, (ITEMS,), LT // 4, LT + 1)
    chosen = jax.random.randint(jax.random.fold_in(key, 7), (ITEMS // ITEMS_DEV,), 0, ITEMS_DEV)
    places = jnp.arange(ITEMS // ITEMS_DEV, dtype=jnp.int32) * ITEMS_DEV + chosen
    return lengths.at[places].set(LT).astype(jnp.int32)


def block_scale(stream_key, extent, cuts, smallest, top_value):
    def one(axis_at, parts):
        draws = jax.random.uniform(jax.random.fold_in(jax.random.fold_in(stream_key, 6), axis_at), (parts,), jnp.float32, smallest / len(cuts), top_value / len(cuts))
        return jnp.repeat(jnp.exp(draws), extent[axis_at] // parts).reshape((-1,) + (1,) * (len(extent) - axis_at - 1))

    gain = one(*cuts[0])
    for cut in cuts[1:]:
        gain = gain * one(*cut)
    return gain


def gaussian(own_key, extent, deviation, limit, cuts=(), kind=jnp.bfloat16):
    loudness = block_scale(own_key, extent, cuts, -0.22, 0.18) if cuts else 1.0
    values = jax.random.normal(own_key, extent, jnp.float32) * deviation * loudness
    return jnp.minimum(jnp.maximum(values, -limit), limit).astype(kind)


def setup_inputs(seed: int = 0) -> dict:
    key_of = jax.random.split(jax.random.key(seed), 15)
    frames_in = gaussian(key_of[0], (ITEMS, LEN, D), 1.0, 6.0, ((0, 8), (1, 4)))
    cond = gaussian(key_of[1], (ITEMS, D), 1.0, 6.0, ((0, 8),))
    text = gaussian(key_of[2], (ITEMS, LT, D), 1.0, 6.0, ((0, 8), (1, 4)))
    item_lengths = draw_item_lengths(jax.random.fold_in(key_of[14], 71), 0)
    text_lengths = draw_text_lengths(jax.random.fold_in(key_of[14], 71), 0)
    ada_weight = gaussian(key_of[5], (D, 9 * D), D ** -0.5, 0.21875)
    qkv_weight = gaussian(key_of[6], (D, 3 * D), D ** -0.5, 0.21875)
    out_weight = gaussian(key_of[7], (D, D), (D // 16) ** -0.5, 0.875)
    cross_q_weight = gaussian(key_of[8], (D, D), D ** -0.5, 0.21875)
    cross_kv_weight = gaussian(key_of[9], (D, 2 * D), D ** -0.5, 0.21875)
    cross_out_weight = gaussian(key_of[10], (D, D), (D // 8) ** -0.5, 0.625)
    up_weight = gaussian(key_of[11], (D, FF), D ** -0.5, 0.21875)
    down_weight = gaussian(key_of[12], (FF, D), FF ** -0.5, 0.109375)
    cotangent = gaussian(key_of[13], (ITEMS, LEN, D), 1.0, 6.0, ((0, 8), (1, 4)))
    return dict(frames_in=frames_in, cond=cond, text=text, item_lengths=item_lengths, text_lengths=text_lengths, ada_weight=ada_weight, qkv_weight=qkv_weight, out_weight=out_weight, cross_q_weight=cross_q_weight, cross_kv_weight=cross_kv_weight, cross_out_weight=cross_out_weight, up_weight=up_weight, down_weight=down_weight, cotangent=cotangent)


@jax.custom_vjp
def low(v):
    return lax.optimization_barrier(v.astype(jnp.bfloat16)).astype(jnp.float32)

@jax.custom_vjp
def low_back(v):
    return v

def low_keep(v):
    return (low(v), None)

def low_pass(kept, grad):
    return (grad,)

def back_keep(v):
    return (v, None)

def back_low(kept, grad):
    return (low(grad),)
low.defvjp(low_keep, low_pass)
low_back.defvjp(back_keep, back_low)

def product(formula, left, right):
    return jnp.einsum(formula, left, right, precision=lax.Precision.HIGHEST)

def layer_norm(tensor):
    centered = tensor - lax.optimization_barrier(jnp.mean(tensor, -1, keepdims=True))
    return centered * lax.rsqrt(lax.optimization_barrier(jnp.mean(centered * centered, -1, keepdims=True)) + 1e-06)

def split_heads(tensor):
    return tensor.reshape(tensor.shape[0], tensor.shape[1], H, HD)

def attention(queries, keys_in, values_in, key_valid):
    scores = low_back(product('ifhd,ijhd->ihfj', split_heads(queries), split_heads(keys_in)) * HD ** (-0.5))
    scores = jnp.where(key_valid[:, None, None, :], scores, -1e+30)
    weights_p = low(jax.nn.softmax(scores, axis=-1))
    mixed = product('ihfj,ijhd->ifhd', weights_p, split_heads(values_in))
    return mixed.reshape(queries.shape)

def layer(frames, cond, text, weights, key_valid, text_valid):
    ada_weight, qkv_weight, out_weight, cross_q_weight, cross_kv_weight, cross_out_weight, up_weight, down_weight = weights
    modulation = product('id,de->ie', low(jax.nn.silu(cond)), ada_weight)
    pieces = [modulation[:, None, position * D:(position + 1) * D] for position in range(9)]
    shift_a, scale_a, gate_a, shift_b, scale_b, gate_b, shift_c, scale_c, gate_c = pieces
    hidden_a = low(layer_norm(frames) * (1.0 + scale_a) + shift_a)
    qkv = low_back(low(product('ifd,de->ife', hidden_a, qkv_weight)))
    attended = low_back(low(attention(qkv[..., :D], qkv[..., D:2 * D], qkv[..., 2 * D:], key_valid)))
    first = frames + gate_a * low_back(product('ifd,de->ife', attended, out_weight))
    hidden_b = low(layer_norm(first) * (1.0 + scale_b) + shift_b)
    cross_q = low_back(low(product('ifd,de->ife', hidden_b, cross_q_weight)))
    text_kv = low_back(low(product('itd,de->ite', text, cross_kv_weight)))
    crossed = low_back(low(attention(cross_q, text_kv[..., :D], text_kv[..., D:], text_valid)))
    second = first + gate_b * low_back(product('ifd,de->ife', crossed, cross_out_weight))
    hidden_c = low(layer_norm(second) * (1.0 + scale_c) + shift_c)
    up_proj = low_back(product('ifd,dk->ifk', hidden_c, up_weight))
    activated = low(jax.nn.gelu(up_proj, approximate=False))
    return second + gate_c * low_back(product('ifk,kd->ifd', activated, down_weight))

def reference(frames_in, cond, text, item_lengths, text_lengths, ada_weight, qkv_weight, out_weight, cross_q_weight, cross_kv_weight, cross_out_weight, up_weight, down_weight, cotangent):
    weights = tuple((tensor.astype(jnp.float32) for tensor in (ada_weight, qkv_weight, out_weight, cross_q_weight, cross_kv_weight, cross_out_weight, up_weight, down_weight)))
    group = 4 if ITEMS % 4 == 0 else 2 if ITEMS % 2 == 0 else 1
    count = ITEMS // group

    def split(tensor):
        return tensor.reshape((count, group) + tensor.shape[1:])
    batches = (split(frames_in.astype(jnp.float32)), split(cond.astype(jnp.float32)), split(text.astype(jnp.float32)), split(item_lengths), split(text_lengths), split(cotangent.astype(jnp.float32)))

    def step(totals, batch):
        frames_g, cond_g, text_g, lengths_g, text_len_g, cot_g = batch
        key_valid = jnp.arange(LEN, dtype=jnp.int32)[None, :] < lengths_g[:, None]
        text_valid = jnp.arange(LT, dtype=jnp.int32)[None, :] < text_len_g[:, None]

        def forward(frames_x, cond_x, text_x, *weight_x):
            return layer(frames_x, cond_x, text_x, weight_x, key_valid, text_valid)
        result, backward = jax.vjp(forward, frames_g, cond_g, text_g, *weights)
        grads = backward(cot_g)
        totals = tuple((total + part for total, part in zip(totals, grads[3:])))
        return (totals, (result, grads[0], grads[2], grads[1]))
    zeros = tuple((jnp.zeros(tensor.shape, jnp.float32) for tensor in weights))
    totals, (results, frame_grads, text_grads, cond_grads) = lax.scan(step, zeros, batches)
    layer_out = results.reshape(ITEMS, LEN, D).astype(jnp.bfloat16)
    return (layer_out, frame_grads.reshape(ITEMS, LEN, D), text_grads.reshape(ITEMS, LT, D), cond_grads.reshape(ITEMS, D), totals[0], totals[1], totals[2], totals[3], totals[4], totals[5], totals[6], totals[7])
```

```python
import functools
from functools import partial

import jax
import jax.numpy as jnp
from jax import lax
from jax.experimental import pallas as pl
from jax.experimental.pallas import tpu as pltpu
from jax.sharding import PartitionSpec as P

H = 12


def norm_parts(tensor):
    centered = tensor - jnp.mean(tensor, -1, keepdims=True)
    inverse = lax.rsqrt(jnp.mean(centered * centered, -1, keepdims=True) + 1e-06)
    return (centered * inverse, inverse)


def norm_back(normed, inverse, incoming):
    return inverse * (
        incoming
        - jnp.mean(incoming, -1, keepdims=True)
        - normed * jnp.mean(incoming * normed, -1, keepdims=True)
    )


def split_heads(tensor):
    return tensor.reshape(tensor.shape[0], tensor.shape[1], H, -1)


def attend(queries, keys_in, values_in, key_valid, score_scale):
    scores = (
        jnp.einsum(
            "ifhd,ijhd->ihfj",
            split_heads(queries),
            split_heads(keys_in),
            preferred_element_type=jnp.float32,
        )
        * score_scale
    )
    scores = jnp.where(key_valid[:, None, None, :], scores, -1e30)
    attn_prob = jax.nn.softmax(scores, axis=-1)
    log_total = jax.nn.logsumexp(scores, axis=-1)
    low_prob = attn_prob.astype(jnp.bfloat16)
    mixed = jnp.einsum(
        "ihfj,ijhd->ifhd", low_prob, split_heads(values_in), preferred_element_type=jnp.float32
    )
    return (attn_prob, low_prob, mixed.astype(jnp.bfloat16).reshape(queries.shape), log_total)


def attend_back(grad_mixed, queries, keys_in, values_in, attn_prob, low_prob, score_scale):
    grad_heads = split_heads(grad_mixed)
    grad_prob = jnp.einsum(
        "ifhd,ijhd->ihfj", grad_heads, split_heads(values_in), preferred_element_type=jnp.float32
    )
    grad_values = jnp.einsum(
        "ihfj,ifhd->ijhd", low_prob, grad_heads, preferred_element_type=jnp.float32
    )
    grad_scores = (
        attn_prob * (grad_prob - jnp.sum(attn_prob * grad_prob, -1, keepdims=True))
    ).astype(jnp.bfloat16)
    grad_queries = (
        jnp.einsum(
            "ihfj,ijhd->ifhd", grad_scores, split_heads(keys_in), preferred_element_type=jnp.float32
        )
        * score_scale
    )
    grad_keys = (
        jnp.einsum(
            "ihfj,ifhd->ijhd", grad_scores, split_heads(queries), preferred_element_type=jnp.float32
        )
        * score_scale
    )
    return (
        grad_queries.reshape(queries.shape),
        grad_keys.reshape(keys_in.shape),
        grad_values.reshape(values_in.shape),
    )


def project(tensor, weight):
    return jnp.einsum("ifd,de->ife", tensor, weight, preferred_element_type=jnp.float32)


def project_back(tensor, weight):
    return jnp.einsum("ife,de->ifd", tensor, weight, preferred_element_type=jnp.float32)


def weight_grad(left, right):
    return jnp.einsum("ifd,ife->de", left, right, preferred_element_type=jnp.float32)


def frames_split(
    frames_in,
    cond,
    text,
    item_lengths,
    text_lengths,
    ada_weight,
    qkv_weight,
    out_weight,
    cross_q_weight,
    cross_kv_weight,
    cross_out_weight,
    up_weight,
    down_weight,
    cotangent,
):
    model_width = frames_in.shape[-1]
    score_scale = (model_width // H) ** (-0.5)
    cond_f = cond.astype(jnp.float32)
    low_cond = jax.nn.silu(cond_f).astype(jnp.bfloat16)
    modulation = jnp.dot(low_cond, ada_weight, preferred_element_type=jnp.float32)
    pieces = [
        modulation[:, None, position * model_width : (position + 1) * model_width]
        for position in range(9)
    ]
    shift_a, scale_a, gate_a, shift_b, scale_b, gate_b, shift_c, scale_c, gate_c = pieces
    residual_in = frames_in.astype(jnp.float32)
    normed_a, inverse_a = norm_parts(residual_in)
    hidden_a = (normed_a * (1.0 + scale_a) + shift_a).astype(jnp.bfloat16)
    qkv = project(hidden_a, qkv_weight).astype(jnp.bfloat16)
    queries = qkv[..., :model_width]
    keys_own = qkv[..., model_width : 2 * model_width]
    values_own = qkv[..., 2 * model_width :]
    keys_all, values_all = (
        lax.all_gather(keys_own, "frames", axis=1, tiled=True),
        lax.all_gather(values_own, "frames", axis=1, tiled=True),
    )
    key_valid = jnp.arange(keys_all.shape[1], dtype=jnp.int32)[None, :] < item_lengths[:, None]
    attn_prob, low_prob, attended, self_total = attend(
        queries, keys_all, values_all, key_valid, score_scale
    )
    branch_a = project(attended, out_weight)
    first = residual_in + gate_a * branch_a
    normed_b, inverse_b = norm_parts(first)
    hidden_b = (normed_b * (1.0 + scale_b) + shift_b).astype(jnp.bfloat16)
    cross_q = project(hidden_b, cross_q_weight).astype(jnp.bfloat16)
    text_own = project(text, cross_kv_weight).astype(jnp.bfloat16)
    text_kv = lax.all_gather(text_own, "frames", axis=1, tiled=True)
    text_keys = text_kv[..., :model_width]
    text_values = text_kv[..., model_width:]
    text_valid = jnp.arange(text_kv.shape[1], dtype=jnp.int32)[None, :] < text_lengths[:, None]
    cross_prob, cross_low, crossed, cross_total = attend(
        cross_q, text_keys, text_values, text_valid, score_scale
    )
    branch_b = project(crossed, cross_out_weight)
    second = first + gate_b * branch_b
    normed_c, inverse_c = norm_parts(second)
    hidden_c = (normed_c * (1.0 + scale_c) + shift_c).astype(jnp.bfloat16)
    up_proj = project(hidden_c, up_weight)
    activated, gelu_back = jax.vjp(partial(jax.nn.gelu, approximate=False), up_proj)
    low_act = activated.astype(jnp.bfloat16)
    branch_c = project(low_act, down_weight)
    layer_out = (second + gate_c * branch_c).astype(jnp.bfloat16)
    upstream = cotangent.astype(jnp.float32)
    d_gate_c = jnp.sum(upstream * branch_c, 1)
    d_branch_c = (upstream * gate_c).astype(jnp.bfloat16)
    grad_down = weight_grad(low_act, d_branch_c)
    d_up = gelu_back(project_back(d_branch_c, down_weight))[0].astype(jnp.bfloat16)
    grad_up = weight_grad(hidden_c, d_up)
    d_hidden_c = project_back(d_up, up_weight)
    d_shift_c = jnp.sum(d_hidden_c, 1)
    d_scale_c = jnp.sum(d_hidden_c * normed_c, 1)
    upstream = upstream + norm_back(normed_c, inverse_c, d_hidden_c * (1.0 + scale_c))
    d_gate_b = jnp.sum(upstream * branch_b, 1)
    d_branch_b = (upstream * gate_b).astype(jnp.bfloat16)
    grad_cross_out = weight_grad(crossed, d_branch_b)
    d_crossed = project_back(d_branch_b, cross_out_weight).astype(jnp.bfloat16)
    d_cross_q, d_text_keys, d_text_values = attend_back(
        d_crossed, cross_q, text_keys, text_values, cross_prob, cross_low, score_scale
    )
    d_cross_q = d_cross_q.astype(jnp.bfloat16)
    grad_cross_q = weight_grad(hidden_b, d_cross_q)
    d_hidden_b = project_back(d_cross_q, cross_q_weight)
    d_text_local = jnp.concatenate([d_text_keys, d_text_values], -1)
    d_shift_b = jnp.sum(d_hidden_b, 1)
    d_scale_b = jnp.sum(d_hidden_b * normed_b, 1)
    upstream = upstream + norm_back(normed_b, inverse_b, d_hidden_b * (1.0 + scale_b))
    d_gate_a = jnp.sum(upstream * branch_a, 1)
    d_branch_a = (upstream * gate_a).astype(jnp.bfloat16)
    grad_out = weight_grad(attended, d_branch_a)
    d_attended = project_back(d_branch_a, out_weight).astype(jnp.bfloat16)
    keys_back, values_back = (
        lax.all_gather(keys_own, "frames", axis=1, tiled=True),
        lax.all_gather(values_own, "frames", axis=1, tiled=True),
    )
    d_queries, d_keys_all, d_values_all = attend_back(
        d_attended, queries, keys_back, values_back, attn_prob, low_prob, score_scale
    )
    d_keys, d_values = (
        lax.psum_scatter(
            d_keys_all.astype(jnp.bfloat16), "frames", scatter_dimension=1, tiled=True
        ).astype(jnp.float32),
        lax.psum_scatter(
            d_values_all.astype(jnp.bfloat16), "frames", scatter_dimension=1, tiled=True
        ).astype(jnp.float32),
    )
    d_qkv = jnp.concatenate(
        [
            d_queries.astype(jnp.bfloat16),
            d_keys.astype(jnp.bfloat16),
            d_values.astype(jnp.bfloat16),
        ],
        -1,
    )
    grad_qkv = weight_grad(hidden_a, d_qkv)
    d_hidden_a = project_back(d_qkv, qkv_weight)
    d_shift_a = jnp.sum(d_hidden_a, 1)
    d_scale_a = jnp.sum(d_hidden_a * normed_a, 1)
    input_grad = upstream + norm_back(normed_a, inverse_a, d_hidden_a * (1.0 + scale_a))
    d_modulation = jnp.concatenate(
        [
            d_shift_a,
            d_scale_a,
            d_gate_a,
            d_shift_b,
            d_scale_b,
            d_gate_b,
            d_shift_c,
            d_scale_c,
            d_gate_c,
        ],
        -1,
    )
    grad_ada = jnp.dot(
        low_cond.astype(jnp.float32).T,
        d_modulation,
        precision=lax.Precision.HIGHEST,
        preferred_element_type=jnp.float32,
    )
    sigmoid_c = jax.nn.sigmoid(cond_f)
    cond_part = jnp.dot(
        d_modulation,
        ada_weight.T,
        precision=lax.Precision.HIGHEST,
        preferred_element_type=jnp.float32,
    ) * (sigmoid_c * (1.0 + cond_f * (1.0 - sigmoid_c)))
    d_text_kv, cond_grad = (
        lax.psum_scatter(d_text_local, "frames", scatter_dimension=1, tiled=True),
        lax.psum_scatter(cond_part, "frames", scatter_dimension=1, tiled=True),
    )
    low_text_kv = d_text_kv.astype(jnp.bfloat16)
    grad_cross_kv = weight_grad(text, low_text_kv)
    text_grad = project_back(low_text_kv, cross_kv_weight)
    grads = (
        grad_ada,
        grad_qkv,
        grad_out,
        grad_cross_q,
        grad_cross_kv,
        grad_cross_out,
        grad_up,
        grad_down,
    )
    partial_sums = (
        lax.psum_scatter(
            grads[0].astype(jnp.bfloat16), "frames", scatter_dimension=1, tiled=True
        ).astype(jnp.float32),
        lax.psum_scatter(
            grads[1].astype(jnp.bfloat16), "frames", scatter_dimension=1, tiled=True
        ).astype(jnp.float32),
        lax.psum_scatter(
            grads[2].astype(jnp.bfloat16), "frames", scatter_dimension=1, tiled=True
        ).astype(jnp.float32),
        lax.psum_scatter(
            grads[3].astype(jnp.bfloat16), "frames", scatter_dimension=1, tiled=True
        ).astype(jnp.float32),
        lax.psum_scatter(
            grads[4].astype(jnp.bfloat16), "frames", scatter_dimension=1, tiled=True
        ).astype(jnp.float32),
        lax.psum_scatter(
            grads[5].astype(jnp.bfloat16), "frames", scatter_dimension=1, tiled=True
        ).astype(jnp.float32),
        lax.psum_scatter(
            grads[6].astype(jnp.bfloat16), "frames", scatter_dimension=1, tiled=True
        ).astype(jnp.float32),
        lax.psum_scatter(
            grads[7].astype(jnp.bfloat16), "frames", scatter_dimension=1, tiled=True
        ).astype(jnp.float32),
    )
    totals = (
        lax.psum_scatter(
            partial_sums[0].astype(jnp.bfloat16), "items", scatter_dimension=0, tiled=True
        ).astype(jnp.float32),
        lax.psum_scatter(
            partial_sums[1].astype(jnp.bfloat16), "items", scatter_dimension=0, tiled=True
        ).astype(jnp.float32),
        lax.psum_scatter(
            partial_sums[2].astype(jnp.bfloat16), "items", scatter_dimension=0, tiled=True
        ).astype(jnp.float32),
        lax.psum_scatter(
            partial_sums[3].astype(jnp.bfloat16), "items", scatter_dimension=0, tiled=True
        ).astype(jnp.float32),
        lax.psum_scatter(
            partial_sums[4].astype(jnp.bfloat16), "items", scatter_dimension=0, tiled=True
        ).astype(jnp.float32),
        lax.psum_scatter(
            partial_sums[5].astype(jnp.bfloat16), "items", scatter_dimension=0, tiled=True
        ).astype(jnp.float32),
        lax.psum_scatter(
            partial_sums[6].astype(jnp.bfloat16), "items", scatter_dimension=0, tiled=True
        ).astype(jnp.float32),
        lax.psum_scatter(
            partial_sums[7].astype(jnp.bfloat16), "items", scatter_dimension=0, tiled=True
        ).astype(jnp.float32),
    )
    return (
        layer_out,
        input_grad,
        text_grad,
        cond_grad,
        totals[0],
        totals[1],
        totals[2],
        totals[3],
        totals[4],
        totals[5],
        totals[6],
        totals[7],
    )


LOG2E = 1.4426950408889634
BF = jnp.bfloat16
F32 = jnp.float32
PACK = 384
LIMIT = 60 * 2**20


def nn(left, right):
    return jnp.dot(left, right, preferred_element_type=F32)


def nt(left, right):
    return lax.dot_general(left, right, (((1,), (1,)), ((), ())), preferred_element_type=F32)


def tn(left, right):
    return lax.dot_general(left, right, (((0,), (0,)), ((), ())), preferred_element_type=F32)


def ln_parts(rows):
    share = 1.0 / rows.shape[-1]
    centered = rows - jnp.sum(rows, -1, keepdims=True) * share
    inverse = lax.rsqrt(jnp.sum(centered * centered, -1, keepdims=True) * share + 1e-06)
    return centered * inverse, inverse


def ln_back(normed, inverse, incoming):
    share = 1.0 / normed.shape[-1]
    mean_in = jnp.sum(incoming, -1, keepdims=True) * share
    mean_dot = jnp.sum(incoming * normed, -1, keepdims=True) * share
    return inverse * (incoming - mean_in - normed * mean_dot)


def gelu_parts(value):
    size = jnp.abs(value)
    inner = 1.0 / (1.0 + (0.3275911 * 0.7071067811865476) * size)
    series = inner * (
        0.5 * 0.254829592
        + inner
        * (
            0.5 * -0.284496736
            + inner * (0.5 * 1.421413741 + inner * (0.5 * -1.453152027 + inner * (0.5 * 1.061405429)))
        )
    )
    bell = jnp.exp2(value * value * (-0.5 * LOG2E))
    tail = series * bell
    below = jnp.where(value >= 0.0, 1.0 - tail, tail)
    return below, below + value * bell * 0.3989422804014327


def lane_half(half):
    lane = lax.broadcasted_iota(jnp.int32, (1, 128), 1)
    return lane < 64 if half == 0 else lane >= 64


def keep_half(rows, half):
    return jnp.where(lane_half(half), rows, jnp.zeros_like(rows))


def pack_square(acc, item, ra, cb, col):
    first = acc[pl.ds(pl.multiple_of(item * ra, 16), ra // 2), col : col + cb]
    second = acc[pl.ds(pl.multiple_of(item * ra + ra // 2, 16), ra // 2), col : col + cb]
    return jnp.concatenate([first, second], 1).astype(BF)


def qkv_kernel(x_ref, mod_ref, w_ref, o_ref, *, score_scale):
    width = x_ref.shape[-1]
    normed, _ = ln_parts(x_ref[0].astype(F32))
    hidden = (normed * (1.0 + mod_ref[0, 1:2]) + mod_ref[0, 0:1]).astype(BF)
    o_ref[0, :, :width] = (nn(hidden, w_ref[:, :width]) * (score_scale * LOG2E)).astype(BF)
    o_ref[0, :, width:] = nn(hidden, w_ref[:, width:]).astype(BF)


def self_fwd_kernel(lens, q_ref, k_ref, v_ref, o_ref, lse_ref, *, qb):
    count = q_ref.shape[1]
    used = lens[pl.program_id(0)]
    for klen in (count // 4, count // 2, count):

        @pl.when(used == klen)
        def _(klen=klen):
            keys = k_ref[0, :klen]
            values = jnp.concatenate([v_ref[0, :klen], jnp.ones((klen, 128), BF)], 1)

            def step(position, carry):
                rows = pl.ds(pl.multiple_of(position * qb, qb), qb)
                queries = q_ref[0, rows]
                outs = []
                for half in (0, 1):
                    scores = nt(keep_half(queries, half), keys)
                    top = jnp.max(scores, 1, keepdims=True)
                    prob = jnp.exp2(scores - top).astype(BF)
                    mixed = nn(prob, values)
                    total = mixed[:, 128:]
                    lse_ref[0, 0, half : half + 1, rows] = (top + jnp.log2(total[:, :1])).T
                    outs.append(mixed[:, :128] / total)
                o_ref[0, rows] = jnp.where(lane_half(0), outs[0], outs[1]).astype(BF)
                return carry

            lax.fori_loop(0, count // qb, step, 0)


def self_bwd_kernel(
    lens, q_ref, k_ref, v_ref, o_ref, do_ref, lse_ref, dq_ref, dk_ref, dv_ref, dk_acc, dv_acc, *, qb, score_scale
):
    count = q_ref.shape[1]
    used = lens[pl.program_id(0)]
    for klen in (count // 4, count // 2, count):

        @pl.when(used == klen)
        def _(klen=klen):
            keys = k_ref[0, :klen]
            values = v_ref[0, :klen]
            dk_acc[:klen] = jnp.zeros((klen, 128), F32)
            dv_acc[:klen] = jnp.zeros((klen, 128), F32)

            def step(position, carry):
                rows = pl.ds(pl.multiple_of(position * qb, qb), qb)
                queries = q_ref[0, rows]
                grad = do_ref[0, rows]
                dots = (grad.astype(F32) * o_ref[0, rows].astype(F32)).T
                d_queries = []
                for half in (0, 1):
                    q_half = keep_half(queries, half)
                    grad_half = keep_half(grad, half)
                    delta = jnp.sum(dots[64 * half : 64 * half + 64], 0, keepdims=True)
                    prob = jnp.exp2(nt(keys, q_half) - lse_ref[0, 0, half : half + 1, rows])
                    d_scores = (prob * (nt(values, grad_half) - delta)).astype(BF)
                    dv_acc[:klen] += nn(prob.astype(BF), grad_half)
                    dk_acc[:klen] += nn(d_scores, q_half)
                    d_queries.append(tn(d_scores, keys))
                dq_ref[0, rows] = (
                    jnp.where(lane_half(0), d_queries[0], d_queries[1]) * score_scale
                ).astype(BF)
                return carry

            lax.fori_loop(0, count // qb, step, 0)
            dk_ref[0, :klen] = (dk_acc[:klen] * (1.0 / LOG2E)).astype(BF)
            dv_ref[0, :klen] = dv_acc[:klen].astype(BF)
            if klen < count:
                dk_ref[0, klen:] = jnp.zeros((count - klen, 128), BF)
                dv_ref[0, klen:] = jnp.zeros((count - klen, 128), BF)


def cross_kernel(
    tlens, att_ref, x_ref, mod_ref, kv_ref, wo_ref, wq_ref, wco_ref,
    first_ref, second_ref, ba_ref, bb_ref, cq_ref, cr_ref, lse_ref, *, score_scale,
):
    width = x_ref.shape[-1]
    slots = kv_ref.shape[1]
    used = tlens[pl.program_id(0)]
    branch_a = nn(att_ref[0], wo_ref[...])
    ba_ref[0] = branch_a.astype(BF)
    first = x_ref[0].astype(F32) + mod_ref[0, 2:3] * branch_a
    first_ref[0] = first
    normed, _ = ln_parts(first)
    hidden = (normed * (1.0 + mod_ref[0, 4:5]) + mod_ref[0, 3:4]).astype(BF)
    cq_ref[0] = (nn(hidden, wq_ref[...]) * (score_scale * LOG2E)).astype(BF)
    valid = lax.broadcasted_iota(jnp.int32, (1, slots), 1) < used
    ones = jnp.ones((slots, 128), BF)
    for pair in range(H // 2):
        cols = slice(pair * 128, pair * 128 + 128)
        queries = cq_ref[0, :, cols]
        keys = kv_ref[0, :, cols]
        values = jnp.concatenate([kv_ref[0, :, width + pair * 128 : width + pair * 128 + 128], ones], 1)
        outs = []
        for half in (0, 1):
            scores = jnp.where(valid, nt(keep_half(queries, half), keys), -1e30)
            top = jnp.max(scores, 1, keepdims=True)
            prob = jnp.exp2(scores - top).astype(BF)
            mixed = nn(prob, values)
            total = mixed[:, 128:]
            lse_ref[0, pair, half : half + 1] = (top + jnp.log2(total[:, :1])).T
            outs.append(mixed[:, :128] / total)
        cr_ref[0, :, cols] = jnp.where(lane_half(0), outs[0], outs[1]).astype(BF)
    branch_b = nn(cr_ref[0], wco_ref[...])
    bb_ref[0] = branch_b.astype(BF)
    second_ref[0] = first + mod_ref[0, 5:6] * branch_b


def mlp_kernel(
    second_ref, cot_ref, mod_ref, wup_ref, wdn_ref,
    out_ref, g2_ref, dmod_ref, gup_ref, gdn_ref, up_acc, dn_acc, *, blocks, total, chunk, nf, ni,
):
    step = pl.program_id(0)
    width = second_ref.shape[-1]
    ff = wup_ref.shape[-1]

    @pl.when(step == 0)
    def _():
        up_acc[...] = jnp.zeros_like(up_acc)
        dn_acc[...] = jnp.zeros_like(dn_acc)

    @pl.when(step < total)
    def _():
        shift, scale, gate = mod_ref[0, 6:7], mod_ref[0, 7:8], mod_ref[0, 8:9]
        second = second_ref[0]
        normed, inverse = ln_parts(second)
        hidden = (normed * (1.0 + scale) + shift).astype(BF)
        upstream = cot_ref[0].astype(F32)
        d_branch = (upstream * gate).astype(BF)
        branch = jnp.zeros(second.shape, F32)
        d_hidden = jnp.zeros(second.shape, F32)
        for at in range(0, ff, chunk):
            cols = slice(at, at + chunk)
            up_proj = nn(hidden, wup_ref[:, cols])
            below, slope = gelu_parts(up_proj)
            act = (up_proj * below).astype(BF)
            branch += nn(act, wdn_ref[cols])
            d_up = (nt(d_branch, wdn_ref[cols]) * slope).astype(BF)
            d_hidden += nt(d_up, wup_ref[:, cols])
            dn_acc[cols] += tn(act, d_branch)
            up_acc[:, cols] += tn(hidden, d_up)
        out_ref[0] = (second + gate * branch).astype(BF)
        g2_ref[0] = upstream + ln_back(normed, inverse, d_hidden * (1.0 + scale))

        @pl.when(step % blocks == 0)
        def _():
            dmod_ref[...] = jnp.zeros_like(dmod_ref)

        dmod_ref[0, 0:1] += jnp.sum(d_hidden, 0, keepdims=True)
        dmod_ref[0, 1:2] += jnp.sum(d_hidden * normed, 0, keepdims=True)
        dmod_ref[0, 2:3] += jnp.sum(upstream * branch, 0, keepdims=True)

    @pl.when(step >= total)
    def _():
        item = step - total
        ra, cb = width // ni, ff // nf
        for frame in range(nf):
            part = up_acc[pl.ds(pl.multiple_of(item * ra, 16), ra), frame * cb : (frame + 1) * cb].astype(BF)
            gup_ref[0, frame] = jnp.concatenate([part[:, :PACK], part[:, PACK:]], 0)
            gdn_ref[0, frame] = pack_square(dn_acc, item, ff // ni, width // nf, frame * (width // nf))


def cross_back_kernel(
    tlens, g2_ref, ba_ref, bb_ref, cr_ref, att_ref, cq_ref, first_ref, mod_ref, kv_ref, lse_ref,
    wo_ref, wq_ref, wco_ref,
    g1_ref, datt_ref, dtext_ref, dmod_ref, gw_ref,
    o_acc, q_acc, co_acc, dcq_ref, *, blocks, total, score_scale, nf, ni,
):
    step = pl.program_id(0)
    width = g2_ref.shape[-1]
    slots = kv_ref.shape[1]

    @pl.when(step == 0)
    def _():
        o_acc[...] = jnp.zeros_like(o_acc)
        q_acc[...] = jnp.zeros_like(q_acc)
        co_acc[...] = jnp.zeros_like(co_acc)

    @pl.when(step < total)
    def _():
        @pl.when(step % blocks == 0)
        def _():
            dmod_ref[...] = jnp.zeros_like(dmod_ref)
            dtext_ref[...] = jnp.zeros_like(dtext_ref)

        used = tlens[step // blocks]
        upstream = g2_ref[0]
        dmod_ref[0, 3:4] += jnp.sum(upstream * bb_ref[0].astype(F32), 0, keepdims=True)
        d_branch_b = (upstream * mod_ref[0, 5:6]).astype(BF)
        co_acc[...] += tn(cr_ref[0], d_branch_b)
        d_crossed = nt(d_branch_b, wco_ref[...])
        valid = lax.broadcasted_iota(jnp.int32, (slots, 1), 0) < used
        for pair in range(H // 2):
            cols = slice(pair * 128, pair * 128 + 128)
            vcols = slice(width + pair * 128, width + pair * 128 + 128)
            queries = cq_ref[0, :, cols]
            keys = kv_ref[0, :, cols]
            values = kv_ref[0, :, vcols]
            grad = d_crossed[:, cols].astype(BF)
            dots = (grad.astype(F32) * cr_ref[0, :, cols].astype(F32)).T
            d_queries = []
            d_keys = 0.0
            d_values = 0.0
            for half in (0, 1):
                q_half = keep_half(queries, half)
                grad_half = keep_half(grad, half)
                delta = jnp.sum(dots[64 * half : 64 * half + 64], 0, keepdims=True)
                scores = jnp.where(valid, nt(keys, q_half), -1e30)
                prob = jnp.exp2(scores - lse_ref[0, pair, half : half + 1])
                d_scores = (prob * (nt(values, grad_half) - delta)).astype(BF)
                d_values += nn(prob.astype(BF), grad_half)
                d_keys += nn(d_scores, q_half)
                d_queries.append(tn(d_scores, keys))
            dtext_ref[0, :, cols] += d_keys * (1.0 / LOG2E)
            dtext_ref[0, :, vcols] += d_values
            dcq_ref[:, cols] = (
                jnp.where(lane_half(0), d_queries[0], d_queries[1]) * score_scale
            ).astype(BF)
        d_cq = dcq_ref[...]
        normed, inverse = ln_parts(first_ref[0])
        shift, scale = mod_ref[0, 3:4], mod_ref[0, 4:5]
        hidden = (normed * (1.0 + scale) + shift).astype(BF)
        q_acc[...] += tn(hidden, d_cq)
        d_hidden = nt(d_cq, wq_ref[...])
        dmod_ref[0, 1:2] += jnp.sum(d_hidden, 0, keepdims=True)
        dmod_ref[0, 2:3] += jnp.sum(d_hidden * normed, 0, keepdims=True)
        upstream = upstream + ln_back(normed, inverse, d_hidden * (1.0 + scale))
        g1_ref[0] = upstream
        dmod_ref[0, 0:1] += jnp.sum(upstream * ba_ref[0].astype(F32), 0, keepdims=True)
        d_branch_a = (upstream * mod_ref[0, 2:3]).astype(BF)
        o_acc[...] += tn(att_ref[0], d_branch_a)
        datt_ref[0] = nt(d_branch_a, wo_ref[...]).astype(BF)

    @pl.when(step >= total)
    def _():
        item = step - total
        ra, cb = width // ni, width // nf
        for frame in range(nf):
            for place, acc in enumerate((o_acc, q_acc, co_acc)):
                gw_ref[0, frame, place * (ra // 2) : (place + 1) * (ra // 2)] = pack_square(
                    acc, item, ra, cb, frame * cb
                )


def qkv_back_kernel(
    dq_ref, dk_ref, dv_ref, x_ref, g1_ref, mod_ref, w_ref, dx_ref, dmod_ref, gw_ref, acc, *, blocks, total, nf, ni
):
    step = pl.program_id(0)
    width = x_ref.shape[-1]

    @pl.when(step == 0)
    def _():
        acc[...] = jnp.zeros_like(acc)

    @pl.when(step < total)
    def _():
        @pl.when(step % blocks == 0)
        def _():
            dmod_ref[...] = jnp.zeros_like(dmod_ref)

        normed, inverse = ln_parts(x_ref[0].astype(F32))
        shift, scale = mod_ref[0, 0:1], mod_ref[0, 1:2]
        hidden = (normed * (1.0 + scale) + shift).astype(BF)
        d_hidden = jnp.zeros(normed.shape, F32)
        for place, ref in enumerate((dq_ref, dk_ref, dv_ref)):
            cols = slice(place * width, (place + 1) * width)
            acc[:, cols] += tn(hidden, ref[0])
            d_hidden += nt(ref[0], w_ref[:, cols])
        dmod_ref[0, 0:1] += jnp.sum(d_hidden, 0, keepdims=True)
        dmod_ref[0, 1:2] += jnp.sum(d_hidden * normed, 0, keepdims=True)
        dx_ref[0] = (g1_ref[0] + ln_back(normed, inverse, d_hidden * (1.0 + scale))).astype(BF)

    @pl.when(step >= total)
    def _():
        item = step - total
        ra, cb = width // ni, 3 * width // nf
        for frame in range(nf):
            part = acc[pl.ds(pl.multiple_of(item * ra, 16), ra), frame * cb : (frame + 1) * cb].astype(BF)
            gw_ref[0, frame, :ra] = part[:, :PACK]
            gw_ref[0, frame, ra:] = jnp.concatenate([part[: ra // 2, PACK:], part[ra // 2 :, PACK:]], 1)


def cost(flops, moved, exps=0):
    return pl.CostEstimate(flops=int(flops), bytes_accessed=int(moved), transcendentals=int(exps))


def params():
    return pltpu.CompilerParams(vmem_limit_bytes=LIMIT)


def whole(shape):
    return pl.BlockSpec(shape, lambda *_: (0,) * len(shape), pipeline_mode=pl.Buffered(1))


def struct(shape, dtype):
    return jax.ShapeDtypeStruct(shape, dtype)


def qkv_call(rows, mod, weight, score_scale, block):
    items, count, width = rows.shape
    return pl.pallas_call(
        partial(qkv_kernel, score_scale=score_scale),
        grid=(items, count // block),
        in_specs=[
            pl.BlockSpec((1, block, width), lambda i, j: (i, j, 0)),
            pl.BlockSpec((1, 9, width), lambda i, j: (i, 0, 0)),
            whole(weight.shape),
        ],
        out_specs=pl.BlockSpec((1, block, 3 * width), lambda i, j: (i, j, 0)),
        out_shape=struct((items, count, 3 * width), BF),
        compiler_params=params(),
        cost_estimate=cost(2 * items * count * width * 3 * width, items * count * width * 8),
        name="qkv_fwd",
    )(rows, mod, weight)


def self_fwd_call(lens, qkv, qb):
    items, count, width = qkv.shape
    width //= 3
    pairs = H // 2
    spec = pltpu.PrefetchScalarGridSpec(
        num_scalar_prefetch=1,
        grid=(items, pairs),
        in_specs=[
            pl.BlockSpec((1, count, 128), lambda i, h, s, part=part: (i, 0, part * pairs + h)) for part in range(3)
        ],
        out_specs=[
            pl.BlockSpec((1, count, 128), lambda i, h, s: (i, 0, h)),
            pl.BlockSpec((1, 1, 2, count), lambda i, h, s: (i, h, 0, 0)),
        ],
    )
    return pl.pallas_call(
        partial(self_fwd_kernel, qb=qb),
        grid_spec=spec,
        out_shape=[struct((items, count, width), BF), struct((items, pairs, 2, count), F32)],
        compiler_params=params(),
        cost_estimate=cost(16 * items * count * count * width, items * count * width * 8, items * H * count * count),
        name="self_fwd",
    )(lens, qkv, qkv, qkv)


def self_bwd_call(lens, qkv, att, d_att, lse, qb, score_scale):
    items, count, width = att.shape
    pairs = H // 2
    block = pl.BlockSpec((1, count, 128), lambda i, h, s: (i, 0, h))
    spec = pltpu.PrefetchScalarGridSpec(
        num_scalar_prefetch=1,
        grid=(items, pairs),
        in_specs=[
            pl.BlockSpec((1, count, 128), lambda i, h, s, part=part: (i, 0, part * pairs + h)) for part in range(3)
        ]
        + [block, block, pl.BlockSpec((1, 1, 2, count), lambda i, h, s: (i, h, 0, 0))],
        out_specs=[block] * 3,
        scratch_shapes=[pltpu.VMEM((count, 128), F32)] * 2,
    )
    return pl.pallas_call(
        partial(self_bwd_kernel, qb=qb, score_scale=score_scale),
        grid_spec=spec,
        out_shape=[struct((items, count, width), BF)] * 3,
        compiler_params=params(),
        cost_estimate=cost(40 * items * count * count * width, items * count * width * 16, items * H * count * count),
        name="self_bwd",
    )(lens, qkv, qkv, qkv, att, d_att, lse)


def cross_call(tlens, att, rows, mod, kv, wo, wq, wco, score_scale, block):
    items, count, width = rows.shape
    slots = kv.shape[1]
    row = pl.BlockSpec((1, block, width), lambda i, j, s: (i, j, 0))
    spec = pltpu.PrefetchScalarGridSpec(
        num_scalar_prefetch=1,
        grid=(items, count // block),
        in_specs=[
            row,
            row,
            pl.BlockSpec((1, 9, width), lambda i, j, s: (i, 0, 0)),
            pl.BlockSpec((1, slots, 2 * width), lambda i, j, s: (i, 0, 0)),
            whole(wo.shape),
            whole(wq.shape),
            whole(wco.shape),
        ],
        out_specs=[row] * 6 + [pl.BlockSpec((1, H // 2, 2, block), lambda i, j, s: (i, 0, 0, j))],
    )
    return pl.pallas_call(
        partial(cross_kernel, score_scale=score_scale),
        grid_spec=spec,
        out_shape=[struct(rows.shape, F32)] * 2
        + [struct(rows.shape, BF)] * 4
        + [struct((items, H // 2, 2, count), F32)],
        compiler_params=params(),
        cost_estimate=cost(
            items * count * (6 * width * width + 16 * slots * width), items * count * width * 20, items * H * count * slots
        ),
        name="cross_fwd",
    )(tlens, att, rows, mod, kv, wo, wq, wco)


def mlp_call(second, cot, mod, wup, wdn, block, chunk, nf, ni):
    items, count, width = second.shape
    ff = wup.shape[1]
    blocks = count // block
    total = items * blocks

    def at(t):
        return jnp.minimum(t, total - 1)

    row = pl.BlockSpec((1, block, width), lambda t: (at(t) // blocks, at(t) % blocks, 0))
    grad = pl.BlockSpec((1, nf, width * ff // (nf * ni * PACK), PACK), lambda t: (jnp.maximum(t - total, 0), 0, 0, 0))
    grad_shape = struct((ni, nf, width * ff // (nf * ni * PACK), PACK), BF)
    return pl.pallas_call(
        partial(mlp_kernel, blocks=blocks, total=total, chunk=chunk, nf=nf, ni=ni),
        grid=(total + ni,),
        in_specs=[
            row,
            row,
            pl.BlockSpec((1, 9, width), lambda t: (at(t) // blocks, 0, 0)),
            whole(wup.shape),
            whole(wdn.shape),
        ],
        out_specs=[row, row, pl.BlockSpec((1, 3, width), lambda t: (at(t) // blocks, 0, 0)), grad, grad],
        out_shape=[
            struct(second.shape, BF),
            struct(second.shape, F32),
            struct((items, 3, width), F32),
            grad_shape,
            grad_shape,
        ],
        scratch_shapes=[pltpu.VMEM((width, ff), F32), pltpu.VMEM((ff, width), F32)],
        compiler_params=params(),
        cost_estimate=cost(12 * items * count * width * ff, items * count * width * 12, items * count * ff * 2),
        name="mlp",
    )(second, cot, mod, wup, wdn)


def cross_back_call(tlens, g2, ba, bb, cr, att, cq, first, mod, kv, lse, wo, wq, wco, score_scale, block, nf, ni):
    items, count, width = g2.shape
    slots = kv.shape[1]
    blocks = count // block
    total = items * blocks

    def at(t):
        return jnp.minimum(t, total - 1)

    def by_item(t, s):
        return (at(t) // blocks, 0, 0)

    row = pl.BlockSpec((1, block, width), lambda t, s: (at(t) // blocks, at(t) % blocks, 0))
    depth = 3 * width * width // (nf * ni * PACK)
    spec = pltpu.PrefetchScalarGridSpec(
        num_scalar_prefetch=1,
        grid=(total + ni,),
        in_specs=[row] * 7
        + [
            pl.BlockSpec((1, 9, width), by_item),
            pl.BlockSpec((1, slots, 2 * width), by_item),
            pl.BlockSpec((1, H // 2, 2, block), lambda t, s: (at(t) // blocks, 0, 0, at(t) % blocks)),
            whole(wo.shape),
            whole(wq.shape),
            whole(wco.shape),
        ],
        out_specs=[
            row,
            row,
            pl.BlockSpec((1, slots, 2 * width), by_item),
            pl.BlockSpec((1, 4, width), by_item),
            pl.BlockSpec((1, nf, depth, PACK), lambda t, s: (jnp.maximum(t - total, 0), 0, 0, 0)),
        ],
        scratch_shapes=[pltpu.VMEM((width, width), F32)] * 3 + [pltpu.VMEM((block, width), BF)],
    )
    return pl.pallas_call(
        partial(cross_back_kernel, blocks=blocks, total=total, score_scale=score_scale, nf=nf, ni=ni),
        grid_spec=spec,
        out_shape=[
            struct(g2.shape, F32),
            struct(g2.shape, BF),
            struct(kv.shape, F32),
            struct((items, 4, width), F32),
            struct((ni, nf, depth, PACK), BF),
        ],
        compiler_params=params(),
        cost_estimate=cost(
            items * count * (12 * width * width + 40 * slots * width), items * count * width * 24, items * H * count * slots
        ),
        name="cross_bwd",
    )(tlens, g2, ba, bb, cr, att, cq, first, mod, kv, lse, wo, wq, wco)


def qkv_back_call(dq, dk, dv, rows, g1, mod, weight, block, nf, ni):
    items, count, width = rows.shape
    blocks = count // block
    total = items * blocks

    def at(t):
        return jnp.minimum(t, total - 1)

    row = pl.BlockSpec((1, block, width), lambda t: (at(t) // blocks, at(t) % blocks, 0))
    depth = 3 * width * width // (nf * ni * PACK)
    return pl.pallas_call(
        partial(qkv_back_kernel, blocks=blocks, total=total, nf=nf, ni=ni),
        grid=(total + ni,),
        in_specs=[row] * 5 + [pl.BlockSpec((1, 9, width), lambda t: (at(t) // blocks, 0, 0)), whole(weight.shape)],
        out_specs=[
            row,
            pl.BlockSpec((1, 2, width), lambda t: (at(t) // blocks, 0, 0)),
            pl.BlockSpec((1, nf, depth, PACK), lambda t: (jnp.maximum(t - total, 0), 0, 0, 0)),
        ],
        out_shape=[
            struct(rows.shape, BF),
            struct((items, 2, width), F32),
            struct((ni, nf, depth, PACK), BF),
        ],
        scratch_shapes=[pltpu.VMEM((width, 3 * width), F32)],
        compiler_params=params(),
        cost_estimate=cost(12 * items * count * width * width * 2, items * count * width * 20),
        name="qkv_bwd",
    )(dq, dk, dv, rows, g1, mod, weight)


def place_items(lengths, nf):
    count = lengths.shape[0]
    index = jnp.arange(count, dtype=jnp.int32)
    ahead = (lengths[None, :] > lengths[:, None]) | (
        (lengths[None, :] == lengths[:, None]) & (index[None, :] < index[:, None])
    )
    rank = jnp.sum(ahead.astype(jnp.int32), 1)
    turn, seat = rank // nf, rank % nf
    device = jnp.where(turn % 2 == 0, seat, nf - 1 - seat)
    place = device * (count // nf) + turn
    held = jnp.sum(jnp.where(place[None, :] == index[:, None], index[None, :], 0), 1)
    return place, held


def swap(block, offset, nf):
    if offset == 0:
        return block
    return lax.ppermute(block, "frames", [(i, i ^ offset) for i in range(nf)])


def to_items(shard, held, me, nf):
    count, rows, width = shard.shape
    per = count // nf
    out = jnp.zeros((per, nf, rows, width), shard.dtype)
    for offset in range(nf):
        partner = me ^ offset
        block = jnp.concatenate(
            [lax.dynamic_slice_in_dim(shard, held[partner * per + slot], 1, 0) for slot in range(per)], 0
        )
        block = swap(block, offset, nf)
        out = lax.dynamic_update_slice(out, block[:, None], (0, partner, 0, 0))
    return out.reshape(per, nf * rows, width)


def to_frames(items, place, me, nf):
    per, count, width = items.shape
    rows = count // nf
    got = []
    for offset in range(nf):
        block = lax.dynamic_slice_in_dim(items, (me ^ offset) * rows, rows, 1)
        got.append(swap(block, offset, nf))
    stacked = jnp.concatenate(got, 0)
    return jnp.concatenate(
        [
            lax.dynamic_slice_in_dim(stacked, ((place[i] // per) ^ me) * per + place[i] % per, 1, 0)
            for i in range(per * nf)
        ],
        0,
    )


def reduce_blocks(blocks):
    ni, nf, depth, pack = blocks.shape
    flat = blocks.reshape(ni * nf, depth, pack)
    return lax.psum_scatter(flat, ("items", "frames"), scatter_dimension=0, tiled=True)[0].astype(F32)


def wide(block, parts):
    rows = block.shape[0] // parts
    return jnp.concatenate([block[p * rows : (p + 1) * rows] for p in range(parts)], 1)


def tall(block):
    half = block.shape[1] // 2
    return jnp.concatenate([block[:, :half], block[:, half:]], 0)


def items_whole(
    ni, nf, frames_in, cond, text, item_lengths, text_lengths, ada_weight, qkv_weight, out_weight,
    cross_q_weight, cross_kv_weight, cross_out_weight, up_weight, down_weight, cotangent,
):
    width = frames_in.shape[-1]
    items = frames_in.shape[0]
    per = items // nf
    score_scale = (width // H) ** (-0.5)
    me = lax.axis_index("frames")
    row_item = lax.axis_index("items")
    place, held = place_items(item_lengths, nf)
    mine = lax.dynamic_slice_in_dim(held, me * per, per, 0)
    pick = (mine[:, None] == jnp.arange(items, dtype=jnp.int32)[None, :]).astype(F32)

    rows = to_items(frames_in, held, me, nf)
    text_rows = to_items(text, held, me, nf)
    cot = to_items(cotangent, held, me, nf)
    lens = jnp.take(item_lengths, mine)
    tlens = jnp.take(text_lengths, mine)

    cond_f = cond.astype(F32)
    low_cond = jax.nn.silu(cond_f).astype(BF)
    modulation = nn(low_cond, ada_weight)
    mod = jnp.sum(pick[:, :, None] * modulation[None], 1).reshape(per, 9, width)
    cond_mine = jnp.sum(pick[:, :, None] * low_cond.astype(F32)[None], 1)

    text_kv = jnp.einsum("itd,de->ite", text_rows, cross_kv_weight, preferred_element_type=F32).astype(BF)
    qkv = qkv_call(rows, mod, qkv_weight, score_scale, 256)
    attended, self_lse = self_fwd_call(lens, qkv, 512)
    first, second, branch_a, branch_b, cross_q, crossed, cross_lse = cross_call(
        tlens, attended, rows, mod, text_kv, out_weight, cross_q_weight, cross_out_weight, score_scale, 256
    )
    layer_rows, g2, dmod_c, g_up, g_down = mlp_call(second, cot, mod, up_weight, down_weight, 256, 768, nf, ni)
    layer_out = to_frames(layer_rows, place, me, nf)
    sum_up, sum_down = reduce_blocks(g_up), reduce_blocks(g_down)
    g1, d_att, d_text, dmod_b, g_sq = cross_back_call(
        tlens, g2, branch_a, branch_b, crossed, attended, cross_q, first, mod, text_kv, cross_lse,
        out_weight, cross_q_weight, cross_out_weight, score_scale, 256, nf, ni,
    )
    low_text = d_text.astype(BF)
    g_kv = weight_grad(text_rows, low_text).astype(BF)
    g_kv = g_kv.reshape(ni, width // ni, nf, 2 * width // nf).transpose(0, 2, 1, 3)
    text_grad = to_frames(project_back(low_text, cross_kv_weight).astype(BF), place, me, nf).astype(F32)
    sum_sq = reduce_blocks(jnp.concatenate([g_sq, g_kv], 2))
    dq, dk, dv = self_bwd_call(lens, qkv, attended, d_att, self_lse, 512, score_scale)
    d_rows, dmod_a, g_qkv = qkv_back_call(dq, dk, dv, rows, g1, mod, qkv_weight, 256, nf, ni)
    sum_qkv = reduce_blocks(g_qkv)
    input_grad = to_frames(d_rows, place, me, nf).astype(F32)

    d_mod = jnp.concatenate([dmod_a, dmod_b, dmod_c], 1).reshape(per, 9 * width)
    every = lax.all_gather(jnp.concatenate([cond_mine, d_mod], 1), ("items", "frames"), axis=0, tiled=True)
    ada_rows, ada_cols = width // ni, 9 * width // nf
    grad_ada = lax.dot_general(
        lax.dynamic_slice_in_dim(every[:, :width], row_item * ada_rows, ada_rows, 1),
        lax.dynamic_slice_in_dim(every[:, width:], me * ada_cols, ada_cols, 1),
        (((0,), (0,)), ((), ())),
        precision=lax.Precision.HIGHEST,
        preferred_element_type=F32,
    )
    cond_part = lax.dot_general(
        d_mod, ada_weight, (((1,), (1,)), ((), ())), precision=lax.Precision.HIGHEST, preferred_element_type=F32
    )
    cond_all = jnp.take(lax.all_gather(cond_part, "frames", axis=0, tiled=True), place, axis=0)
    sigmoid_c = jax.nn.sigmoid(cond_f)
    slope = sigmoid_c * (1.0 + cond_f * (1.0 - sigmoid_c))
    cond_grad = lax.dynamic_slice_in_dim(cond_all * slope, me * (width // nf), width // nf, 1)

    half = width // ni // 2
    return (
        layer_out,
        input_grad,
        text_grad,
        cond_grad,
        grad_ada,
        jnp.concatenate([sum_qkv[: 2 * half], tall(sum_qkv[2 * half :])], 1),
        tall(sum_sq[:half]),
        tall(sum_sq[half : 2 * half]),
        sum_sq[3 * half :],
        tall(sum_sq[2 * half : 3 * half]),
        wide(sum_up, 2),
        tall(sum_down),
    )


def on_device(mesh, *args):
    ni, nf = mesh.shape["items"], mesh.shape["frames"]
    if nf == 4 and args[0].shape[0] % nf == 0 and args[0].shape[-1] == 768 and 768 % (32 * ni) == 0:
        return items_whole(ni, nf, *args)
    return frames_split(*args)


def solution(mesh):
    in_specs = (
        P("items", "frames", None),
        P("items", None),
        P("items", "frames", None),
        P("items"),
        P("items"),
        P(),
        P(),
        P(),
        P(),
        P(),
        P(),
        P(),
        P(),
        P("items", "frames", None),
    )
    out_specs = (
        P("items", "frames", None),
        P("items", "frames", None),
        P("items", "frames", None),
        P("items", "frames"),
        P("items", "frames"),
        P("items", "frames"),
        P("items", "frames"),
        P("items", "frames"),
        P("items", "frames"),
        P("items", "frames"),
        P("items", "frames"),
        P("items", "frames"),
    )
    return jax.shard_map(
        partial(on_device, mesh), mesh=mesh, in_specs=in_specs, out_specs=out_specs, check_vma=False
    )
```

```python
import functools
from functools import partial

import jax
import jax.numpy as jnp
from jax import lax
from jax.experimental import pallas as pl
from jax.experimental.pallas import tpu as pltpu
from jax.sharding import PartitionSpec as P

H = 12


def norm_parts(tensor):
    centered = tensor - jnp.mean(tensor, -1, keepdims=True)
    inverse = lax.rsqrt(jnp.mean(centered * centered, -1, keepdims=True) + 1e-06)
    return (centered * inverse, inverse)


def norm_back(normed, inverse, incoming):
    return inverse * (
        incoming
        - jnp.mean(incoming, -1, keepdims=True)
        - normed * jnp.mean(incoming * normed, -1, keepdims=True)
    )


def split_heads(tensor):
    return tensor.reshape(tensor.shape[0], tensor.shape[1], H, -1)


def attend(queries, keys_in, values_in, key_valid, score_scale):
    scores = (
        jnp.einsum(
            "ifhd,ijhd->ihfj",
            split_heads(queries),
            split_heads(keys_in),
            preferred_element_type=jnp.float32,
        )
        * score_scale
    )
    scores = jnp.where(key_valid[:, None, None, :], scores, -1e30)
    attn_prob = jax.nn.softmax(scores, axis=-1)
    log_total = jax.nn.logsumexp(scores, axis=-1)
    low_prob = attn_prob.astype(jnp.bfloat16)
    mixed = jnp.einsum(
        "ihfj,ijhd->ifhd", low_prob, split_heads(values_in), preferred_element_type=jnp.float32
    )
    return (attn_prob, low_prob, mixed.astype(jnp.bfloat16).reshape(queries.shape), log_total)


def attend_back(grad_mixed, queries, keys_in, values_in, attn_prob, low_prob, score_scale):
    grad_heads = split_heads(grad_mixed)
    grad_prob = jnp.einsum(
        "ifhd,ijhd->ihfj", grad_heads, split_heads(values_in), preferred_element_type=jnp.float32
    )
    grad_values = jnp.einsum(
        "ihfj,ifhd->ijhd", low_prob, grad_heads, preferred_element_type=jnp.float32
    )
    grad_scores = (
        attn_prob * (grad_prob - jnp.sum(attn_prob * grad_prob, -1, keepdims=True))
    ).astype(jnp.bfloat16)
    grad_queries = (
        jnp.einsum(
            "ihfj,ijhd->ifhd", grad_scores, split_heads(keys_in), preferred_element_type=jnp.float32
        )
        * score_scale
    )
    grad_keys = (
        jnp.einsum(
            "ihfj,ifhd->ijhd", grad_scores, split_heads(queries), preferred_element_type=jnp.float32
        )
        * score_scale
    )
    return (
        grad_queries.reshape(queries.shape),
        grad_keys.reshape(keys_in.shape),
        grad_values.reshape(values_in.shape),
    )


def project(tensor, weight):
    return jnp.einsum("ifd,de->ife", tensor, weight, preferred_element_type=jnp.float32)


def project_back(tensor, weight):
    return jnp.einsum("ife,de->ifd", tensor, weight, preferred_element_type=jnp.float32)


def weight_grad(left, right):
    return jnp.einsum("ifd,ife->de", left, right, preferred_element_type=jnp.float32)


def frames_split(
    frames_in,
    cond,
    text,
    item_lengths,
    text_lengths,
    ada_weight,
    qkv_weight,
    out_weight,
    cross_q_weight,
    cross_kv_weight,
    cross_out_weight,
    up_weight,
    down_weight,
    cotangent,
):
    model_width = frames_in.shape[-1]
    score_scale = (model_width // H) ** (-0.5)
    cond_f = cond.astype(jnp.float32)
    low_cond = jax.nn.silu(cond_f).astype(jnp.bfloat16)
    modulation = jnp.dot(low_cond, ada_weight, preferred_element_type=jnp.float32)
    pieces = [
        modulation[:, None, position * model_width : (position + 1) * model_width]
        for position in range(9)
    ]
    shift_a, scale_a, gate_a, shift_b, scale_b, gate_b, shift_c, scale_c, gate_c = pieces
    residual_in = frames_in.astype(jnp.float32)
    normed_a, inverse_a = norm_parts(residual_in)
    hidden_a = (normed_a * (1.0 + scale_a) + shift_a).astype(jnp.bfloat16)
    qkv = project(hidden_a, qkv_weight).astype(jnp.bfloat16)
    queries = qkv[..., :model_width]
    keys_own = qkv[..., model_width : 2 * model_width]
    values_own = qkv[..., 2 * model_width :]
    keys_all, values_all = (
        lax.all_gather(keys_own, "frames", axis=1, tiled=True),
        lax.all_gather(values_own, "frames", axis=1, tiled=True),
    )
    key_valid = jnp.arange(keys_all.shape[1], dtype=jnp.int32)[None, :] < item_lengths[:, None]
    attn_prob, low_prob, attended, self_total = attend(
        queries, keys_all, values_all, key_valid, score_scale
    )
    branch_a = project(attended, out_weight)
    first = residual_in + gate_a * branch_a
    normed_b, inverse_b = norm_parts(first)
    hidden_b = (normed_b * (1.0 + scale_b) + shift_b).astype(jnp.bfloat16)
    cross_q = project(hidden_b, cross_q_weight).astype(jnp.bfloat16)
    text_own = project(text, cross_kv_weight).astype(jnp.bfloat16)
    text_kv = lax.all_gather(text_own, "frames", axis=1, tiled=True)
    text_keys = text_kv[..., :model_width]
    text_values = text_kv[..., model_width:]
    text_valid = jnp.arange(text_kv.shape[1], dtype=jnp.int32)[None, :] < text_lengths[:, None]
    cross_prob, cross_low, crossed, cross_total = attend(
        cross_q, text_keys, text_values, text_valid, score_scale
    )
    branch_b = project(crossed, cross_out_weight)
    second = first + gate_b * branch_b
    normed_c, inverse_c = norm_parts(second)
    hidden_c = (normed_c * (1.0 + scale_c) + shift_c).astype(jnp.bfloat16)
    up_proj = project(hidden_c, up_weight)
    activated, gelu_back = jax.vjp(partial(jax.nn.gelu, approximate=False), up_proj)
    low_act = activated.astype(jnp.bfloat16)
    branch_c = project(low_act, down_weight)
    layer_out = (second + gate_c * branch_c).astype(jnp.bfloat16)
    upstream = cotangent.astype(jnp.float32)
    d_gate_c = jnp.sum(upstream * branch_c, 1)
    d_branch_c = (upstream * gate_c).astype(jnp.bfloat16)
    grad_down = weight_grad(low_act, d_branch_c)
    d_up = gelu_back(project_back(d_branch_c, down_weight))[0].astype(jnp.bfloat16)
    grad_up = weight_grad(hidden_c, d_up)
    d_hidden_c = project_back(d_up, up_weight)
    d_shift_c = jnp.sum(d_hidden_c, 1)
    d_scale_c = jnp.sum(d_hidden_c * normed_c, 1)
    upstream = upstream + norm_back(normed_c, inverse_c, d_hidden_c * (1.0 + scale_c))
    d_gate_b = jnp.sum(upstream * branch_b, 1)
    d_branch_b = (upstream * gate_b).astype(jnp.bfloat16)
    grad_cross_out = weight_grad(crossed, d_branch_b)
    d_crossed = project_back(d_branch_b, cross_out_weight).astype(jnp.bfloat16)
    d_cross_q, d_text_keys, d_text_values = attend_back(
        d_crossed, cross_q, text_keys, text_values, cross_prob, cross_low, score_scale
    )
    d_cross_q = d_cross_q.astype(jnp.bfloat16)
    grad_cross_q = weight_grad(hidden_b, d_cross_q)
    d_hidden_b = project_back(d_cross_q, cross_q_weight)
    d_text_local = jnp.concatenate([d_text_keys, d_text_values], -1)
    d_shift_b = jnp.sum(d_hidden_b, 1)
    d_scale_b = jnp.sum(d_hidden_b * normed_b, 1)
    upstream = upstream + norm_back(normed_b, inverse_b, d_hidden_b * (1.0 + scale_b))
    d_gate_a = jnp.sum(upstream * branch_a, 1)
    d_branch_a = (upstream * gate_a).astype(jnp.bfloat16)
    grad_out = weight_grad(attended, d_branch_a)
    d_attended = project_back(d_branch_a, out_weight).astype(jnp.bfloat16)
    keys_back, values_back = (
        lax.all_gather(keys_own, "frames", axis=1, tiled=True),
        lax.all_gather(values_own, "frames", axis=1, tiled=True),
    )
    d_queries, d_keys_all, d_values_all = attend_back(
        d_attended, queries, keys_back, values_back, attn_prob, low_prob, score_scale
    )
    d_keys, d_values = (
        lax.psum_scatter(
            d_keys_all.astype(jnp.bfloat16), "frames", scatter_dimension=1, tiled=True
        ).astype(jnp.float32),
        lax.psum_scatter(
            d_values_all.astype(jnp.bfloat16), "frames", scatter_dimension=1, tiled=True
        ).astype(jnp.float32),
    )
    d_qkv = jnp.concatenate(
        [
            d_queries.astype(jnp.bfloat16),
            d_keys.astype(jnp.bfloat16),
            d_values.astype(jnp.bfloat16),
        ],
        -1,
    )
    grad_qkv = weight_grad(hidden_a, d_qkv)
    d_hidden_a = project_back(d_qkv, qkv_weight)
    d_shift_a = jnp.sum(d_hidden_a, 1)
    d_scale_a = jnp.sum(d_hidden_a * normed_a, 1)
    input_grad = upstream + norm_back(normed_a, inverse_a, d_hidden_a * (1.0 + scale_a))
    d_modulation = jnp.concatenate(
        [
            d_shift_a,
            d_scale_a,
            d_gate_a,
            d_shift_b,
            d_scale_b,
            d_gate_b,
            d_shift_c,
            d_scale_c,
            d_gate_c,
        ],
        -1,
    )
    grad_ada = jnp.dot(
        low_cond.astype(jnp.float32).T,
        d_modulation,
        precision=lax.Precision.HIGHEST,
        preferred_element_type=jnp.float32,
    )
    sigmoid_c = jax.nn.sigmoid(cond_f)
    cond_part = jnp.dot(
        d_modulation,
        ada_weight.T,
        precision=lax.Precision.HIGHEST,
        preferred_element_type=jnp.float32,
    ) * (sigmoid_c * (1.0 + cond_f * (1.0 - sigmoid_c)))
    d_text_kv, cond_grad = (
        lax.psum_scatter(d_text_local, "frames", scatter_dimension=1, tiled=True),
        lax.psum_scatter(cond_part, "frames", scatter_dimension=1, tiled=True),
    )
    low_text_kv = d_text_kv.astype(jnp.bfloat16)
    grad_cross_kv = weight_grad(text, low_text_kv)
    text_grad = project_back(low_text_kv, cross_kv_weight)
    grads = (
        grad_ada,
        grad_qkv,
        grad_out,
        grad_cross_q,
        grad_cross_kv,
        grad_cross_out,
        grad_up,
        grad_down,
    )
    partial_sums = (
        lax.psum_scatter(
            grads[0].astype(jnp.bfloat16), "frames", scatter_dimension=1, tiled=True
        ).astype(jnp.float32),
        lax.psum_scatter(
            grads[1].astype(jnp.bfloat16), "frames", scatter_dimension=1, tiled=True
        ).astype(jnp.float32),
        lax.psum_scatter(
            grads[2].astype(jnp.bfloat16), "frames", scatter_dimension=1, tiled=True
        ).astype(jnp.float32),
        lax.psum_scatter(
            grads[3].astype(jnp.bfloat16), "frames", scatter_dimension=1, tiled=True
        ).astype(jnp.float32),
        lax.psum_scatter(
            grads[4].astype(jnp.bfloat16), "frames", scatter_dimension=1, tiled=True
        ).astype(jnp.float32),
        lax.psum_scatter(
            grads[5].astype(jnp.bfloat16), "frames", scatter_dimension=1, tiled=True
        ).astype(jnp.float32),
        lax.psum_scatter(
            grads[6].astype(jnp.bfloat16), "frames", scatter_dimension=1, tiled=True
        ).astype(jnp.float32),
        lax.psum_scatter(
            grads[7].astype(jnp.bfloat16), "frames", scatter_dimension=1, tiled=True
        ).astype(jnp.float32),
    )
    totals = (
        lax.psum_scatter(
            partial_sums[0].astype(jnp.bfloat16), "items", scatter_dimension=0, tiled=True
        ).astype(jnp.float32),
        lax.psum_scatter(
            partial_sums[1].astype(jnp.bfloat16), "items", scatter_dimension=0, tiled=True
        ).astype(jnp.float32),
        lax.psum_scatter(
            partial_sums[2].astype(jnp.bfloat16), "items", scatter_dimension=0, tiled=True
        ).astype(jnp.float32),
        lax.psum_scatter(
            partial_sums[3].astype(jnp.bfloat16), "items", scatter_dimension=0, tiled=True
        ).astype(jnp.float32),
        lax.psum_scatter(
            partial_sums[4].astype(jnp.bfloat16), "items", scatter_dimension=0, tiled=True
        ).astype(jnp.float32),
        lax.psum_scatter(
            partial_sums[5].astype(jnp.bfloat16), "items", scatter_dimension=0, tiled=True
        ).astype(jnp.float32),
        lax.psum_scatter(
            partial_sums[6].astype(jnp.bfloat16), "items", scatter_dimension=0, tiled=True
        ).astype(jnp.float32),
        lax.psum_scatter(
            partial_sums[7].astype(jnp.bfloat16), "items", scatter_dimension=0, tiled=True
        ).astype(jnp.float32),
    )
    return (
        layer_out,
        input_grad,
        text_grad,
        cond_grad,
        totals[0],
        totals[1],
        totals[2],
        totals[3],
        totals[4],
        totals[5],
        totals[6],
        totals[7],
    )


LOG2E = 1.4426950408889634
BF = jnp.bfloat16
F32 = jnp.float32
PACK = 384
LIMIT = 60 * 2**20


def nn(left, right):
    return jnp.dot(left, right, preferred_element_type=F32)


def nt(left, right):
    return lax.dot_general(left, right, (((1,), (1,)), ((), ())), preferred_element_type=F32)


def tn(left, right):
    return lax.dot_general(left, right, (((0,), (0,)), ((), ())), preferred_element_type=F32)


def ln_parts(rows):
    share = 1.0 / rows.shape[-1]
    centered = rows - jnp.sum(rows, -1, keepdims=True) * share
    inverse = lax.rsqrt(jnp.sum(centered * centered, -1, keepdims=True) * share + 1e-06)
    return centered * inverse, inverse


def ln_back(normed, inverse, incoming):
    share = 1.0 / normed.shape[-1]
    mean_in = jnp.sum(incoming, -1, keepdims=True) * share
    mean_dot = jnp.sum(incoming * normed, -1, keepdims=True) * share
    return inverse * (incoming - mean_in - normed * mean_dot)


def gelu_parts(value):
    size = jnp.abs(value)
    inner = 1.0 / (1.0 + (0.3275911 * 0.7071067811865476) * size)
    series = inner * (
        0.5 * 0.254829592
        + inner
        * (
            0.5 * -0.284496736
            + inner * (0.5 * 1.421413741 + inner * (0.5 * -1.453152027 + inner * (0.5 * 1.061405429)))
        )
    )
    bell = jnp.exp2(value * value * (-0.5 * LOG2E))
    tail = series * bell
    below = jnp.where(value >= 0.0, 1.0 - tail, tail)
    return below, below + value * bell * 0.3989422804014327


def lane_half(half):
    lane = lax.broadcasted_iota(jnp.int32, (1, 128), 1)
    return lane < 64 if half == 0 else lane >= 64


def keep_half(rows, half):
    return jnp.where(lane_half(half), rows, jnp.zeros_like(rows))


def pack_square(acc, item, ra, cb, col):
    first = acc[pl.ds(pl.multiple_of(item * ra, 16), ra // 2), col : col + cb]
    second = acc[pl.ds(pl.multiple_of(item * ra + ra // 2, 16), ra // 2), col : col + cb]
    return jnp.concatenate([first, second], 1).astype(BF)


def store_block(value, frame, me, row, keep_ref, send_ref):
    place = frame ^ me

    @pl.when(place & 1 == 0)
    def _():
        keep_ref[0, place >> 1, row : row + value.shape[0]] = value

    @pl.when(place & 1 == 1)
    def _():
        send_ref[0, place >> 1, row : row + value.shape[0]] = value


def start_kernel(where, lengths, text_lengths, table, *, items, nf):
    per = items // nf
    me = where[0]
    table[0] = me
    table[1] = where[1]
    at = 2 + 3 * per
    for i in range(items):
        rank = jnp.int32(0)
        for j in range(items):
            if j < i:
                ahead = lengths[j] >= lengths[i]
            elif j > i:
                ahead = lengths[j] > lengths[i]
            else:
                continue
            rank = rank + ahead.astype(jnp.int32)
        turn, seat = rank // nf, rank % nf
        device = jnp.where(turn % 2 == 0, seat, nf - 1 - seat)
        table[at + i] = device
        table[at + items + i] = turn
        table[at + 2 * items + device * per + turn] = i
    for slot in range(per):
        item = table[at + 2 * items + me * per + slot]
        table[2 + slot] = item
        table[2 + per + slot] = lengths[item]
        table[2 + 2 * per + slot] = text_lengths[item]


def copy_kernel(table, *refs):
    half = len(refs) // 2
    for source, out in zip(refs[:half], refs[half:]):
        out[...] = source[...].reshape(out.shape)


def gate_kernel(*refs):
    pass


def text_kernel(table, rows_ref, w_ref, kv_ref):
    parts = [rows_ref[at, 0] for at in range(rows_ref.shape[0])]
    kv_ref[0] = nn(jnp.concatenate(parts, 0), w_ref[...]).astype(BF)


def text_back_kernel(
    table, d_ref, rows_ref, w_ref, ck_ref, cs_ref, out_ref, keep_ref, send_ref, acc, *, total, nf, ni
):
    step = pl.program_id(0)
    width = rows_ref.shape[-1]
    block = rows_ref.shape[2]

    @pl.when(step == 0)
    def _():
        acc[...] = jnp.zeros_like(acc)

    @pl.when(step < total)
    def _():
        low = d_ref[0].astype(BF)
        rows = jnp.concatenate([rows_ref[at, 0] for at in range(nf)], 0)
        acc[...] += tn(rows, low)
        made = nt(low, w_ref[...]).astype(BF)
        for frame in range(nf):
            out_ref[frame, 0] = made[frame * block : (frame + 1) * block]

    @pl.when(step >= total)
    def _():
        item = (step - total) ^ table[1]
        ra, cb = width // ni, 2 * width // nf
        skip = ck_ref.shape[2]
        keep_ref[0, :, :skip] = ck_ref[0]
        send_ref[0, :, :skip] = cs_ref[0]
        for frame in range(nf):
            part = acc[pl.ds(pl.multiple_of(item * ra, 16), ra), frame * cb : (frame + 1) * cb].astype(BF)
            store_block(part, frame, table[0], skip, keep_ref, send_ref)


def self_fwd_kernel(
    table, x_ref, mod_ref, w_ref, *refs, blocks, qb, score_scale, length_at
):
    rows_ref, qkv_ref, att_ref, lse_ref, held = refs[-5:]
    step = pl.program_id(0)
    width = rows_ref.shape[-1]
    count = att_ref.shape[1]
    block = rows_ref.shape[1]
    pairs = H // 2

    @pl.when(step < blocks)
    def _():
        rows_ref[0] = x_ref[0]
        normed, _ = ln_parts(x_ref[0].astype(F32))
        hidden = (normed * (1.0 + mod_ref[0, 1:2]) + mod_ref[0, 0:1]).astype(BF)
        at = pl.ds(pl.multiple_of(step * block, block), block)
        for part in range(3):
            made = nn(hidden, w_ref[:, part * width : (part + 1) * width])
            if part == 0:
                made = made * (score_scale * LOG2E)
            made = made.astype(BF)
            qkv_ref[0, :, part * width : (part + 1) * width] = made
            for pair in range(pairs):
                held[part * pairs + pair, at] = made[:, pair * 128 : pair * 128 + 128]

    for klen in (count // 4, count // 2, count):

        @pl.when((step >= blocks) & (table[length_at] == klen))
        def _(klen=klen):
            pair = step - blocks
            keys = held[pairs + pair, :klen]
            values = jnp.concatenate([held[2 * pairs + pair, :klen], jnp.ones((klen, 128), BF)], 1)

            def inner(position, carry):
                rows = pl.ds(pl.multiple_of(position * qb, qb), qb)
                queries = held[pair, rows]
                outs = []
                for half in (0, 1):
                    scores = nt(keep_half(queries, half), keys)
                    top = jnp.max(scores, 1, keepdims=True)
                    prob = jnp.exp2(scores - top).astype(BF)
                    mixed = nn(prob, values)
                    total = mixed[:, 128:]
                    lse_ref[0, 0, half : half + 1, rows] = (top + jnp.log2(total[:, :1])).T
                    outs.append(mixed[:, :128] / total)
                att_ref[0, rows] = jnp.where(lane_half(0), outs[0], outs[1]).astype(BF)
                return carry

            lax.fori_loop(0, count // qb, inner, 0)


def self_bwd_kernel(
    table, q_ref, k_ref, v_ref, o_ref, do_ref, lse_ref, *refs, length_at, qb, score_scale
):
    dq_ref, dk_ref, dv_ref, dk_acc, dv_acc = refs[-5:]
    count = q_ref.shape[1]
    used = table[length_at]
    for klen in (count // 4, count // 2, count):

        @pl.when(used == klen)
        def _(klen=klen):
            keys = k_ref[0, :klen]
            values = v_ref[0, :klen]
            dk_acc[:klen] = jnp.zeros((klen, 128), F32)
            dv_acc[:klen] = jnp.zeros((klen, 128), F32)

            def step(position, carry):
                rows = pl.ds(pl.multiple_of(position * qb, qb), qb)
                queries = q_ref[0, rows]
                grad = do_ref[0, rows]
                dots = (grad.astype(F32) * o_ref[0, rows].astype(F32)).T
                d_queries = []
                for half in (0, 1):
                    q_half = keep_half(queries, half)
                    grad_half = keep_half(grad, half)
                    delta = jnp.sum(dots[64 * half : 64 * half + 64], 0, keepdims=True)
                    prob = jnp.exp2(nt(keys, q_half) - lse_ref[0, 0, half : half + 1, rows])
                    d_scores = (prob * (nt(values, grad_half) - delta)).astype(BF)
                    dv_acc[:klen] += nn(prob.astype(BF), grad_half)
                    dk_acc[:klen] += nn(d_scores, q_half)
                    d_queries.append(tn(d_scores, keys))
                dq_ref[0, rows] = (
                    jnp.where(lane_half(0), d_queries[0], d_queries[1]) * score_scale
                ).astype(BF)
                return carry

            lax.fori_loop(0, count // qb, step, 0)
            dk_ref[0, :klen] = (dk_acc[:klen] * (1.0 / LOG2E)).astype(BF)
            dv_ref[0, :klen] = dv_acc[:klen].astype(BF)
            if klen < count:
                dk_ref[0, klen:] = jnp.zeros((count - klen, 128), BF)
                dv_ref[0, klen:] = jnp.zeros((count - klen, 128), BF)


def cross_kernel(
    table, att_ref, x_ref, mod_ref, kv_ref, wo_ref, wq_ref, wco_ref,
    first_ref, second_ref, ba_ref, bb_ref, cq_ref, cr_ref, lse_ref, *, score_scale, length_at,
):
    width = x_ref.shape[-1]
    slots = kv_ref.shape[1]
    used = table[length_at + pl.program_id(0)]
    branch_a = nn(att_ref[0], wo_ref[...])
    ba_ref[0] = branch_a.astype(BF)
    first = x_ref[0].astype(F32) + mod_ref[0, 2:3] * branch_a
    first_ref[0] = first
    normed, _ = ln_parts(first)
    hidden = (normed * (1.0 + mod_ref[0, 4:5]) + mod_ref[0, 3:4]).astype(BF)
    cq_ref[0] = (nn(hidden, wq_ref[...]) * (score_scale * LOG2E)).astype(BF)
    valid = lax.broadcasted_iota(jnp.int32, (1, slots), 1) < used
    ones = jnp.ones((slots, 128), BF)
    for pair in range(H // 2):
        cols = slice(pair * 128, pair * 128 + 128)
        queries = cq_ref[0, :, cols]
        keys = kv_ref[0, :, cols]
        values = jnp.concatenate([kv_ref[0, :, width + pair * 128 : width + pair * 128 + 128], ones], 1)
        outs = []
        for half in (0, 1):
            scores = jnp.where(valid, nt(keep_half(queries, half), keys), -1e30)
            top = jnp.max(scores, 1, keepdims=True)
            prob = jnp.exp2(scores - top).astype(BF)
            mixed = nn(prob, values)
            total = mixed[:, 128:]
            lse_ref[0, pair, half : half + 1] = (top + jnp.log2(total[:, :1])).T
            outs.append(mixed[:, :128] / total)
        cr_ref[0, :, cols] = jnp.where(lane_half(0), outs[0], outs[1]).astype(BF)
    branch_b = nn(cr_ref[0], wco_ref[...])
    bb_ref[0] = branch_b.astype(BF)
    second_ref[0] = first + mod_ref[0, 5:6] * branch_b


def mlp_kernel(
    table, second_ref, cot_ref, mod_ref, wup_ref, wdn_ref,
    out_ref, g2_ref, dmod_ref, gw_ref, up_acc, dn_acc, *, blocks, total, chunk, nf, ni,
):
    step = pl.program_id(0)
    width = second_ref.shape[-1]
    ff = wup_ref.shape[-1]

    @pl.when(step == 0)
    def _():
        up_acc[...] = jnp.zeros_like(up_acc)
        dn_acc[...] = jnp.zeros_like(dn_acc)

    @pl.when(step < total)
    def _():
        shift, scale, gate = mod_ref[0, 6:7], mod_ref[0, 7:8], mod_ref[0, 8:9]
        second = second_ref[0]
        normed, inverse = ln_parts(second)
        hidden = (normed * (1.0 + scale) + shift).astype(BF)
        upstream = cot_ref[0, 0].astype(F32)
        d_branch = (upstream * gate).astype(BF)
        branch = jnp.zeros(second.shape, F32)
        d_hidden = jnp.zeros(second.shape, F32)
        for at in range(0, ff, chunk):
            cols = slice(at, at + chunk)
            up_proj = nn(hidden, wup_ref[:, cols])
            below, slope = gelu_parts(up_proj)
            act = (up_proj * below).astype(BF)
            branch += nn(act, wdn_ref[cols])
            d_up = (nt(d_branch, wdn_ref[cols]) * slope).astype(BF)
            d_hidden += nt(d_up, wup_ref[:, cols])
            dn_acc[cols] += tn(act, d_branch)
            up_acc[:, cols] += tn(hidden, d_up)
        out_ref[0, 0] = (second + gate * branch).astype(BF)
        g2_ref[0] = upstream + ln_back(normed, inverse, d_hidden * (1.0 + scale))

        @pl.when(step % blocks == 0)
        def _():
            dmod_ref[...] = jnp.zeros_like(dmod_ref)

        dmod_ref[0, 0:1] += jnp.sum(d_hidden, 0, keepdims=True)
        dmod_ref[0, 1:2] += jnp.sum(d_hidden * normed, 0, keepdims=True)
        dmod_ref[0, 2:3] += jnp.sum(upstream * branch, 0, keepdims=True)

    @pl.when(step >= total)
    def _():
        item = step - total
        ra, cb = width // ni, ff // nf
        for frame in range(nf):
            part = up_acc[pl.ds(pl.multiple_of(item * ra, 16), ra), frame * cb : (frame + 1) * cb].astype(BF)
            gw_ref[0, frame, :ra] = part[:, :PACK]
            gw_ref[0, frame, ra : 2 * ra] = part[:, PACK:]
            gw_ref[0, frame, 2 * ra :] = pack_square(dn_acc, item, ff // ni, width // nf, frame * (width // nf))


def cross_att_back_kernel(
    table, g2_ref, bb_ref, cr_ref, cq_ref, mod_ref, kv_ref, lse_ref, wco_ref,
    dcq_ref, dtext_ref, dmod_ref, keep_ref, send_ref, co_acc, *, blocks, total, score_scale, nf, ni, length_at,
):
    step = pl.program_id(0)
    width = g2_ref.shape[-1]
    slots = kv_ref.shape[1]

    @pl.when(step == 0)
    def _():
        co_acc[...] = jnp.zeros_like(co_acc)

    @pl.when(step < total)
    def _():
        @pl.when(step % blocks == 0)
        def _():
            dmod_ref[...] = jnp.zeros_like(dmod_ref)
            dtext_ref[...] = jnp.zeros_like(dtext_ref)

        used = table[length_at + step // blocks]
        upstream = g2_ref[0]
        dmod_ref[0] += jnp.sum(upstream * bb_ref[0].astype(F32), 0, keepdims=True)
        d_branch_b = (upstream * mod_ref[0, 5:6]).astype(BF)
        co_acc[...] += tn(cr_ref[0], d_branch_b)
        d_crossed = nt(d_branch_b, wco_ref[...])
        valid = lax.broadcasted_iota(jnp.int32, (slots, 1), 0) < used
        for pair in range(H // 2):
            cols = slice(pair * 128, pair * 128 + 128)
            vcols = slice(width + pair * 128, width + pair * 128 + 128)
            queries = cq_ref[0, :, cols]
            keys = kv_ref[0, :, cols]
            values = kv_ref[0, :, vcols]
            grad = d_crossed[:, cols].astype(BF)
            dots = (grad.astype(F32) * cr_ref[0, :, cols].astype(F32)).T
            d_queries = []
            d_keys = 0.0
            d_values = 0.0
            for half in (0, 1):
                q_half = keep_half(queries, half)
                grad_half = keep_half(grad, half)
                delta = jnp.sum(dots[64 * half : 64 * half + 64], 0, keepdims=True)
                scores = jnp.where(valid, nt(keys, q_half), -1e30)
                prob = jnp.exp2(scores - lse_ref[0, pair, half : half + 1])
                d_scores = (prob * (nt(values, grad_half) - delta)).astype(BF)
                d_values += nn(prob.astype(BF), grad_half)
                d_keys += nn(d_scores, q_half)
                d_queries.append(tn(d_scores, keys))
            dtext_ref[0, :, cols] += d_keys * (1.0 / LOG2E)
            dtext_ref[0, :, vcols] += d_values
            dcq_ref[0, :, cols] = (
                jnp.where(lane_half(0), d_queries[0], d_queries[1]) * score_scale
            ).astype(BF)

    @pl.when(step >= total)
    def _():
        item = (step - total) ^ table[1]
        for frame in range(nf):
            part = pack_square(co_acc, item, width // ni, width // nf, frame * (width // nf))
            store_block(part, frame, table[0], 0, keep_ref, send_ref)


def cross_in_back_kernel(
    table, g2_ref, dcq_ref, ba_ref, att_ref, first_ref, mod_ref, wo_ref, wq_ref, ek_ref, es_ref,
    g1_ref, datt_ref, dmod_ref, keep_ref, send_ref, o_acc, q_acc, *, blocks, total, nf, ni,
):
    step = pl.program_id(0)
    width = g2_ref.shape[-1]

    @pl.when(step == 0)
    def _():
        o_acc[...] = jnp.zeros_like(o_acc)
        q_acc[...] = jnp.zeros_like(q_acc)

    @pl.when(step < total)
    def _():
        @pl.when(step % blocks == 0)
        def _():
            dmod_ref[...] = jnp.zeros_like(dmod_ref)

        d_cq = dcq_ref[0]
        normed, inverse = ln_parts(first_ref[0])
        shift, scale = mod_ref[0, 3:4], mod_ref[0, 4:5]
        hidden = (normed * (1.0 + scale) + shift).astype(BF)
        q_acc[...] += tn(hidden, d_cq)
        d_hidden = nt(d_cq, wq_ref[...])
        dmod_ref[0, 1:2] += jnp.sum(d_hidden, 0, keepdims=True)
        dmod_ref[0, 2:3] += jnp.sum(d_hidden * normed, 0, keepdims=True)
        upstream = g2_ref[0] + ln_back(normed, inverse, d_hidden * (1.0 + scale))
        g1_ref[0] = upstream
        dmod_ref[0, 0:1] += jnp.sum(upstream * ba_ref[0].astype(F32), 0, keepdims=True)
        d_branch_a = (upstream * mod_ref[0, 2:3]).astype(BF)
        o_acc[...] += tn(att_ref[0], d_branch_a)
        datt_ref[0] = nt(d_branch_a, wo_ref[...]).astype(BF)

    @pl.when(step >= total)
    def _():
        item = (step - total) ^ table[1]
        ra, cb = width // ni, width // nf
        skip = ek_ref.shape[2]
        keep_ref[0, :, :skip] = ek_ref[0]
        send_ref[0, :, :skip] = es_ref[0]
        for frame in range(nf):
            for place, acc in enumerate((o_acc, q_acc)):
                part = pack_square(acc, item, ra, cb, frame * cb)
                store_block(part, frame, table[0], skip + place * (ra // 2), keep_ref, send_ref)


def qkv_weight_kernel(table, dq_ref, dk_ref, dv_ref, x_ref, mod_ref, keep_ref, send_ref, acc, *, total, nf, ni):
    step = pl.program_id(0)
    width = x_ref.shape[-1]

    @pl.when(step == 0)
    def _():
        acc[...] = jnp.zeros_like(acc)

    @pl.when(step < total)
    def _():
        normed, _ = ln_parts(x_ref[0].astype(F32))
        hidden = (normed * (1.0 + mod_ref[0, 1:2]) + mod_ref[0, 0:1]).astype(BF)
        for place, ref in enumerate((dq_ref, dk_ref, dv_ref)):
            acc[:, place * width : (place + 1) * width] += tn(hidden, ref[0])

    @pl.when(step >= total)
    def _():
        item = (step - total) ^ table[1]
        ra, cb = width // ni, 3 * width // nf
        for frame in range(nf):
            part = acc[pl.ds(pl.multiple_of(item * ra, 16), ra), frame * cb : (frame + 1) * cb].astype(BF)
            rest = jnp.concatenate([part[: ra // 2, PACK:], part[ra // 2 :, PACK:]], 1)
            store_block(jnp.concatenate([part[:, :PACK], rest], 0), frame, table[0], 0, keep_ref, send_ref)


def qkv_in_back_kernel(
    table, dq_ref, dk_ref, dv_ref, x_ref, g1_ref, mod_ref, w_ref, out_ref, dmod_ref
):
    step = pl.program_id(0)
    width = x_ref.shape[-1]

    @pl.when(step == 0)
    def _():
        dmod_ref[...] = jnp.zeros_like(dmod_ref)

    normed, inverse = ln_parts(x_ref[0].astype(F32))
    d_hidden = jnp.zeros(normed.shape, F32)
    for place, ref in enumerate((dq_ref, dk_ref, dv_ref)):
        d_hidden += nt(ref[0], w_ref[:, place * width : (place + 1) * width])
    dmod_ref[0, 0:1] += jnp.sum(d_hidden, 0, keepdims=True)
    dmod_ref[0, 1:2] += jnp.sum(d_hidden * normed, 0, keepdims=True)
    out_ref[0] = (g1_ref[0] + ln_back(normed, inverse, d_hidden * (1.0 + mod_ref[0, 1:2]))).astype(BF)


def deal_kernel(table, *refs, at):
    out_ref = refs[-1]
    sources = refs[:-1]
    if len(sources) == 1:
        out_ref[0] = sources[0][0, 0].astype(out_ref.dtype)
        return
    slot_of = table[at + pl.num_programs(0) + pl.program_id(0)]
    for slot, ref in enumerate(sources):

        @pl.when(slot_of == slot)
        def _(ref=ref):
            out_ref[0] = ref[0, 0].astype(out_ref.dtype)


def cost(flops, moved, exps=0):
    return pl.CostEstimate(flops=int(flops), bytes_accessed=int(moved), transcendentals=int(exps))


def params():
    return pltpu.CompilerParams(vmem_limit_bytes=LIMIT)


def whole(shape):
    return pl.BlockSpec(shape, lambda *_: (0,) * len(shape), pipeline_mode=pl.Buffered(1))


def run(kernel, name, grid, in_specs, args, out_specs, out_shape, scratch=(), deps=(), work=None, aliases=None):
    inputs = len(args)

    def body(*refs):
        kernel(*refs[:inputs], *refs[inputs + len(deps) :])

    return pl.pallas_call(
        body,
        grid_spec=pltpu.PrefetchScalarGridSpec(
            num_scalar_prefetch=1,
            grid=grid,
            in_specs=list(in_specs) + [pl.BlockSpec(memory_space=pl.ANY)] * len(deps),
            out_specs=out_specs,
            scratch_shapes=list(scratch),
        ),
        out_shape=out_shape,
        input_output_aliases=aliases or {},
        compiler_params=params(),
        cost_estimate=work,
        name=name,
    )(*args, *deps)


def any_spec(count):
    return [pl.BlockSpec(memory_space=pl.ANY)] * count


def struct(shape, dtype):
    return jax.ShapeDtypeStruct(shape, dtype)


def start_call(where, lengths, text_lengths, items, nf):
    size = 2 + 3 * (items // nf) + 3 * items
    smem = pl.BlockSpec(memory_space=pltpu.SMEM)
    return pl.pallas_call(
        partial(start_kernel, items=items, nf=nf),
        in_specs=[smem] * 3,
        out_specs=smem,
        out_shape=struct((size,), jnp.int32),
        name="start",
    )(where, lengths, text_lengths)


def gather_first_call(table, rows, nf):
    items, block, width = rows.shape
    per = items // nf
    at = 2 + 3 * per + 2 * items
    return run(
        copy_kernel,
        "gather_first",
        (nf,),
        [pl.BlockSpec((1, block, width), lambda t, s: (s[at + t * per], 0, 0))],
        (table, rows),
        [pl.BlockSpec((1, block, width), lambda t, s: (t, 0, 0))],
        [struct((nf, block, width), BF)],
    )[0]


def gather_call(table, rows, text, cot, nf):
    items, block, width = rows.shape
    per = items // nf
    at = 2 + 3 * per + 2 * items
    short = text.shape[1]

    def source(size):
        return pl.BlockSpec((1, size, width), lambda t, s: (s[at + t], 0, 0))

    def out(size):
        return pl.BlockSpec((1, 1, size, width), lambda t, s: (t // per, t % per, 0, 0))

    return run(
        copy_kernel,
        "gather",
        (items,),
        [source(block), source(short), source(block)],
        (table, rows, text, cot),
        [
            pl.BlockSpec((1, 1, block, width), lambda t, s: (jnp.maximum(t % per - 1, 0), t // per, 0, 0)),
            out(short),
            out(block),
        ],
        [
            struct((per - 1, nf, block, width), BF),
            struct((nf, per, short, width), BF),
            struct((nf, per, block, width), BF),
        ],
    )


def gate_call(arrays, deps):
    return pl.pallas_call(
        gate_kernel,
        in_specs=any_spec(len(arrays) + len(deps)),
        out_specs=any_spec(len(arrays)),
        out_shape=[struct(array.shape, array.dtype) for array in arrays],
        input_output_aliases={at: at for at in range(len(arrays))},
        compiler_params=params(),
        name="gate",
    )(*arrays, *deps)


def text_call(table, text, weight):
    nf, per, block, width = text.shape
    slots = nf * block
    return run(
        text_kernel,
        "text_fwd",
        (per,),
        [pl.BlockSpec((nf, 1, block, width), lambda i, s: (0, i, 0, 0)), whole(weight.shape)],
        (table, text, weight),
        pl.BlockSpec((1, slots, 2 * width), lambda i, s: (i, 0, 0)),
        struct((per, slots, 2 * width), BF),
        work=cost(4 * per * slots * width * width, 0),
    )


def halves(ni, nf, depth, total):
    spec = pl.BlockSpec((1, nf // 2, depth, PACK), lambda t, s: (jnp.maximum(t - total, 0), 0, 0, 0))
    return [spec] * 2, [struct((ni, nf // 2, depth, PACK), BF)] * 2


def text_back_call(table, d_text, text, weight, co, ni, deps):
    nf, per, block, width = text.shape
    slots = nf * block
    skip = co[0].shape[2]
    specs, shapes = halves(ni, nf, skip + 2 * width * width // (nf * ni * PACK), per)

    def at(t, s):
        return (jnp.minimum(t, per - 1), 0, 0)

    by_slot = pl.BlockSpec((nf, 1, block, width), lambda t, s: (0, jnp.minimum(t, per - 1), 0, 0))
    into = pl.BlockSpec((1, nf // 2, skip, PACK), lambda t, s: (jnp.maximum(t - per, 0), 0, 0, 0))
    return run(
        partial(text_back_kernel, total=per, nf=nf, ni=ni),
        "text_bwd",
        (per + ni,),
        [pl.BlockSpec((1, slots, 2 * width), at), by_slot, whole(weight.shape), into, into],
        (table, d_text, text, weight, *co),
        [by_slot] + specs,
        [struct(text.shape, BF)] + shapes,
        scratch=[pltpu.VMEM((width, 2 * width), F32)],
        deps=deps,
        work=cost(8 * per * slots * width * width, 0),
    )


def self_fwd_call(table, slot, rows, mod, weight, kept, per, qb, score_scale, deps):
    blocks, block, width = rows.shape
    count = blocks * block
    pairs = H // 2

    def early(t):
        return jnp.minimum(t, blocks - 1)

    def late(t):
        return jnp.maximum(t - blocks, 0)

    return run(
        partial(self_fwd_kernel, blocks=blocks, qb=qb, score_scale=score_scale, length_at=2 + per + slot),
        "self_fwd",
        (blocks + pairs,),
        [pl.BlockSpec((1, block, width), lambda t, s: (early(t), 0, 0))]
        + [pl.BlockSpec((1, 9, width), lambda t, s: (slot, 0, 0)), whole(weight.shape)]
        + any_spec(len(kept)),
        (table, rows, mod, weight, *kept),
        [
            pl.BlockSpec((1, block, width), lambda t, s: (slot, early(t), 0)),
            pl.BlockSpec((1, block, 3 * width), lambda t, s: (slot, early(t), 0)),
            pl.BlockSpec((1, count, 128), lambda t, s: (slot, 0, late(t))),
            pl.BlockSpec((1, 1, 2, count), lambda t, s: (slot, late(t), 0, 0)),
        ],
        [
            struct((per, count, width), BF),
            struct((per, count, 3 * width), BF),
            struct((per, count, width), BF),
            struct((per, pairs, 2, count), F32),
        ],
        scratch=[pltpu.VMEM((3 * pairs, count, 128), BF)],
        deps=deps,
        work=cost(6 * count * width * width + 16 * count * count * width, count * width * 16, H * count * count),
        aliases={4 + at: at for at in range(len(kept))},
    )


def self_bwd_call(table, slot, qkv, att, d_att, lse, kept, qb, score_scale, deps):
    per, count, width = att.shape
    pairs = H // 2
    block = pl.BlockSpec((1, count, 128), lambda h, s: (slot, 0, h))
    return run(
        partial(self_bwd_kernel, length_at=2 + per + slot, qb=qb, score_scale=score_scale),
        "self_bwd",
        (pairs,),
        [pl.BlockSpec((1, count, 128), lambda h, s, part=part: (slot, 0, part * pairs + h)) for part in range(3)]
        + [block, block, pl.BlockSpec((1, 1, 2, count), lambda h, s: (slot, h, 0, 0))]
        + any_spec(len(kept)),
        (table, qkv, qkv, qkv, att, d_att, lse, *kept),
        [block] * 3,
        [struct((per, count, width), BF)] * 3,
        scratch=[pltpu.VMEM((count, 128), F32)] * 2,
        deps=deps,
        work=cost(40 * count * count * width, count * width * 16, H * count * count),
        aliases={7 + at: at for at in range(len(kept))},
    )


def cross_call(table, att, rows, mod, kv, wo, wq, wco, score_scale, block, deps):
    items, count, width = rows.shape
    slots = kv.shape[1]
    row = pl.BlockSpec((1, block, width), lambda i, j, s: (i, j, 0))
    return run(
        partial(cross_kernel, score_scale=score_scale, length_at=2 + 2 * items),
        "cross_fwd",
        (items, count // block),
        [
            row,
            row,
            pl.BlockSpec((1, 9, width), lambda i, j, s: (i, 0, 0)),
            pl.BlockSpec((1, slots, 2 * width), lambda i, j, s: (i, 0, 0)),
            whole(wo.shape),
            whole(wq.shape),
            whole(wco.shape),
        ],
        (table, att, rows, mod, kv, wo, wq, wco),
        [row] * 6 + [pl.BlockSpec((1, H // 2, 2, block), lambda i, j, s: (i, 0, 0, j))],
        [struct(rows.shape, F32)] * 2 + [struct(rows.shape, BF)] * 4 + [struct((items, H // 2, 2, count), F32)],
        deps=deps,
        work=cost(
            items * count * (6 * width * width + 16 * slots * width), items * count * width * 20, items * H * count * slots
        ),
    )


def back_grid(items, count, block):
    blocks = count // block
    total = items * blocks

    def at(t):
        return jnp.minimum(t, total - 1)

    def by_item(t, s):
        return (at(t) // blocks, 0, 0)

    def by_row(t, s):
        return (at(t) // blocks, at(t) % blocks, 0)

    return blocks, total, by_item, by_row


def mlp_call(table, second, cot, mod, wup, wdn, block, chunk, nf, ni, deps):
    items, count, width = second.shape
    ff = wup.shape[1]
    blocks, total, by_item, by_row = back_grid(items, count, block)
    row = pl.BlockSpec((1, block, width), by_row)
    shard = pl.BlockSpec((1, 1, block, width), lambda t, s: (by_row(t, s)[1], by_row(t, s)[0], 0, 0))
    depth = 2 * width * ff // (nf * ni * PACK)
    return run(
        partial(mlp_kernel, blocks=blocks, total=total, chunk=chunk, nf=nf, ni=ni),
        "mlp",
        (total + ni,),
        [row, shard, pl.BlockSpec((1, 9, width), by_item), whole(wup.shape), whole(wdn.shape)],
        (table, second, cot, mod, wup, wdn),
        [shard, row, pl.BlockSpec((1, 3, width), by_item)]
        + [pl.BlockSpec((1, nf, depth, PACK), lambda t, s: (jnp.maximum(t - total, 0), 0, 0, 0))],
        [struct(cot.shape, BF), struct(second.shape, F32), struct((items, 3, width), F32)]
        + [struct((ni, nf, depth, PACK), BF)],
        scratch=[pltpu.VMEM((width, ff), F32), pltpu.VMEM((ff, width), F32)],
        deps=deps,
        work=cost(12 * items * count * width * ff, items * count * width * 16, items * count * ff * 2),
    )


def cross_att_back_call(table, g2, bb, cr, cq, mod, kv, lse, wco, score_scale, block, nf, ni, deps):
    items, count, width = g2.shape
    slots = kv.shape[1]
    blocks, total, by_item, by_row = back_grid(items, count, block)
    row = pl.BlockSpec((1, block, width), by_row)
    specs, shapes = halves(ni, nf, width * width // (nf * ni * PACK), total)
    lse_spec = pl.BlockSpec((1, H // 2, 2, block), lambda t, s: (by_row(t, s)[0], 0, 0, by_row(t, s)[1]))
    return run(
        partial(
            cross_att_back_kernel,
            blocks=blocks,
            total=total,
            score_scale=score_scale,
            nf=nf,
            ni=ni,
            length_at=2 + 2 * items,
        ),
        "cross_att_bwd",
        (total + ni,),
        [row] * 4
        + [pl.BlockSpec((1, 9, width), by_item), pl.BlockSpec((1, slots, 2 * width), by_item), lse_spec, whole(wco.shape)],
        (table, g2, bb, cr, cq, mod, kv, lse, wco),
        [row, pl.BlockSpec((1, slots, 2 * width), by_item), pl.BlockSpec((1, 1, width), by_item)] + specs,
        [struct(g2.shape, BF), struct(kv.shape, F32), struct((items, 1, width), F32)] + shapes,
        scratch=[pltpu.VMEM((width, width), F32)],
        deps=deps,
        work=cost(
            items * count * (4 * width * width + 40 * slots * width), items * count * width * 16, items * H * count * slots
        ),
    )


def cross_in_back_call(table, g2, dcq, ba, att, first, mod, wo, wq, earlier, block, nf, ni, deps):
    items, count, width = g2.shape
    blocks, total, by_item, by_row = back_grid(items, count, block)
    row = pl.BlockSpec((1, block, width), by_row)
    skip = earlier[0].shape[2]
    into = pl.BlockSpec((1, nf // 2, skip, PACK), lambda t, s: (jnp.maximum(t - total, 0), 0, 0, 0))
    specs, shapes = halves(ni, nf, skip + 2 * width * width // (nf * ni * PACK), total)
    return run(
        partial(cross_in_back_kernel, blocks=blocks, total=total, nf=nf, ni=ni),
        "cross_in_bwd",
        (total + ni,),
        [row] * 5 + [pl.BlockSpec((1, 9, width), by_item), whole(wo.shape), whole(wq.shape), into, into],
        (table, g2, dcq, ba, att, first, mod, wo, wq, *earlier),
        [row, row, pl.BlockSpec((1, 3, width), by_item)] + specs,
        [struct(g2.shape, F32), struct(g2.shape, BF), struct((items, 3, width), F32)] + shapes,
        scratch=[pltpu.VMEM((width, width), F32)] * 2,
        deps=deps,
        work=cost(items * count * 8 * width * width, items * count * width * 20),
    )


def qkv_weight_call(table, dq, dk, dv, rows, mod, block, nf, ni, deps):
    items, count, width = rows.shape
    blocks, total, by_item, by_row = back_grid(items, count, block)
    row = pl.BlockSpec((1, block, width), by_row)
    specs, shapes = halves(ni, nf, 3 * width * width // (nf * ni * PACK), total)
    return run(
        partial(qkv_weight_kernel, total=total, nf=nf, ni=ni),
        "qkv_weight_bwd",
        (total + ni,),
        [row] * 4 + [pl.BlockSpec((1, 9, width), by_item)],
        (table, dq, dk, dv, rows, mod),
        specs,
        shapes,
        scratch=[pltpu.VMEM((width, 3 * width), F32)],
        deps=deps,
        work=cost(6 * items * count * width * width, items * count * width * 8),
    )


def qkv_in_back_call(table, slot, dq, dk, dv, rows, g1, mod, weight, block, deps):
    _, count, width = rows.shape
    row = pl.BlockSpec((1, block, width), lambda t, s: (slot, t, 0))
    return run(
        qkv_in_back_kernel,
        "qkv_in_bwd",
        (count // block,),
        [row] * 5 + [pl.BlockSpec((1, 9, width), lambda t, s: (slot, 0, 0)), whole(weight.shape)],
        (table, dq, dk, dv, rows, g1, mod, weight),
        [pl.BlockSpec((1, block, width), lambda t, s: (t, 0, 0)), pl.BlockSpec((1, 2, width), lambda t, s: (0, 0, 0))],
        [struct((count // block, block, width), BF), struct((1, 2, width), F32)],
        deps=deps,
        work=cost(6 * count * width * width, count * width * 16),
    )


def deal_call(table, got, per, dtype, name):
    nf, _, block, width = got[0].shape
    items = nf * per
    at = 2 + 3 * per
    if len(got) == 1:
        specs = [pl.BlockSpec((1, 1, block, width), lambda t, s: (s[at + t], s[at + items + t], 0, 0))]
    else:
        specs = [pl.BlockSpec((1, 1, block, width), lambda t, s: (s[at + t], 0, 0, 0))] * len(got)
    return run(
        partial(deal_kernel, at=at),
        name,
        (items,),
        specs,
        (table, *got),
        pl.BlockSpec((1, block, width), lambda t, s: (t, 0, 0)),
        struct((items, block, width), dtype),
        work=cost(0, items * block * width * 6),
    )


def exchange(blocks):
    return lax.all_to_all(blocks, "frames", 0, 0, tiled=True)


def swap(block, offset, nf):
    if offset == 0:
        return block
    return lax.ppermute(block, "frames", [(i, i ^ offset) for i in range(nf)])


def bits_of(count):
    return count.bit_length() - 1


class Sum:
    def __init__(self, keep, send, order, sizes):
        self.sizes = sizes
        ni, nf = sizes["items"], sizes["frames"]
        self.dims = [("items", bit) for bit in reversed(range(bits_of(ni)))]
        self.dims += [("frames", bit) for bit in reversed(range(1, bits_of(nf)))]
        shape = (2,) * len(self.dims) + keep.shape[2:]
        self.keep, self.send = keep.reshape(shape), send
        self.shape = shape
        self.steps = [("frames", 0)] + list(order)
        self.got = None

    def launch(self):
        name, bit = self.steps.pop(0)
        self.got = lax.ppermute(self.send, name, [(i, i ^ (1 << bit)) for i in range(self.sizes[name])])

    def land(self):
        got = self.got.reshape(self.keep.shape)
        if not self.steps:
            return self.keep.astype(F32) + got.astype(F32)
        dim = self.dims.index(self.steps[0])
        self.dims.remove(self.steps[0])
        cut = [
            (lax.index_in_dim(self.keep, half, dim, False).astype(F32) + lax.index_in_dim(got, half, dim, False).astype(F32))
            for half in (0, 1)
        ]
        self.keep, self.send = cut[0].astype(BF), cut[1].astype(BF)
        return None


def collect_items(rows, ni):
    for bit in range(bits_of(ni)):
        rows = jnp.concatenate([rows, lax.ppermute(rows, "items", [(i, i ^ (1 << bit)) for i in range(ni)])], 0)
    return rows


def wide(block, parts):
    rows = block.shape[0] // parts
    return jnp.concatenate([block[p * rows : (p + 1) * rows] for p in range(parts)], 1)


def tall(block):
    half = block.shape[1] // 2
    return jnp.concatenate([block[:, :half], block[:, half:]], 0)


def items_whole(
    ni, nf, frames_in, cond, text, item_lengths, text_lengths, ada_weight, qkv_weight, out_weight,
    cross_q_weight, cross_kv_weight, cross_out_weight, up_weight, down_weight, cotangent,
):
    items, block, width = frames_in.shape
    per = items // nf
    sizes = {"items": ni, "frames": nf}
    score_scale = (width // H) ** (-0.5)
    me = lax.axis_index("frames")
    row_item = lax.axis_index("items")
    x_first = [("items", bit) for bit in range(bits_of(ni))] + [("frames", bit) for bit in range(1, bits_of(nf))]
    z_first = x_first[1:2] + x_first[:1] + x_first[2:]

    table = start_call(jnp.stack([me, row_item]), item_lengths, text_lengths, items, nf)
    got = [exchange(gather_first_call(table, frames_in, nf))]
    row_sends, text_send, cot_send = gather_call(table, frames_in, text, cotangent, nf)

    cond_f = cond.astype(F32)
    low_cond = jax.nn.silu(cond_f).astype(BF)
    modulation = nn(low_cond, ada_weight)
    pick = table[2 : 2 + per, None] == jnp.arange(items, dtype=jnp.int32)[None, :]
    mod = jnp.sum(jnp.where(pick[:, :, None], modulation[None], 0.0), 1).reshape(per, 9, width)

    *sends, text_send = gate_call([row_sends[slot] for slot in range(per - 1)] + [text_send], got)
    got += [exchange(send) for send in sends]
    text_rows = exchange(text_send)

    kept = self_fwd_call(table, 0, got[0], mod, qkv_weight, (), per, 512, score_scale, sends + [text_send])
    (cot_send,) = gate_call([cot_send], got[1:] + [text_rows])
    cot = exchange(cot_send)
    for slot in range(1, per):
        kept = self_fwd_call(table, slot, got[slot], mod, qkv_weight, kept, per, 512, score_scale, [cot_send])
    rows, qkv, attended, self_lse = kept
    text_kv = text_call(table, text_rows, cross_kv_weight)
    first, second, branch_a, branch_b, cross_q, crossed, cross_lse = cross_call(
        table, attended, rows, mod, text_kv, out_weight, cross_q_weight, cross_out_weight, score_scale, block, []
    )
    layer_send, g2, dmod_c, g_mlp = mlp_call(
        table, second, cot, mod, up_weight, down_weight, block, 768, nf, ni, []
    )
    layer_got = exchange(layer_send)
    sum_mlp = lax.psum_scatter(
        g_mlp.reshape((ni * nf,) + g_mlp.shape[2:]), ("items", "frames"), scatter_dimension=0, tiled=True
    )[0]
    dcq, d_text, dgate_b, *co = cross_att_back_call(
        table, g2, branch_b, crossed, cross_q, mod, text_kv, cross_lse, cross_out_weight, score_scale, block, nf, ni, []
    )
    text_back, *earlier = text_back_call(table, d_text, text_rows, cross_kv_weight, co, ni, [layer_got])
    text_got = exchange(text_back)
    g1, d_att, dmod_b, mid_keep, mid_send = cross_in_back_call(
        table, g2, dcq, branch_a, attended, first, mod, out_weight, cross_q_weight, earlier, block, nf, ni, []
    )
    mid = Sum(mid_keep, mid_send, x_first, sizes)
    mid.launch()
    kept = self_bwd_call(table, 0, qkv, attended, d_att, self_lse, (), 512, score_scale, [text_got])
    mid.land()
    mid.launch()
    for slot in range(1, per):
        kept = self_bwd_call(table, slot, qkv, attended, d_att, self_lse, kept, 512, score_scale, [mid.send])
    dq, dk, dv = kept
    mid.land()
    mid.launch()
    qkv_keep, qkv_send = qkv_weight_call(table, dq, dk, dv, rows, mod, block, nf, ni, [mid.send, sum_mlp])
    grad = Sum(qkv_keep, qkv_send, z_first, sizes)
    grad.launch()
    mid.land()
    mid.launch()
    grad_got = []
    dmod_a = []
    for slot in range(per):
        made, dmod = qkv_in_back_call(
            table, slot, dq, dk, dv, rows, g1, mod, qkv_weight, block, [grad.send, mid.send]
        )
        grad_got.append(exchange(made)[:, None])
        dmod_a.append(dmod)
        grad.land()
        grad.launch()
    mid.land()
    mid.launch()
    sum_mid = mid.land()
    while grad.steps:
        grad.land()
        grad.launch()
    sum_qkv = grad.land()
    layer_out = deal_call(table, [layer_got], per, BF, "deal_out")
    text_grad = deal_call(table, [text_got], per, F32, "deal_text")
    input_grad = deal_call(table, grad_got, per, F32, "deal_in")

    d_mod = jnp.concatenate([jnp.concatenate(dmod_a, 0), dmod_b[:, :1], dmod_b[:, 1:], dgate_b, dmod_c], 1)
    d_mod = d_mod.reshape(per, 9 * width)
    ada_rows, ada_cols, cond_cols = width // ni, 9 * width // nf, width // nf
    at = 2 + 3 * per
    spot = table[at : at + items] * per + table[at + items : at + 2 * items]
    pick_row = spot[:, None] == jnp.arange(items, dtype=jnp.int32)[None, :]

    def my_items(per_item, cols):
        cut = exchange(per_item.reshape(per, nf, cols).transpose(1, 0, 2)).reshape(items, cols)
        return jnp.sum(jnp.where(pick_row[:, :, None], cut[None], 0.0), 1)

    every_cond = collect_items(low_cond, ni)
    every_mod = collect_items(my_items(d_mod, ada_cols), ni)
    grad_ada = lax.dot_general(
        lax.dynamic_slice(every_cond, (0, row_item * ada_rows), (items * ni, ada_rows), allow_negative_indices=False).astype(
            F32
        ),
        every_mod,
        (((0,), (0,)), ((), ())),
        precision=lax.Precision.HIGHEST,
        preferred_element_type=F32,
    )
    high = d_mod.astype(BF)
    rest = (d_mod - high.astype(F32)).astype(BF)
    parts = nt(jnp.concatenate([high, rest], 0), ada_weight)
    cond_part = my_items(parts[:per] + parts[per:], cond_cols)
    cond_mine = lax.dynamic_slice(cond_f, (0, me * cond_cols), (items, cond_cols), allow_negative_indices=False)
    sigmoid_c = jax.nn.sigmoid(cond_mine)
    cond_grad = cond_part * (sigmoid_c * (1.0 + cond_mine * (1.0 - sigmoid_c)))

    half = width // ni // 2
    deep = 2 * half
    sum_mlp = sum_mlp.astype(F32)
    return (
        layer_out,
        input_grad,
        text_grad,
        cond_grad,
        grad_ada,
        jnp.concatenate([sum_qkv[:deep], tall(sum_qkv[deep:])], 1),
        tall(sum_mid[3 * half : 4 * half]),
        tall(sum_mid[4 * half :]),
        sum_mid[half : 3 * half],
        tall(sum_mid[:half]),
        wide(sum_mlp[: 2 * deep], 2),
        tall(sum_mlp[2 * deep :]),
    )


def on_device(mesh, *args):
    ni, nf = mesh.shape["items"], mesh.shape["frames"]
    if nf == 4 and args[0].shape[0] % nf == 0 and args[0].shape[-1] == 768 and 768 % (32 * ni) == 0:
        return items_whole(ni, nf, *args)
    return frames_split(*args)


def solution(mesh):
    in_specs = (
        P("items", "frames", None),
        P("items", None),
        P("items", "frames", None),
        P("items"),
        P("items"),
        P(),
        P(),
        P(),
        P(),
        P(),
        P(),
        P(),
        P(),
        P("items", "frames", None),
    )
    out_specs = (
        P("items", "frames", None),
        P("items", "frames", None),
        P("items", "frames", None),
        P("items", "frames"),
        P("items", "frames"),
        P("items", "frames"),
        P("items", "frames"),
        P("items", "frames"),
        P("items", "frames"),
        P("items", "frames"),
        P("items", "frames"),
        P("items", "frames"),
    )
    return jax.shard_map(
        partial(on_device, mesh), mesh=mesh, in_specs=in_specs, out_specs=out_specs, check_vma=False
    )
```

```python
import functools
from functools import partial

import jax
import jax.numpy as jnp
from jax import lax
from jax.experimental import pallas as pl
from jax.experimental.pallas import tpu as pltpu
from jax.sharding import PartitionSpec as P

H = 12


def norm_parts(tensor):
    centered = tensor - jnp.mean(tensor, -1, keepdims=True)
    inverse = lax.rsqrt(jnp.mean(centered * centered, -1, keepdims=True) + 1e-06)
    return (centered * inverse, inverse)


def norm_back(normed, inverse, incoming):
    return inverse * (
        incoming
        - jnp.mean(incoming, -1, keepdims=True)
        - normed * jnp.mean(incoming * normed, -1, keepdims=True)
    )


def split_heads(tensor):
    return tensor.reshape(tensor.shape[0], tensor.shape[1], H, -1)


def attend(queries, keys_in, values_in, key_valid, score_scale):
    scores = (
        jnp.einsum(
            "ifhd,ijhd->ihfj",
            split_heads(queries),
            split_heads(keys_in),
            preferred_element_type=jnp.float32,
        )
        * score_scale
    )
    scores = jnp.where(key_valid[:, None, None, :], scores, -1e30)
    attn_prob = jax.nn.softmax(scores, axis=-1)
    log_total = jax.nn.logsumexp(scores, axis=-1)
    low_prob = attn_prob.astype(jnp.bfloat16)
    mixed = jnp.einsum(
        "ihfj,ijhd->ifhd", low_prob, split_heads(values_in), preferred_element_type=jnp.float32
    )
    return (attn_prob, low_prob, mixed.astype(jnp.bfloat16).reshape(queries.shape), log_total)


def attend_back(grad_mixed, queries, keys_in, values_in, attn_prob, low_prob, score_scale):
    grad_heads = split_heads(grad_mixed)
    grad_prob = jnp.einsum(
        "ifhd,ijhd->ihfj", grad_heads, split_heads(values_in), preferred_element_type=jnp.float32
    )
    grad_values = jnp.einsum(
        "ihfj,ifhd->ijhd", low_prob, grad_heads, preferred_element_type=jnp.float32
    )
    grad_scores = (
        attn_prob * (grad_prob - jnp.sum(attn_prob * grad_prob, -1, keepdims=True))
    ).astype(jnp.bfloat16)
    grad_queries = (
        jnp.einsum(
            "ihfj,ijhd->ifhd", grad_scores, split_heads(keys_in), preferred_element_type=jnp.float32
        )
        * score_scale
    )
    grad_keys = (
        jnp.einsum(
            "ihfj,ifhd->ijhd", grad_scores, split_heads(queries), preferred_element_type=jnp.float32
        )
        * score_scale
    )
    return (
        grad_queries.reshape(queries.shape),
        grad_keys.reshape(keys_in.shape),
        grad_values.reshape(values_in.shape),
    )


def project(tensor, weight):
    return jnp.einsum("ifd,de->ife", tensor, weight, preferred_element_type=jnp.float32)


def project_back(tensor, weight):
    return jnp.einsum("ife,de->ifd", tensor, weight, preferred_element_type=jnp.float32)


def weight_grad(left, right):
    return jnp.einsum("ifd,ife->de", left, right, preferred_element_type=jnp.float32)


def frames_split(
    frames_in,
    cond,
    text,
    item_lengths,
    text_lengths,
    ada_weight,
    qkv_weight,
    out_weight,
    cross_q_weight,
    cross_kv_weight,
    cross_out_weight,
    up_weight,
    down_weight,
    cotangent,
):
    model_width = frames_in.shape[-1]
    score_scale = (model_width // H) ** (-0.5)
    cond_f = cond.astype(jnp.float32)
    low_cond = jax.nn.silu(cond_f).astype(jnp.bfloat16)
    modulation = jnp.dot(low_cond, ada_weight, preferred_element_type=jnp.float32)
    pieces = [
        modulation[:, None, position * model_width : (position + 1) * model_width]
        for position in range(9)
    ]
    shift_a, scale_a, gate_a, shift_b, scale_b, gate_b, shift_c, scale_c, gate_c = pieces
    residual_in = frames_in.astype(jnp.float32)
    normed_a, inverse_a = norm_parts(residual_in)
    hidden_a = (normed_a * (1.0 + scale_a) + shift_a).astype(jnp.bfloat16)
    qkv = project(hidden_a, qkv_weight).astype(jnp.bfloat16)
    queries = qkv[..., :model_width]
    keys_own = qkv[..., model_width : 2 * model_width]
    values_own = qkv[..., 2 * model_width :]
    keys_all, values_all = (
        lax.all_gather(keys_own, "frames", axis=1, tiled=True),
        lax.all_gather(values_own, "frames", axis=1, tiled=True),
    )
    key_valid = jnp.arange(keys_all.shape[1], dtype=jnp.int32)[None, :] < item_lengths[:, None]
    attn_prob, low_prob, attended, self_total = attend(
        queries, keys_all, values_all, key_valid, score_scale
    )
    branch_a = project(attended, out_weight)
    first = residual_in + gate_a * branch_a
    normed_b, inverse_b = norm_parts(first)
    hidden_b = (normed_b * (1.0 + scale_b) + shift_b).astype(jnp.bfloat16)
    cross_q = project(hidden_b, cross_q_weight).astype(jnp.bfloat16)
    text_own = project(text, cross_kv_weight).astype(jnp.bfloat16)
    text_kv = lax.all_gather(text_own, "frames", axis=1, tiled=True)
    text_keys = text_kv[..., :model_width]
    text_values = text_kv[..., model_width:]
    text_valid = jnp.arange(text_kv.shape[1], dtype=jnp.int32)[None, :] < text_lengths[:, None]
    cross_prob, cross_low, crossed, cross_total = attend(
        cross_q, text_keys, text_values, text_valid, score_scale
    )
    branch_b = project(crossed, cross_out_weight)
    second = first + gate_b * branch_b
    normed_c, inverse_c = norm_parts(second)
    hidden_c = (normed_c * (1.0 + scale_c) + shift_c).astype(jnp.bfloat16)
    up_proj = project(hidden_c, up_weight)
    activated, gelu_back = jax.vjp(partial(jax.nn.gelu, approximate=False), up_proj)
    low_act = activated.astype(jnp.bfloat16)
    branch_c = project(low_act, down_weight)
    layer_out = (second + gate_c * branch_c).astype(jnp.bfloat16)
    upstream = cotangent.astype(jnp.float32)
    d_gate_c = jnp.sum(upstream * branch_c, 1)
    d_branch_c = (upstream * gate_c).astype(jnp.bfloat16)
    grad_down = weight_grad(low_act, d_branch_c)
    d_up = gelu_back(project_back(d_branch_c, down_weight))[0].astype(jnp.bfloat16)
    grad_up = weight_grad(hidden_c, d_up)
    d_hidden_c = project_back(d_up, up_weight)
    d_shift_c = jnp.sum(d_hidden_c, 1)
    d_scale_c = jnp.sum(d_hidden_c * normed_c, 1)
    upstream = upstream + norm_back(normed_c, inverse_c, d_hidden_c * (1.0 + scale_c))
    d_gate_b = jnp.sum(upstream * branch_b, 1)
    d_branch_b = (upstream * gate_b).astype(jnp.bfloat16)
    grad_cross_out = weight_grad(crossed, d_branch_b)
    d_crossed = project_back(d_branch_b, cross_out_weight).astype(jnp.bfloat16)
    d_cross_q, d_text_keys, d_text_values = attend_back(
        d_crossed, cross_q, text_keys, text_values, cross_prob, cross_low, score_scale
    )
    d_cross_q = d_cross_q.astype(jnp.bfloat16)
    grad_cross_q = weight_grad(hidden_b, d_cross_q)
    d_hidden_b = project_back(d_cross_q, cross_q_weight)
    d_text_local = jnp.concatenate([d_text_keys, d_text_values], -1)
    d_shift_b = jnp.sum(d_hidden_b, 1)
    d_scale_b = jnp.sum(d_hidden_b * normed_b, 1)
    upstream = upstream + norm_back(normed_b, inverse_b, d_hidden_b * (1.0 + scale_b))
    d_gate_a = jnp.sum(upstream * branch_a, 1)
    d_branch_a = (upstream * gate_a).astype(jnp.bfloat16)
    grad_out = weight_grad(attended, d_branch_a)
    d_attended = project_back(d_branch_a, out_weight).astype(jnp.bfloat16)
    keys_back, values_back = (
        lax.all_gather(keys_own, "frames", axis=1, tiled=True),
        lax.all_gather(values_own, "frames", axis=1, tiled=True),
    )
    d_queries, d_keys_all, d_values_all = attend_back(
        d_attended, queries, keys_back, values_back, attn_prob, low_prob, score_scale
    )
    d_keys, d_values = (
        lax.psum_scatter(
            d_keys_all.astype(jnp.bfloat16), "frames", scatter_dimension=1, tiled=True
        ).astype(jnp.float32),
        lax.psum_scatter(
            d_values_all.astype(jnp.bfloat16), "frames", scatter_dimension=1, tiled=True
        ).astype(jnp.float32),
    )
    d_qkv = jnp.concatenate(
        [
            d_queries.astype(jnp.bfloat16),
            d_keys.astype(jnp.bfloat16),
            d_values.astype(jnp.bfloat16),
        ],
        -1,
    )
    grad_qkv = weight_grad(hidden_a, d_qkv)
    d_hidden_a = project_back(d_qkv, qkv_weight)
    d_shift_a = jnp.sum(d_hidden_a, 1)
    d_scale_a = jnp.sum(d_hidden_a * normed_a, 1)
    input_grad = upstream + norm_back(normed_a, inverse_a, d_hidden_a * (1.0 + scale_a))
    d_modulation = jnp.concatenate(
        [
            d_shift_a,
            d_scale_a,
            d_gate_a,
            d_shift_b,
            d_scale_b,
            d_gate_b,
            d_shift_c,
            d_scale_c,
            d_gate_c,
        ],
        -1,
    )
    grad_ada = jnp.dot(
        low_cond.astype(jnp.float32).T,
        d_modulation,
        precision=lax.Precision.HIGHEST,
        preferred_element_type=jnp.float32,
    )
    sigmoid_c = jax.nn.sigmoid(cond_f)
    cond_part = jnp.dot(
        d_modulation,
        ada_weight.T,
        precision=lax.Precision.HIGHEST,
        preferred_element_type=jnp.float32,
    ) * (sigmoid_c * (1.0 + cond_f * (1.0 - sigmoid_c)))
    d_text_kv, cond_grad = (
        lax.psum_scatter(d_text_local, "frames", scatter_dimension=1, tiled=True),
        lax.psum_scatter(cond_part, "frames", scatter_dimension=1, tiled=True),
    )
    low_text_kv = d_text_kv.astype(jnp.bfloat16)
    grad_cross_kv = weight_grad(text, low_text_kv)
    text_grad = project_back(low_text_kv, cross_kv_weight)
    grads = (
        grad_ada,
        grad_qkv,
        grad_out,
        grad_cross_q,
        grad_cross_kv,
        grad_cross_out,
        grad_up,
        grad_down,
    )
    partial_sums = (
        lax.psum_scatter(
            grads[0].astype(jnp.bfloat16), "frames", scatter_dimension=1, tiled=True
        ).astype(jnp.float32),
        lax.psum_scatter(
            grads[1].astype(jnp.bfloat16), "frames", scatter_dimension=1, tiled=True
        ).astype(jnp.float32),
        lax.psum_scatter(
            grads[2].astype(jnp.bfloat16), "frames", scatter_dimension=1, tiled=True
        ).astype(jnp.float32),
        lax.psum_scatter(
            grads[3].astype(jnp.bfloat16), "frames", scatter_dimension=1, tiled=True
        ).astype(jnp.float32),
        lax.psum_scatter(
            grads[4].astype(jnp.bfloat16), "frames", scatter_dimension=1, tiled=True
        ).astype(jnp.float32),
        lax.psum_scatter(
            grads[5].astype(jnp.bfloat16), "frames", scatter_dimension=1, tiled=True
        ).astype(jnp.float32),
        lax.psum_scatter(
            grads[6].astype(jnp.bfloat16), "frames", scatter_dimension=1, tiled=True
        ).astype(jnp.float32),
        lax.psum_scatter(
            grads[7].astype(jnp.bfloat16), "frames", scatter_dimension=1, tiled=True
        ).astype(jnp.float32),
    )
    totals = (
        lax.psum_scatter(
            partial_sums[0].astype(jnp.bfloat16), "items", scatter_dimension=0, tiled=True
        ).astype(jnp.float32),
        lax.psum_scatter(
            partial_sums[1].astype(jnp.bfloat16), "items", scatter_dimension=0, tiled=True
        ).astype(jnp.float32),
        lax.psum_scatter(
            partial_sums[2].astype(jnp.bfloat16), "items", scatter_dimension=0, tiled=True
        ).astype(jnp.float32),
        lax.psum_scatter(
            partial_sums[3].astype(jnp.bfloat16), "items", scatter_dimension=0, tiled=True
        ).astype(jnp.float32),
        lax.psum_scatter(
            partial_sums[4].astype(jnp.bfloat16), "items", scatter_dimension=0, tiled=True
        ).astype(jnp.float32),
        lax.psum_scatter(
            partial_sums[5].astype(jnp.bfloat16), "items", scatter_dimension=0, tiled=True
        ).astype(jnp.float32),
        lax.psum_scatter(
            partial_sums[6].astype(jnp.bfloat16), "items", scatter_dimension=0, tiled=True
        ).astype(jnp.float32),
        lax.psum_scatter(
            partial_sums[7].astype(jnp.bfloat16), "items", scatter_dimension=0, tiled=True
        ).astype(jnp.float32),
    )
    return (
        layer_out,
        input_grad,
        text_grad,
        cond_grad,
        totals[0],
        totals[1],
        totals[2],
        totals[3],
        totals[4],
        totals[5],
        totals[6],
        totals[7],
    )


LOG2E = 1.4426950408889634
BF = jnp.bfloat16
F32 = jnp.float32
PACK = 384
FIN = 2
LIMIT = 60 * 2**20


def nn(left, right):
    return jnp.dot(left, right, preferred_element_type=F32)


def nt(left, right):
    return lax.dot_general(left, right, (((1,), (1,)), ((), ())), preferred_element_type=F32)


def tn(left, right):
    return lax.dot_general(left, right, (((0,), (0,)), ((), ())), preferred_element_type=F32)


def ln_parts(rows):
    share = 1.0 / rows.shape[-1]
    centered = rows - jnp.sum(rows, -1, keepdims=True) * share
    inverse = lax.rsqrt(jnp.sum(centered * centered, -1, keepdims=True) * share + 1e-06)
    return centered * inverse, inverse


def ln_back(normed, inverse, incoming):
    share = 1.0 / normed.shape[-1]
    mean_in = jnp.sum(incoming, -1, keepdims=True) * share
    mean_dot = jnp.sum(incoming * normed, -1, keepdims=True) * share
    return inverse * (incoming - mean_in - normed * mean_dot)


def gelu_parts(value):
    size = jnp.abs(value)
    inner = 1.0 / (1.0 + (0.3275911 * 0.7071067811865476) * size)
    series = inner * (
        0.5 * 0.254829592
        + inner
        * (
            0.5 * -0.284496736
            + inner * (0.5 * 1.421413741 + inner * (0.5 * -1.453152027 + inner * (0.5 * 1.061405429)))
        )
    )
    bell = jnp.exp2(value * value * (-0.5 * LOG2E))
    tail = series * bell
    below = jnp.where(value >= 0.0, 1.0 - tail, tail)
    return below, below + value * bell * 0.3989422804014327


def strips(body, *arrays, rows=16):
    made = [body(*(array[at : at + rows] for array in arrays)) for at in range(0, arrays[0].shape[0], rows)]
    if not isinstance(made[0], tuple):
        return jnp.concatenate(made, 0)
    return tuple(jnp.concatenate(column, 0) for column in zip(*made))


def fold(rows):
    return jnp.sum(rows.reshape(rows.shape[0] // 8, 8, rows.shape[1]), 0)


def modulate(rows, shift, scale):
    normed, _ = ln_parts(rows.astype(F32))
    return (normed * (1.0 + scale) + shift).astype(BF)


class Columns:
    def __init__(self, count):
        self.parts = [None] * count

    def add(self, at, rows):
        made = fold(rows)
        self.parts[at] = made if self.parts[at] is None else self.parts[at] + made

    def total(self, at):
        return jnp.sum(self.parts[at], 0, keepdims=True)


def lane_half(half):
    lane = lax.broadcasted_iota(jnp.int32, (1, 128), 1)
    return lane < 64 if half == 0 else lane >= 64


def keep_half(rows, half):
    return jnp.where(lane_half(half), rows, jnp.zeros_like(rows))


def pack_square(acc, item, ra, cb, col):
    first = acc[pl.ds(pl.multiple_of(item * ra, 16), ra // 2), col : col + cb]
    second = acc[pl.ds(pl.multiple_of(item * ra + ra // 2, 16), ra // 2), col : col + cb]
    return jnp.concatenate([first, second], 1).astype(BF)


def store_block(value, part, frame, me, row, keep_ref, send_ref):
    place = frame ^ me

    @pl.when(place & 1 == 0)
    def _():
        keep_ref[part, place >> 1, row : row + value.shape[0]] = value

    @pl.when(place & 1 == 1)
    def _():
        send_ref[part, place >> 1, row : row + value.shape[0]] = value


def start_kernel(where, lengths, text_lengths, table, *, items, nf):
    per = items // nf
    me = where[0]
    table[0] = me
    table[1] = where[1]
    at = 2 + 3 * per
    for i in range(items):
        rank = jnp.int32(0)
        for j in range(items):
            if j < i:
                ahead = lengths[j] >= lengths[i]
            elif j > i:
                ahead = lengths[j] > lengths[i]
            else:
                continue
            rank = rank + ahead.astype(jnp.int32)
        turn, seat = rank // nf, rank % nf
        device = jnp.where(turn % 2 == 0, seat, nf - 1 - seat)
        table[at + i] = device
        table[at + items + i] = turn
        table[at + 2 * items + device * per + turn] = i
    for slot in range(per):
        item = table[at + 2 * items + me * per + slot]
        table[2 + slot] = item
        table[2 + per + slot] = lengths[item]
        table[2 + 2 * per + slot] = text_lengths[item]


def copy_kernel(table, source, out):
    out[...] = source[...]


def gather_kernel(table, *refs, per):
    rows, texts, cots, mixed, cot = refs[0], refs[1 : 1 + per], refs[1 + per : 1 + 2 * per], refs[-2], refs[-1]
    block, short = rows.shape[1], texts[0].shape[1]
    mixed[0, :block] = rows[0]
    for slot in range(per):
        mixed[0, block + slot * short : block + (slot + 1) * short] = texts[slot][0]
        cot[0, slot] = cots[slot][0]


def gate_kernel(*refs):
    pass


def soften(scores):
    top = jnp.max(scores, 1, keepdims=True)
    return jnp.exp2(scores - top).astype(BF), top


def soft_back(scores, d_prob, lse, delta):
    prob = jnp.exp2(scores - lse)
    return prob.astype(BF), (prob * (d_prob - delta)).astype(BF)


def self_fwd_kernel(
    table, x_ref, mod_ref, w_ref, *refs, blocks, qb, score_scale, length_at
):
    rows_ref, qkv_ref, att_ref, lse_ref, held = refs[-5:]
    step = pl.program_id(0)
    width = rows_ref.shape[-1]
    count = att_ref.shape[1]
    block = rows_ref.shape[1]
    pairs = H // 2

    @pl.when(step < blocks)
    def _():
        rows_ref[0] = x_ref[0]
        shift, scale = mod_ref[0, 0:1], mod_ref[0, 1:2]
        hidden = strips(lambda rows: modulate(rows, shift, scale), x_ref[0])
        at = pl.ds(pl.multiple_of(step * block, block), block)
        for part in range(3):
            made = nn(hidden, w_ref[:, part * width : (part + 1) * width])
            if part == 0:
                made = made * (score_scale * LOG2E)
            made = made.astype(BF)
            qkv_ref[0, :, part * width : (part + 1) * width] = made
            for pair in range(pairs):
                held[part * pairs + pair, at] = made[:, pair * 128 : pair * 128 + 128]

    for klen in (count // 4, count // 2, count):

        @pl.when((step >= blocks) & (table[length_at] == klen))
        def _(klen=klen):
            pair = step - blocks
            keys = held[pairs + pair, :klen]
            values = jnp.concatenate([held[2 * pairs + pair, :klen], jnp.ones((klen, 128), BF)], 1)

            def inner(position, carry):
                rows = pl.ds(pl.multiple_of(position * qb, qb), qb)
                queries = held[pair, rows]
                outs = []
                for half in (0, 1):
                    prob, top = strips(soften, nt(keep_half(queries, half), keys))
                    mixed = nn(prob, values)
                    total = mixed[:, 128:]
                    lse_ref[0, 0, half : half + 1, rows] = (top + jnp.log2(total[:, :1])).T
                    outs.append(mixed[:, :128] / total)
                att_ref[0, rows] = jnp.where(lane_half(0), outs[0], outs[1]).astype(BF)
                return carry

            lax.fori_loop(0, count // qb, inner, 0)


def self_bwd_kernel(
    table, q_ref, k_ref, v_ref, o_ref, do_ref, lse_ref, x_ref, g1_ref, mod_ref, w_ref, *refs,
    slot, length_at, pairs, blocks, qb, score_scale, nf, ni, last,
):
    if last:
        d_early, x_early, mod_early, dx_ref, dmod_ref, keep_ref, send_ref, held, dk_acc, dv_acc, acc = refs
    else:
        text_ref, dx_ref, dmod_ref, d_out, held, dk_acc, dv_acc = refs
    step = pl.program_id(0)
    count = q_ref.shape[1]
    width = x_ref.shape[-1]
    block = x_ref.shape[1]
    used = table[length_at]
    for klen in (count // 4, count // 2, count):

        @pl.when((step < pairs) & (used == klen))
        def _(klen=klen):
            keys = k_ref[0, :klen]
            values = v_ref[0, :klen]
            dk_acc[:klen] = jnp.zeros((klen, 128), F32)
            dv_acc[:klen] = jnp.zeros((klen, 128), F32)

            def inner(position, carry):
                rows = pl.ds(pl.multiple_of(position * qb, qb), qb)
                queries = q_ref[0, rows]
                grad = do_ref[0, rows]
                dots = (grad.astype(F32) * o_ref[0, rows].astype(F32)).T
                d_queries = []
                for half in (0, 1):
                    q_half = keep_half(queries, half)
                    grad_half = keep_half(grad, half)
                    delta = jnp.sum(dots[64 * half : 64 * half + 64], 0, keepdims=True)
                    lse = lse_ref[0, 0, half : half + 1, rows]
                    prob, d_scores = strips(
                        partial(soft_back, lse=lse, delta=delta), nt(keys, q_half), nt(values, grad_half)
                    )
                    dv_acc[:klen] += nn(prob, grad_half)
                    dk_acc[:klen] += nn(d_scores, q_half)
                    d_queries.append(tn(d_scores, keys))
                held[step, rows] = (jnp.where(lane_half(0), d_queries[0], d_queries[1]) * score_scale).astype(BF)
                return carry

            lax.fori_loop(0, count // qb, inner, 0)
            held[pairs + step, :klen] = (dk_acc[:klen] * (1.0 / LOG2E)).astype(BF)
            held[2 * pairs + step, :klen] = dv_acc[:klen].astype(BF)
            if klen < count:
                held[pairs + step, klen:] = jnp.zeros((count - klen, 128), BF)
                held[2 * pairs + step, klen:] = jnp.zeros((count - klen, 128), BF)

    @pl.when(step == pairs)
    def _():
        dmod_ref[...] = jnp.zeros_like(dmod_ref)
        if last:
            acc[...] = jnp.zeros_like(acc)

    @pl.when((step >= pairs) & (step < pairs + blocks))
    def _():
        rows = pl.ds(pl.multiple_of((step - pairs) * block, block), block)
        d_qkv = jnp.concatenate([held[at, rows] for at in range(3 * pairs)], 1)
        shift, scale = mod_ref[0, 0:1], mod_ref[0, 1:2]
        d_hidden = nt(d_qkv, w_ref[...])
        sums = Columns(2)

        def leave(x, dh, upstream):
            normed, inverse = ln_parts(x.astype(F32))
            sums.add(0, dh)
            sums.add(1, dh * normed)
            out = upstream.astype(F32) + ln_back(normed, inverse, dh * (1.0 + scale))
            return out.astype(BF), (normed * (1.0 + scale) + shift).astype(BF)

        dx_ref[0, :block], hidden = strips(leave, x_ref[0], d_hidden, g1_ref[0])
        for at in range(2):
            dmod_ref[0, at : at + 1] += sums.total(at)
        if last:
            acc[...] += tn(hidden, d_qkv)
        else:
            d_out[...] = d_qkv
            short = text_ref.shape[2]
            for part in range(text_ref.shape[1]):
                dx_ref[0, block + part * short : block + (part + 1) * short] = text_ref[0, part]

    if last:

        @pl.when((step >= pairs + blocks) & (step < pairs + 2 * blocks))
        def _():
            shift, scale = mod_early[0, 0:1], mod_early[0, 1:2]
            hidden = strips(lambda rows: modulate(rows, shift, scale), x_early[0])
            acc[...] += tn(hidden, d_early[...])

        @pl.when(step >= pairs + 2 * blocks)
        def _():
            ra, cb = width // ni, 3 * width // nf
            for part in range(FIN):
                item = ((step - pairs - 2 * blocks) * FIN + part) ^ table[1]
                for frame in range(nf):
                    cut = acc[pl.ds(pl.multiple_of(item * ra, 16), ra), frame * cb : (frame + 1) * cb].astype(BF)
                    rest = jnp.concatenate([cut[: ra // 2, PACK:], cut[ra // 2 :, PACK:]], 1)
                    store_block(
                        jnp.concatenate([cut[:, :PACK], rest], 0), part, frame, table[0], 0, keep_ref, send_ref
                    )


def cross_kernel(
    table, att_ref, x_ref, mod_ref, text_ref, wkv_ref, wo_ref, wq_ref, wco_ref,
    kv_ref, text_rows, first_ref, second_ref, ba_ref, bb_ref, cq_ref, cr_ref, lse_ref, *, score_scale, length_at,
):
    width = x_ref.shape[-1]
    slots = kv_ref.shape[1]
    used = table[length_at + pl.program_id(0)]

    @pl.when(pl.program_id(1) == 0)
    def _():
        text_rows[0] = jnp.concatenate([text_ref[at] for at in range(text_ref.shape[0])], 0)
        kv_ref[0] = nn(text_rows[0], wkv_ref[...]).astype(BF)

    branch_a = nn(att_ref[0], wo_ref[...])
    gate_a, gate_b, shift, scale = mod_ref[0, 2:3], mod_ref[0, 5:6], mod_ref[0, 3:4], mod_ref[0, 4:5]

    def enter(rows, branch):
        first = rows.astype(F32) + gate_a * branch
        return branch.astype(BF), first, modulate(first, shift, scale)

    ba_ref[0], first, hidden = strips(enter, x_ref[0], branch_a)
    first_ref[0] = first.astype(BF)
    cq_ref[0] = (nn(hidden, wq_ref[...]) * (score_scale * LOG2E)).astype(BF)
    valid = lax.broadcasted_iota(jnp.int32, (1, slots), 1) < used
    ones = jnp.ones((slots, 128), BF)
    for pair in range(H // 2):
        cols = slice(pair * 128, pair * 128 + 128)
        queries = cq_ref[0, :, cols]
        keys = kv_ref[0, :, cols]
        values = jnp.concatenate([kv_ref[0, :, width + pair * 128 : width + pair * 128 + 128], ones], 1)
        outs = []
        for half in (0, 1):
            prob, top = strips(
                lambda scores: soften(jnp.where(valid, scores, -1e30)), nt(keep_half(queries, half), keys)
            )
            mixed = nn(prob, values)
            total = mixed[:, 128:]
            lse_ref[0, pair, half : half + 1] = (top + jnp.log2(total[:, :1])).T
            outs.append(mixed[:, :128] / total)
        cr_ref[0, :, cols] = jnp.where(lane_half(0), outs[0], outs[1]).astype(BF)
    branch_b = nn(cr_ref[0], wco_ref[...])
    bb_ref[0], second_ref[0] = strips(
        lambda rows, branch: (branch.astype(BF), (rows + gate_b * branch).astype(BF)), first, branch_b
    )


def mlp_kernel(
    table, second_ref, cot_ref, mod_ref, wup_ref, wdn_ref,
    out_ref, g2_ref, dmod_ref, gw_ref, up_acc, dn_acc, *, blocks, total, chunk, nf, ni,
):
    step = pl.program_id(0)
    width = second_ref.shape[-1]
    ff = wup_ref.shape[-1]

    @pl.when(step == 0)
    def _():
        up_acc[...] = jnp.zeros_like(up_acc)
        dn_acc[...] = jnp.zeros_like(dn_acc)

    @pl.when(step < total)
    def _():
        shift, scale, gate = mod_ref[0, 6:7], mod_ref[0, 7:8], mod_ref[0, 8:9]
        hidden = strips(lambda rows: modulate(rows, shift, scale), second_ref[0])
        d_branch = strips(lambda rows: (rows.astype(F32) * gate).astype(BF), cot_ref[0, 0])
        branch = jnp.zeros(second_ref.shape[1:], F32)
        d_hidden = jnp.zeros(second_ref.shape[1:], F32)

        def middle(up_proj, d_act):
            below, slope = gelu_parts(up_proj)
            return (up_proj * below).astype(BF), (d_act * slope).astype(BF)

        for at in range(0, ff, chunk):
            cols = slice(at, at + chunk)
            act, d_up = strips(middle, nn(hidden, wup_ref[:, cols]), nt(d_branch, wdn_ref[cols]))
            branch += nn(act, wdn_ref[cols])
            d_hidden += nt(d_up, wup_ref[:, cols])
            dn_acc[cols] += tn(act, d_branch)
            up_acc[:, cols] += tn(hidden, d_up)

        @pl.when(step % blocks == 0)
        def _():
            dmod_ref[...] = jnp.zeros_like(dmod_ref)

        sums = Columns(3)

        def leave(second, cot, branch_rows, dh):
            second = second.astype(F32)
            normed, inverse = ln_parts(second)
            upstream = cot.astype(F32)
            sums.add(0, dh)
            sums.add(1, dh * normed)
            sums.add(2, upstream * branch_rows)
            upstream = upstream + ln_back(normed, inverse, dh * (1.0 + scale))
            return (second + gate * branch_rows).astype(BF), upstream.astype(BF)

        out_ref[0, 0], g2_ref[0] = strips(leave, second_ref[0], cot_ref[0, 0], branch, d_hidden)
        for at in range(3):
            dmod_ref[0, at : at + 1] += sums.total(at)

    @pl.when(step >= total)
    def _():
        ra, cb = width // ni, ff // nf
        for part in range(FIN):
            item = (step - total) * FIN + part
            for frame in range(nf):
                cut = up_acc[pl.ds(pl.multiple_of(item * ra, 16), ra), frame * cb : (frame + 1) * cb].astype(BF)
                gw_ref[part, frame, :ra] = cut[:, :PACK]
                gw_ref[part, frame, ra : 2 * ra] = cut[:, PACK:]
                gw_ref[part, frame, 2 * ra :] = pack_square(
                    dn_acc, item, ff // ni, width // nf, frame * (width // nf)
                )


def cross_back_kernel(
    table, g2_ref, bb_ref, cr_ref, cq_ref, att_ref, ba_ref, first_ref, mod_ref, kv_ref, lse_ref, text_ref,
    wo_ref, wq_ref, wco_ref, wkv_ref,
    g1_ref, datt_ref, text_out, dmod_ref, keep_ref, send_ref,
    o_acc, q_acc, co_acc, kv_acc, dtext, *, blocks, total, score_scale, nf, ni, length_at,
):
    step = pl.program_id(0)
    width = g2_ref.shape[-1]
    slots = kv_ref.shape[1]

    @pl.when(step == 0)
    def _():
        o_acc[...] = jnp.zeros_like(o_acc)
        q_acc[...] = jnp.zeros_like(q_acc)
        co_acc[...] = jnp.zeros_like(co_acc)
        kv_acc[...] = jnp.zeros_like(kv_acc)

    @pl.when(step < total)
    def _():
        @pl.when(step % blocks == 0)
        def _():
            dmod_ref[...] = jnp.zeros_like(dmod_ref)
            dtext[...] = jnp.zeros_like(dtext)

        used = table[length_at + step // blocks]
        gate_b = mod_ref[0, 5:6]
        sums = Columns(4)

        def enter(upstream, branch):
            upstream = upstream.astype(F32)
            sums.add(3, upstream * branch.astype(F32))
            return (upstream * gate_b).astype(BF)

        d_branch_b = strips(enter, g2_ref[0], bb_ref[0])
        co_acc[...] += tn(cr_ref[0], d_branch_b)
        d_crossed = nt(d_branch_b, wco_ref[...])
        slot_of = lax.broadcasted_iota(jnp.int32, (slots, 1), 0)
        parts = []
        for pair in range(H // 2):
            cols = slice(pair * 128, pair * 128 + 128)
            vcols = slice(width + pair * 128, width + pair * 128 + 128)
            queries = cq_ref[0, :, cols]
            keys = kv_ref[0, :, cols]
            values = kv_ref[0, :, vcols]
            grad = d_crossed[:, cols].astype(BF)
            dots = (grad.astype(F32) * cr_ref[0, :, cols].astype(F32)).T
            d_queries = []
            d_keys = 0.0
            d_values = 0.0
            for half in (0, 1):
                q_half = keep_half(queries, half)
                grad_half = keep_half(grad, half)
                delta = jnp.sum(dots[64 * half : 64 * half + 64], 0, keepdims=True)
                lse = lse_ref[0, pair, half : half + 1]

                def back(scores, d_prob, at, lse=lse, delta=delta):
                    return soft_back(jnp.where(at < used, scores, -1e30), d_prob, lse, delta)

                prob, d_scores = strips(back, nt(keys, q_half), nt(values, grad_half), slot_of)
                d_values += nn(prob, grad_half)
                d_keys += nn(d_scores, q_half)
                d_queries.append(tn(d_scores, keys))
            dtext[:, cols] += d_keys * (1.0 / LOG2E)
            dtext[:, vcols] += d_values
            parts.append((jnp.where(lane_half(0), d_queries[0], d_queries[1]) * score_scale).astype(BF))
        d_cq = jnp.concatenate(parts, 1)
        shift, scale, gate = mod_ref[0, 3:4], mod_ref[0, 4:5], mod_ref[0, 2:3]
        d_hidden = nt(d_cq, wq_ref[...])

        def leave(first, dh, upstream, branch):
            normed, inverse = ln_parts(first.astype(F32))
            sums.add(1, dh)
            sums.add(2, dh * normed)
            upstream = upstream.astype(F32) + ln_back(normed, inverse, dh * (1.0 + scale))
            sums.add(0, upstream * branch.astype(F32))
            return (normed * (1.0 + scale) + shift).astype(BF), upstream.astype(BF), (upstream * gate).astype(BF)

        hidden, g1_ref[0], d_branch_a = strips(leave, first_ref[0], d_hidden, g2_ref[0], ba_ref[0])
        for at in range(4):
            dmod_ref[0, at : at + 1] += sums.total(at)
        datt_ref[0] = nt(d_branch_a, wo_ref[...]).astype(BF)
        q_acc[...] += tn(hidden, d_cq)
        o_acc[...] += tn(att_ref[0], d_branch_a)

        @pl.when(step % blocks == blocks - 1)
        def _():
            low = dtext[...].astype(BF)
            kv_acc[...] += tn(text_ref[0], low)
            made = nt(low, wkv_ref[...]).astype(BF)
            short = text_out.shape[2]
            for frame in range(nf):
                text_out[frame, 0] = made[frame * short : (frame + 1) * short]

    @pl.when(step >= total)
    def _():
        ra, cb = width // ni, width // nf
        half = ra // 2
        for part in range(FIN):
            item = ((step - total) * FIN + part) ^ table[1]
            for frame in range(nf):
                for place, acc in enumerate((o_acc, q_acc, co_acc)):
                    cut = pack_square(acc, item, ra, cb, frame * cb)
                    store_block(cut, part, frame, table[0], place * half, keep_ref, send_ref)
                cut = kv_acc[pl.ds(pl.multiple_of(item * ra, 16), ra), 2 * frame * cb : 2 * (frame + 1) * cb].astype(BF)
                store_block(cut, part, frame, table[0], 3 * half, keep_ref, send_ref)


def deal_kernel(table, *refs, at, items, group):
    out_ref = refs[-1]
    count = (len(refs) - 1) // group
    for part in range(group):
        sources = refs[part * count : (part + 1) * count]
        if count == 1:
            out_ref[part] = sources[0][0, 0].astype(out_ref.dtype)
            continue
        slot_of = table[at + items + pl.program_id(0) * group + part]
        for slot, ref in enumerate(sources):

            @pl.when(slot_of == slot)
            def _(ref=ref, part=part):
                out_ref[part] = ref[0, 0].astype(out_ref.dtype)


def land_kernel(keep, got, *refs):
    outs = refs[-2:]
    for half, out in enumerate(outs):
        out[...] = (keep[0, half].astype(F32) + got[0, half].astype(F32)).astype(BF)[None]


def finish_mlp_kernel(sum_ref, *refs):
    up, down = refs[-2:]
    ra, cb = up.shape
    up[:, : cb // 2] = sum_ref[:ra].astype(F32)
    up[:, cb // 2 :] = sum_ref[ra : 2 * ra].astype(F32)
    down[...] = untall(sum_ref[2 * ra :].astype(F32))


def finish_mid_kernel(keep, got, *refs):
    outs = refs[-4:]
    half = outs[0].shape[0] // 2
    total = keep[...].astype(F32) + got[...].astype(F32)
    for place in range(3):
        outs[place][...] = untall(total[place * half : (place + 1) * half])
    outs[3][...] = total[3 * half :]


def finish_qkv_kernel(keep, got, *refs):
    out = refs[-1]
    ra = out.shape[0]
    total = keep[...].astype(F32) + got[...].astype(F32)
    out[:, :PACK] = total[:ra]
    out[:, PACK:] = untall(total[ra:])


def untall(block):
    half = block.shape[1] // 2
    return jnp.concatenate([block[:, :half], block[:, half:]], 0)


def cost(flops, moved, exps=0):
    return pl.CostEstimate(flops=int(flops), bytes_accessed=int(moved), transcendentals=int(exps))


def params():
    return pltpu.CompilerParams(vmem_limit_bytes=LIMIT)


def whole(shape):
    return pl.BlockSpec(shape, lambda *_: (0,) * len(shape), pipeline_mode=pl.Buffered(1))


def run(kernel, name, grid, in_specs, args, out_specs, out_shape, scratch=(), deps=(), work=None, aliases=None):
    inputs = len(args)

    def body(*refs):
        kernel(*refs[:inputs], *refs[inputs + len(deps) :])

    return pl.pallas_call(
        body,
        grid_spec=pltpu.PrefetchScalarGridSpec(
            num_scalar_prefetch=1,
            grid=grid,
            in_specs=list(in_specs) + [pl.BlockSpec(memory_space=pl.ANY)] * len(deps),
            out_specs=out_specs,
            scratch_shapes=list(scratch),
        ),
        out_shape=out_shape,
        input_output_aliases=aliases or {},
        compiler_params=params(),
        cost_estimate=work,
        name=name,
    )(*args, *deps)


def any_spec(count):
    return [pl.BlockSpec(memory_space=pl.ANY)] * count


def struct(shape, dtype):
    return jax.ShapeDtypeStruct(shape, dtype)


def start_call(where, lengths, text_lengths, items, nf):
    size = 2 + 3 * (items // nf) + 3 * items
    smem = pl.BlockSpec(memory_space=pltpu.SMEM)
    return pl.pallas_call(
        partial(start_kernel, items=items, nf=nf),
        in_specs=[smem] * 3,
        out_specs=smem,
        out_shape=struct((size,), jnp.int32),
        name="start",
    )(where, lengths, text_lengths)


def gather_first_call(table, rows, nf):
    items, block, width = rows.shape
    per = items // nf
    at = 2 + 3 * per + 2 * items
    return run(
        copy_kernel,
        "gather_first",
        (nf,),
        [pl.BlockSpec((1, block, width), lambda t, s: (s[at + t * per], 0, 0))],
        (table, rows),
        pl.BlockSpec((1, block, width), lambda t, s: (t, 0, 0)),
        struct((nf, block, width), BF),
    )


def gather_call(table, rows, text, cot, nf):
    items, block, width = rows.shape
    per = items // nf
    at = 2 + 3 * per + 2 * items
    short = text.shape[1]

    def source(size, slot):
        return pl.BlockSpec((1, size, width), lambda t, s: (s[at + t * per + slot], 0, 0))

    return run(
        partial(gather_kernel, per=per),
        "gather",
        (nf,),
        [source(block, 1)] + [source(short, slot) for slot in range(per)] + [source(block, slot) for slot in range(per)],
        (table, rows) + (text,) * per + (cot,) * per,
        [
            pl.BlockSpec((1, block + per * short, width), lambda t, s: (t, 0, 0)),
            pl.BlockSpec((1, per, block, width), lambda t, s: (t, 0, 0, 0)),
        ],
        [struct((nf, block + per * short, width), BF), struct((nf, per, block, width), BF)],
    )


def gate_call(arrays, deps):
    return pl.pallas_call(
        gate_kernel,
        in_specs=any_spec(len(arrays) + len(deps)),
        out_specs=any_spec(len(arrays)),
        out_shape=[struct(array.shape, array.dtype) for array in arrays],
        input_output_aliases={at: at for at in range(len(arrays))},
        compiler_params=params(),
        name="gate",
    )(*arrays, *deps)


def halves(ni, nf, depth, total):
    spec = pl.BlockSpec((FIN, nf // 2, depth, PACK), lambda t, s: (jnp.maximum(t - total, 0), 0, 0, 0))
    return [spec] * 2, [struct((ni, nf // 2, depth, PACK), BF)] * 2


def self_fwd_call(table, slot, rows, mod, weight, kept, per, block, qb, score_scale, deps):
    blocks, _, width = rows.shape
    count = blocks * block
    pairs = H // 2

    def early(t):
        return jnp.minimum(t, blocks - 1)

    def late(t):
        return jnp.maximum(t - blocks, 0)

    return run(
        partial(self_fwd_kernel, blocks=blocks, qb=qb, score_scale=score_scale, length_at=2 + per + slot),
        "self_fwd",
        (blocks + pairs,),
        [pl.BlockSpec((1, block, width), lambda t, s: (early(t), 0, 0))]
        + [pl.BlockSpec((1, 9, width), lambda t, s: (slot, 0, 0)), whole(weight.shape)]
        + any_spec(len(kept)),
        (table, rows, mod, weight, *kept),
        [
            pl.BlockSpec((1, block, width), lambda t, s: (slot, early(t), 0)),
            pl.BlockSpec((1, block, 3 * width), lambda t, s: (slot, early(t), 0)),
            pl.BlockSpec((1, count, 128), lambda t, s: (slot, 0, late(t))),
            pl.BlockSpec((1, 1, 2, count), lambda t, s: (slot, late(t), 0, 0)),
        ],
        [
            struct((per, count, width), BF),
            struct((per, count, 3 * width), BF),
            struct((per, count, width), BF),
            struct((per, pairs, 2, count), F32),
        ],
        scratch=[pltpu.VMEM((3 * pairs, count, 128), BF)],
        deps=deps,
        work=cost(6 * count * width * width + 16 * count * count * width, count * width * 16, H * count * count),
        aliases={4 + at: at for at in range(len(kept))},
    )


def self_bwd_call(
    table, slot, qkv, att, d_att, lse, rows, g1, mod, weight, early, text, qb, score_scale, block, nf, ni, deps
):
    per, count, width = att.shape
    pairs = H // 2
    blocks = count // block
    last = early is not None
    steps = pairs + blocks
    lines = block if last else block + text.shape[1] * text.shape[2]

    def pair(t):
        return jnp.minimum(t, pairs - 1)

    def row(t):
        return jnp.clip(t - pairs, 0, blocks - 1)

    def row_early(t):
        return jnp.clip(t - pairs - blocks, 0, blocks - 1)

    column = pl.BlockSpec((1, count, 128), lambda t, s: (slot, 0, pair(t)))
    by_row = pl.BlockSpec((1, block, width), lambda t, s: (slot, row(t), 0))
    in_specs = [
        pl.BlockSpec((1, count, 128), lambda t, s, part=part: (slot, 0, part * pairs + pair(t))) for part in range(3)
    ] + [column, column, pl.BlockSpec((1, 1, 2, count), lambda t, s: (slot, pair(t), 0, 0))]
    in_specs += [by_row, by_row, pl.BlockSpec((1, 9, width), lambda t, s: (slot, 0, 0)), whole(weight.shape)]
    args = [table, qkv, qkv, qkv, att, d_att, lse, rows, g1, mod, weight]
    out_specs = [
        pl.BlockSpec((1, lines, width), lambda t, s: (row(t), 0, 0)),
        pl.BlockSpec((1, 2, width), lambda t, s: (0, 0, 0)),
    ]
    out_shape = [struct((blocks, lines, width), BF), struct((1, 2, width), F32)]
    scratch = [pltpu.VMEM((3 * pairs, count, 128), BF)] + [pltpu.VMEM((count, 128), F32)] * 2
    if last:
        in_specs += [
            pl.BlockSpec((block, 3 * width), lambda t, s: (row_early(t), 0)),
            pl.BlockSpec((1, block, width), lambda t, s: (slot - 1, row_early(t), 0)),
            pl.BlockSpec((1, 9, width), lambda t, s: (slot - 1, 0, 0)),
        ]
        args += [early, rows, mod]
        specs, shapes = halves(ni, nf, 3 * width * width // (nf * ni * PACK), steps + blocks)
        out_specs += specs
        out_shape += shapes
        scratch += [pltpu.VMEM((width, 3 * width), F32)]
        steps += blocks + ni // FIN
    else:
        in_specs += [pl.BlockSpec((1,) + text.shape[1:], lambda t, s: (row(t), 0, 0, 0))]
        args += [text]
        out_specs += [pl.BlockSpec((block, 3 * width), lambda t, s: (row(t), 0))]
        out_shape += [struct((count, 3 * width), BF)]
    return run(
        partial(
            self_bwd_kernel,
            slot=slot,
            length_at=2 + per + slot,
            pairs=pairs,
            blocks=blocks,
            qb=qb,
            score_scale=score_scale,
            nf=nf,
            ni=ni,
            last=last,
        ),
        "self_bwd",
        (steps,),
        in_specs,
        args,
        out_specs,
        out_shape,
        scratch=scratch,
        deps=deps,
        work=cost(40 * count * count * width + 12 * count * width * width, count * width * 30, H * count * count),
    )


def cross_call(table, att, rows, mod, text, short, wkv, wo, wq, wco, score_scale, block, deps):
    items, count, width = rows.shape
    nf, lines, _ = text.shape
    skip = lines // short - items
    slots = nf * short
    row = pl.BlockSpec((1, block, width), lambda i, j, s: (i, j, 0))
    return run(
        partial(cross_kernel, score_scale=score_scale, length_at=2 + 2 * items),
        "cross_fwd",
        (items, count // block),
        [
            row,
            row,
            pl.BlockSpec((1, 9, width), lambda i, j, s: (i, 0, 0)),
            pl.BlockSpec((nf, short, width), lambda i, j, s: (0, skip + i, 0)),
            whole(wkv.shape),
            whole(wo.shape),
            whole(wq.shape),
            whole(wco.shape),
        ],
        (table, att, rows, mod, text, wkv, wo, wq, wco),
        [pl.BlockSpec((1, slots, 2 * width), lambda i, j, s: (i, 0, 0))]
        + [pl.BlockSpec((1, slots, width), lambda i, j, s: (i, 0, 0))]
        + [row] * 6
        + [pl.BlockSpec((1, H // 2, 2, block), lambda i, j, s: (i, 0, 0, j))],
        [struct((items, slots, 2 * width), BF), struct((items, slots, width), BF)]
        + [struct(rows.shape, BF)] * 6
        + [struct((items, H // 2, 2, count), F32)],
        deps=deps,
        work=cost(
            items * count * (6 * width * width + 16 * slots * width), items * count * width * 20, items * H * count * slots
        ),
    )


def back_grid(items, count, block):
    blocks = count // block
    total = items * blocks

    def at(t):
        return jnp.minimum(t, total - 1)

    def by_item(t, s):
        return (at(t) // blocks, 0, 0)

    def by_row(t, s):
        return (at(t) // blocks, at(t) % blocks, 0)

    return blocks, total, by_item, by_row


def mlp_call(table, second, cot, mod, wup, wdn, block, chunk, nf, ni, deps):
    items, count, width = second.shape
    ff = wup.shape[1]
    blocks, total, by_item, by_row = back_grid(items, count, block)
    row = pl.BlockSpec((1, block, width), by_row)
    shard = pl.BlockSpec((1, 1, block, width), lambda t, s: (by_row(t, s)[1], by_row(t, s)[0], 0, 0))
    depth = 2 * width * ff // (nf * ni * PACK)
    return run(
        partial(mlp_kernel, blocks=blocks, total=total, chunk=chunk, nf=nf, ni=ni),
        "mlp",
        (total + ni // FIN,),
        [row, shard, pl.BlockSpec((1, 9, width), by_item), whole(wup.shape), whole(wdn.shape)],
        (table, second, cot, mod, wup, wdn),
        [shard, row, pl.BlockSpec((1, 3, width), by_item)]
        + [pl.BlockSpec((FIN, nf, depth, PACK), lambda t, s: (jnp.maximum(t - total, 0), 0, 0, 0))],
        [struct(cot.shape, BF), struct(second.shape, BF), struct((items, 3, width), F32)]
        + [struct((ni, nf, depth, PACK), BF)],
        scratch=[pltpu.VMEM((width, ff), F32), pltpu.VMEM((ff, width), F32)],
        deps=deps,
        work=cost(12 * items * count * width * ff, items * count * width * 16, items * count * ff * 2),
    )


def cross_back_call(
    table, g2, bb, cr, cq, att, ba, first, mod, kv, lse, text, wo, wq, wco, wkv, score_scale, block, nf, ni, deps
):
    items, count, width = g2.shape
    slots = kv.shape[1]
    short = slots // nf
    blocks, total, by_item, by_row = back_grid(items, count, block)
    row = pl.BlockSpec((1, block, width), by_row)
    by_slot = pl.BlockSpec((nf, 1, short, width), lambda t, s: (0, by_item(t, s)[0], 0, 0))
    specs, shapes = halves(ni, nf, 5 * width * width // (nf * ni * PACK), total)
    lse_spec = pl.BlockSpec((1, H // 2, 2, block), lambda t, s: (by_row(t, s)[0], 0, 0, by_row(t, s)[1]))
    return run(
        partial(
            cross_back_kernel,
            blocks=blocks,
            total=total,
            score_scale=score_scale,
            nf=nf,
            ni=ni,
            length_at=2 + 2 * items,
        ),
        "cross_bwd",
        (total + ni // FIN,),
        [row] * 7
        + [pl.BlockSpec((1, 9, width), by_item), pl.BlockSpec((1, slots, 2 * width), by_item), lse_spec]
        + [pl.BlockSpec((1, slots, width), by_item)]
        + [whole(weight.shape) for weight in (wo, wq, wco, wkv)],
        (table, g2, bb, cr, cq, att, ba, first, mod, kv, lse, text, wo, wq, wco, wkv),
        [row, row, by_slot, pl.BlockSpec((1, 4, width), by_item)] + specs,
        [struct(g2.shape, BF)] * 2 + [struct((nf, items, short, width), BF), struct((items, 4, width), F32)] + shapes,
        scratch=[pltpu.VMEM((width, width), F32)] * 3
        + [pltpu.VMEM((width, 2 * width), F32), pltpu.VMEM((slots, 2 * width), F32)],
        deps=deps,
        work=cost(
            items * count * (12 * width * width + 40 * slots * width), items * count * width * 24, items * H * count * slots
        ),
    )


def deal_call(table, got, per, block, skip, dtype, name, deps=(), group=2):
    nf, _, _, width = got[0].shape
    items = nf * per
    at = 2 + 3 * per
    specs = []
    for part in range(group):
        if len(got) == 1:
            specs.append(
                pl.BlockSpec(
                    (1, 1, block, width),
                    lambda t, s, part=part: (s[at + t * group + part], 0, skip + s[at + items + t * group + part], 0),
                )
            )
        else:
            specs += [
                pl.BlockSpec((1, 1, block, width), lambda t, s, part=part: (s[at + t * group + part], 0, 0, 0))
            ] * len(got)
    return run(
        partial(deal_kernel, at=at, items=items, group=group),
        name,
        (items // group,),
        specs,
        (table,) + tuple(got) * group,
        pl.BlockSpec((group, block, width), lambda t, s: (t, 0, 0)),
        struct((items, block, width), dtype),
        deps=deps,
        work=cost(0, items * block * width * 6),
    )


def small_call(kernel, name, args, out_shape, deps=()):
    return pl.pallas_call(
        kernel,
        in_specs=[pl.BlockSpec(arg.shape, lambda: (0,) * arg.ndim) for arg in args] + any_spec(len(deps)),
        out_specs=[pl.BlockSpec(out.shape, lambda: (0,) * len(out.shape)) for out in out_shape],
        out_shape=out_shape,
        compiler_params=params(),
        name=name,
    )(*args, *deps)


def exchange(blocks):
    return lax.all_to_all(blocks, "frames", 0, 0, tiled=True)


def swap(block, offset, nf):
    if offset == 0:
        return block
    return lax.ppermute(block, "frames", [(i, i ^ offset) for i in range(nf)])


def bits_of(count):
    return count.bit_length() - 1


class Sum:
    def __init__(self, keep, send, order, sizes):
        self.sizes = sizes
        ni, nf = sizes["items"], sizes["frames"]
        self.dims = [("items", bit) for bit in reversed(range(bits_of(ni)))]
        self.dims += [("frames", bit) for bit in reversed(range(1, bits_of(nf)))]
        shape = (2,) * len(self.dims) + keep.shape[2:]
        self.keep, self.send = keep.reshape(shape), send
        self.shape = shape
        self.steps = [("frames", 0)] + list(order)
        self.got = None

    def launch(self):
        name, bit = self.steps.pop(0)
        self.got = lax.ppermute(self.send, name, [(i, i ^ (1 << bit)) for i in range(self.sizes[name])])

    def land(self, deps=()):
        got = self.got.reshape(self.keep.shape)
        if not self.steps:
            return self.keep, got
        dim = self.dims.index(self.steps[0])
        self.dims.remove(self.steps[0])
        shape = self.keep.shape
        outer, inner = 2**dim, 2 ** (len(shape) - 3 - dim)
        view = (outer, 2, inner) + shape[-2:]
        out = struct((outer, inner) + shape[-2:], BF)
        source = pl.BlockSpec((1,) + view[1:], lambda t: (t, 0, 0, 0, 0))
        target = pl.BlockSpec((1,) + out.shape[1:], lambda t: (t, 0, 0, 0))
        self.keep, self.send = pl.pallas_call(
            land_kernel,
            grid=(outer,),
            in_specs=[source] * 2 + any_spec(len(deps)),
            out_specs=[target] * 2,
            out_shape=[out] * 2,
            compiler_params=params(),
            name="land",
        )(self.keep.reshape(view), got.reshape(view), *deps)
        left = shape[:dim] + shape[dim + 1 :]
        self.keep = self.keep.reshape(left)
        return None


def collect_items(rows, ni):
    for bit in range(bits_of(ni)):
        rows = jnp.concatenate([rows, lax.ppermute(rows, "items", [(i, i ^ (1 << bit)) for i in range(ni)])], 0)
    return rows


def items_whole(
    ni, nf, frames_in, cond, text, item_lengths, text_lengths, ada_weight, qkv_weight, out_weight,
    cross_q_weight, cross_kv_weight, cross_out_weight, up_weight, down_weight, cotangent,
):
    items, block, width = frames_in.shape
    per = items // nf
    ff = up_weight.shape[1]
    sizes = {"items": ni, "frames": nf}
    score_scale = (width // H) ** (-0.5)
    me = lax.axis_index("frames")
    row_item = lax.axis_index("items")
    x_first = [("items", bit) for bit in range(bits_of(ni))] + [("frames", bit) for bit in range(1, bits_of(nf))]

    table = start_call(jnp.stack([me, row_item]), item_lengths, text_lengths, items, nf)
    rows_first = exchange(gather_first_call(table, frames_in, nf))
    mixed_send, cot_send = gather_call(table, frames_in, text, cotangent, nf)

    cond_f = cond.astype(F32)
    low_cond = jax.nn.silu(cond_f).astype(BF)
    modulation = nn(low_cond, ada_weight)
    pick = table[2 : 2 + per, None] == jnp.arange(items, dtype=jnp.int32)[None, :]
    mod = jnp.sum(jnp.where(pick[:, :, None], modulation[None], 0.0), 1).reshape(per, 9, width)

    (mixed_send,) = gate_call([mixed_send], [rows_first, mod])
    mixed = exchange(mixed_send)
    kept = self_fwd_call(table, 0, rows_first, mod, qkv_weight, (), per, block, 512, score_scale, [mixed_send])
    (cot_send,) = gate_call([cot_send], [mixed])
    cot = exchange(cot_send)
    kept = self_fwd_call(table, 1, mixed, mod, qkv_weight, kept, per, block, 512, score_scale, [cot_send])
    rows, qkv, attended, self_lse = kept
    text_kv, text_rows, first, second, branch_a, branch_b, cross_q, crossed, cross_lse = cross_call(
        table, attended, rows, mod, mixed, text.shape[1], cross_kv_weight, out_weight, cross_q_weight, cross_out_weight,
        score_scale, 2 * block, [],
    )
    layer_send, g2, dmod_c, g_mlp = mlp_call(
        table, second, cot, mod, up_weight, down_weight, block, 768, nf, ni, []
    )
    layer_got = exchange(layer_send)
    sum_mlp = lax.psum_scatter(
        g_mlp.reshape((ni * nf,) + g_mlp.shape[2:]), ("items", "frames"), scatter_dimension=0, tiled=True
    )[0]
    g1, d_att, text_back, dmod_b, mid_keep, mid_send = cross_back_call(
        table, g2, branch_b, crossed, cross_q, attended, branch_a, first, mod, text_kv, cross_lse, text_rows,
        out_weight, cross_q_weight, cross_out_weight, cross_kv_weight, score_scale, 2 * block, nf, ni, [],
    )
    mid = Sum(mid_keep, mid_send, x_first, sizes)
    mid.launch()
    made_0, dmod_0, early = self_bwd_call(
        table, 0, qkv, attended, d_att, self_lse, rows, g1, mod, qkv_weight, None, text_back, 1024, score_scale, block, nf, ni,
        [layer_got],
    )
    mid.land()
    mid.launch()
    got_0 = exchange(made_0)
    made_1, dmod_1, grad_keep, grad_send = self_bwd_call(
        table, 1, qkv, attended, d_att, self_lse, rows, g1, mod, qkv_weight, early, None, 1024, score_scale, block, nf, ni,
        [mid.send],
    )
    made_1, grad_send = gate_call([made_1, grad_send], [mid.got, got_0, sum_mlp])
    grad = Sum(grad_keep, grad_send, x_first, sizes)
    grad.launch()
    got_1 = exchange(made_1)
    layer_got = layer_got.reshape(nf, 1, per * block, width)
    layer_out = deal_call(table, [layer_got], per, block, 0, BF, "deal_out")
    grad.land([layer_out])
    grad.launch()
    mid.land([grad.send])
    mid.launch()
    text_grad = deal_call(
        table, [got_0[:, None]], per, text.shape[1], block // text.shape[1], F32, "deal_text", [mid.send]
    )
    (dmod_1,) = gate_call([dmod_1], [text_grad])
    d_mod = jnp.concatenate([jnp.concatenate([dmod_0, dmod_1], 0), dmod_b, dmod_c], 1).reshape(per, 9 * width)
    ada_rows, ada_cols, cond_cols = width // ni, 9 * width // nf, width // nf
    high = d_mod.astype(BF)
    rest = (d_mod - high.astype(F32)).astype(BF)
    parts = nt(jnp.concatenate([high, rest], 0), ada_weight)
    parts = jnp.concatenate(
        [d_mod.reshape(per, nf, ada_cols), (parts[:per] + parts[per:]).reshape(per, nf, cond_cols)], 2
    ).transpose(1, 0, 2)
    mid.land([parts])
    mid.launch()
    (parts,) = gate_call([parts], [got_1, mid.send])
    parts = exchange(parts).reshape(items, ada_cols + cond_cols)
    input_grad = deal_call(table, [got_0[:, None], got_1[:, None]], per, block, 0, F32, "deal_in", [mid.send])
    grad.land([input_grad])
    grad.launch()
    mid.land([grad.send])
    mid.launch()
    at = 2 + 3 * per
    spot = table[at : at + items] * per + table[at + items : at + 2 * items]
    pick_row = spot[:, None] == jnp.arange(items, dtype=jnp.int32)[None, :]
    parts = jnp.sum(jnp.where(pick_row[:, :, None], parts[None], 0.0), 1)
    every = collect_items(jnp.concatenate([parts[:, :ada_cols], low_cond.astype(F32)], 1), ni)
    grad_ada = lax.dot_general(
        lax.dynamic_slice(every, (0, ada_cols + row_item * ada_rows), (items * ni, ada_rows), allow_negative_indices=False),
        every[:, :ada_cols],
        (((0,), (0,)), ((), ())),
        precision=lax.Precision.HIGHEST,
        preferred_element_type=F32,
    )
    cond_mine = lax.dynamic_slice(cond_f, (0, me * cond_cols), (items, cond_cols), allow_negative_indices=False)
    sigmoid_c = jax.nn.sigmoid(cond_mine)
    cond_grad = parts[:, ada_cols:] * (sigmoid_c * (1.0 + cond_mine * (1.0 - sigmoid_c)))

    grad_up, grad_down = small_call(
        finish_mlp_kernel,
        "finish_mlp",
        [sum_mlp],
        [struct((width // ni, ff // nf), F32), struct((ff // ni, width // nf), F32)],
        [grad.send],
    )
    while grad.steps:
        grad.land()
        grad.launch()
    mid_sum = mid.land()
    square = struct((ada_rows, cond_cols), F32)
    grad_out, grad_cross_q, grad_cross_out, grad_cross_kv = small_call(
        finish_mid_kernel, "finish_mid", mid_sum, [square] * 3 + [struct((ada_rows, 2 * cond_cols), F32)]
    )
    (grad_qkv,) = small_call(finish_qkv_kernel, "finish_qkv", grad.land(), [struct((ada_rows, 3 * cond_cols), F32)])
    return (
        layer_out,
        input_grad,
        text_grad,
        cond_grad,
        grad_ada,
        grad_qkv,
        grad_out,
        grad_cross_q,
        grad_cross_kv,
        grad_cross_out,
        grad_up,
        grad_down,
    )


def on_device(mesh, *args):
    ni, nf = mesh.shape["items"], mesh.shape["frames"]
    if nf == 4 and args[0].shape[0] == 2 * nf and args[0].shape[-1] == 768 and 768 % (32 * ni) == 0:
        return items_whole(ni, nf, *args)
    return frames_split(*args)


def solution(mesh):
    in_specs = (
        P("items", "frames", None),
        P("items", None),
        P("items", "frames", None),
        P("items"),
        P("items"),
        P(),
        P(),
        P(),
        P(),
        P(),
        P(),
        P(),
        P(),
        P("items", "frames", None),
    )
    out_specs = (
        P("items", "frames", None),
        P("items", "frames", None),
        P("items", "frames", None),
        P("items", "frames"),
        P("items", "frames"),
        P("items", "frames"),
        P("items", "frames"),
        P("items", "frames"),
        P("items", "frames"),
        P("items", "frames"),
        P("items", "frames"),
        P("items", "frames"),
    )
    return jax.shard_map(
        partial(on_device, mesh), mesh=mesh, in_specs=in_specs, out_specs=out_specs, check_vma=False
    )
```

```python
import functools
from functools import partial

import jax
import jax.numpy as jnp
from jax import lax
from jax.experimental import pallas as pl
from jax.experimental.pallas import tpu as pltpu
from jax.sharding import PartitionSpec as P

H = 12


def norm_parts(tensor):
    centered = tensor - jnp.mean(tensor, -1, keepdims=True)
    inverse = lax.rsqrt(jnp.mean(centered * centered, -1, keepdims=True) + 1e-06)
    return (centered * inverse, inverse)


def norm_back(normed, inverse, incoming):
    return inverse * (
        incoming
        - jnp.mean(incoming, -1, keepdims=True)
        - normed * jnp.mean(incoming * normed, -1, keepdims=True)
    )


def split_heads(tensor):
    return tensor.reshape(tensor.shape[0], tensor.shape[1], H, -1)


def attend(queries, keys_in, values_in, key_valid, score_scale):
    scores = (
        jnp.einsum(
            "ifhd,ijhd->ihfj",
            split_heads(queries),
            split_heads(keys_in),
            preferred_element_type=jnp.float32,
        )
        * score_scale
    )
    scores = jnp.where(key_valid[:, None, None, :], scores, -1e30)
    attn_prob = jax.nn.softmax(scores, axis=-1)
    log_total = jax.nn.logsumexp(scores, axis=-1)
    low_prob = attn_prob.astype(jnp.bfloat16)
    mixed = jnp.einsum(
        "ihfj,ijhd->ifhd", low_prob, split_heads(values_in), preferred_element_type=jnp.float32
    )
    return (attn_prob, low_prob, mixed.astype(jnp.bfloat16).reshape(queries.shape), log_total)


def attend_back(grad_mixed, queries, keys_in, values_in, attn_prob, low_prob, score_scale):
    grad_heads = split_heads(grad_mixed)
    grad_prob = jnp.einsum(
        "ifhd,ijhd->ihfj", grad_heads, split_heads(values_in), preferred_element_type=jnp.float32
    )
    grad_values = jnp.einsum(
        "ihfj,ifhd->ijhd", low_prob, grad_heads, preferred_element_type=jnp.float32
    )
    grad_scores = (
        attn_prob * (grad_prob - jnp.sum(attn_prob * grad_prob, -1, keepdims=True))
    ).astype(jnp.bfloat16)
    grad_queries = (
        jnp.einsum(
            "ihfj,ijhd->ifhd", grad_scores, split_heads(keys_in), preferred_element_type=jnp.float32
        )
        * score_scale
    )
    grad_keys = (
        jnp.einsum(
            "ihfj,ifhd->ijhd", grad_scores, split_heads(queries), preferred_element_type=jnp.float32
        )
        * score_scale
    )
    return (
        grad_queries.reshape(queries.shape),
        grad_keys.reshape(keys_in.shape),
        grad_values.reshape(values_in.shape),
    )


def project(tensor, weight):
    return jnp.einsum("ifd,de->ife", tensor, weight, preferred_element_type=jnp.float32)


def project_back(tensor, weight):
    return jnp.einsum("ife,de->ifd", tensor, weight, preferred_element_type=jnp.float32)


def weight_grad(left, right):
    return jnp.einsum("ifd,ife->de", left, right, preferred_element_type=jnp.float32)


def frames_split(
    frames_in,
    cond,
    text,
    item_lengths,
    text_lengths,
    ada_weight,
    qkv_weight,
    out_weight,
    cross_q_weight,
    cross_kv_weight,
    cross_out_weight,
    up_weight,
    down_weight,
    cotangent,
):
    model_width = frames_in.shape[-1]
    score_scale = (model_width // H) ** (-0.5)
    cond_f = cond.astype(jnp.float32)
    low_cond = jax.nn.silu(cond_f).astype(jnp.bfloat16)
    modulation = jnp.dot(low_cond, ada_weight, preferred_element_type=jnp.float32)
    pieces = [
        modulation[:, None, position * model_width : (position + 1) * model_width]
        for position in range(9)
    ]
    shift_a, scale_a, gate_a, shift_b, scale_b, gate_b, shift_c, scale_c, gate_c = pieces
    residual_in = frames_in.astype(jnp.float32)
    normed_a, inverse_a = norm_parts(residual_in)
    hidden_a = (normed_a * (1.0 + scale_a) + shift_a).astype(jnp.bfloat16)
    qkv = project(hidden_a, qkv_weight).astype(jnp.bfloat16)
    queries = qkv[..., :model_width]
    keys_own = qkv[..., model_width : 2 * model_width]
    values_own = qkv[..., 2 * model_width :]
    keys_all, values_all = (
        lax.all_gather(keys_own, "frames", axis=1, tiled=True),
        lax.all_gather(values_own, "frames", axis=1, tiled=True),
    )
    key_valid = jnp.arange(keys_all.shape[1], dtype=jnp.int32)[None, :] < item_lengths[:, None]
    attn_prob, low_prob, attended, self_total = attend(
        queries, keys_all, values_all, key_valid, score_scale
    )
    branch_a = project(attended, out_weight)
    first = residual_in + gate_a * branch_a
    normed_b, inverse_b = norm_parts(first)
    hidden_b = (normed_b * (1.0 + scale_b) + shift_b).astype(jnp.bfloat16)
    cross_q = project(hidden_b, cross_q_weight).astype(jnp.bfloat16)
    text_own = project(text, cross_kv_weight).astype(jnp.bfloat16)
    text_kv = lax.all_gather(text_own, "frames", axis=1, tiled=True)
    text_keys = text_kv[..., :model_width]
    text_values = text_kv[..., model_width:]
    text_valid = jnp.arange(text_kv.shape[1], dtype=jnp.int32)[None, :] < text_lengths[:, None]
    cross_prob, cross_low, crossed, cross_total = attend(
        cross_q, text_keys, text_values, text_valid, score_scale
    )
    branch_b = project(crossed, cross_out_weight)
    second = first + gate_b * branch_b
    normed_c, inverse_c = norm_parts(second)
    hidden_c = (normed_c * (1.0 + scale_c) + shift_c).astype(jnp.bfloat16)
    up_proj = project(hidden_c, up_weight)
    activated, gelu_back = jax.vjp(partial(jax.nn.gelu, approximate=False), up_proj)
    low_act = activated.astype(jnp.bfloat16)
    branch_c = project(low_act, down_weight)
    layer_out = (second + gate_c * branch_c).astype(jnp.bfloat16)
    upstream = cotangent.astype(jnp.float32)
    d_gate_c = jnp.sum(upstream * branch_c, 1)
    d_branch_c = (upstream * gate_c).astype(jnp.bfloat16)
    grad_down = weight_grad(low_act, d_branch_c)
    d_up = gelu_back(project_back(d_branch_c, down_weight))[0].astype(jnp.bfloat16)
    grad_up = weight_grad(hidden_c, d_up)
    d_hidden_c = project_back(d_up, up_weight)
    d_shift_c = jnp.sum(d_hidden_c, 1)
    d_scale_c = jnp.sum(d_hidden_c * normed_c, 1)
    upstream = upstream + norm_back(normed_c, inverse_c, d_hidden_c * (1.0 + scale_c))
    d_gate_b = jnp.sum(upstream * branch_b, 1)
    d_branch_b = (upstream * gate_b).astype(jnp.bfloat16)
    grad_cross_out = weight_grad(crossed, d_branch_b)
    d_crossed = project_back(d_branch_b, cross_out_weight).astype(jnp.bfloat16)
    d_cross_q, d_text_keys, d_text_values = attend_back(
        d_crossed, cross_q, text_keys, text_values, cross_prob, cross_low, score_scale
    )
    d_cross_q = d_cross_q.astype(jnp.bfloat16)
    grad_cross_q = weight_grad(hidden_b, d_cross_q)
    d_hidden_b = project_back(d_cross_q, cross_q_weight)
    d_text_local = jnp.concatenate([d_text_keys, d_text_values], -1)
    d_shift_b = jnp.sum(d_hidden_b, 1)
    d_scale_b = jnp.sum(d_hidden_b * normed_b, 1)
    upstream = upstream + norm_back(normed_b, inverse_b, d_hidden_b * (1.0 + scale_b))
    d_gate_a = jnp.sum(upstream * branch_a, 1)
    d_branch_a = (upstream * gate_a).astype(jnp.bfloat16)
    grad_out = weight_grad(attended, d_branch_a)
    d_attended = project_back(d_branch_a, out_weight).astype(jnp.bfloat16)
    keys_back, values_back = (
        lax.all_gather(keys_own, "frames", axis=1, tiled=True),
        lax.all_gather(values_own, "frames", axis=1, tiled=True),
    )
    d_queries, d_keys_all, d_values_all = attend_back(
        d_attended, queries, keys_back, values_back, attn_prob, low_prob, score_scale
    )
    d_keys, d_values = (
        lax.psum_scatter(
            d_keys_all.astype(jnp.bfloat16), "frames", scatter_dimension=1, tiled=True
        ).astype(jnp.float32),
        lax.psum_scatter(
            d_values_all.astype(jnp.bfloat16), "frames", scatter_dimension=1, tiled=True
        ).astype(jnp.float32),
    )
    d_qkv = jnp.concatenate(
        [
            d_queries.astype(jnp.bfloat16),
            d_keys.astype(jnp.bfloat16),
            d_values.astype(jnp.bfloat16),
        ],
        -1,
    )
    grad_qkv = weight_grad(hidden_a, d_qkv)
    d_hidden_a = project_back(d_qkv, qkv_weight)
    d_shift_a = jnp.sum(d_hidden_a, 1)
    d_scale_a = jnp.sum(d_hidden_a * normed_a, 1)
    input_grad = upstream + norm_back(normed_a, inverse_a, d_hidden_a * (1.0 + scale_a))
    d_modulation = jnp.concatenate(
        [
            d_shift_a,
            d_scale_a,
            d_gate_a,
            d_shift_b,
            d_scale_b,
            d_gate_b,
            d_shift_c,
            d_scale_c,
            d_gate_c,
        ],
        -1,
    )
    grad_ada = jnp.dot(
        low_cond.astype(jnp.float32).T,
        d_modulation,
        precision=lax.Precision.HIGHEST,
        preferred_element_type=jnp.float32,
    )
    sigmoid_c = jax.nn.sigmoid(cond_f)
    cond_part = jnp.dot(
        d_modulation,
        ada_weight.T,
        precision=lax.Precision.HIGHEST,
        preferred_element_type=jnp.float32,
    ) * (sigmoid_c * (1.0 + cond_f * (1.0 - sigmoid_c)))
    d_text_kv, cond_grad = (
        lax.psum_scatter(d_text_local, "frames", scatter_dimension=1, tiled=True),
        lax.psum_scatter(cond_part, "frames", scatter_dimension=1, tiled=True),
    )
    low_text_kv = d_text_kv.astype(jnp.bfloat16)
    grad_cross_kv = weight_grad(text, low_text_kv)
    text_grad = project_back(low_text_kv, cross_kv_weight)
    grads = (
        grad_ada,
        grad_qkv,
        grad_out,
        grad_cross_q,
        grad_cross_kv,
        grad_cross_out,
        grad_up,
        grad_down,
    )
    partial_sums = (
        lax.psum_scatter(
            grads[0].astype(jnp.bfloat16), "frames", scatter_dimension=1, tiled=True
        ).astype(jnp.float32),
        lax.psum_scatter(
            grads[1].astype(jnp.bfloat16), "frames", scatter_dimension=1, tiled=True
        ).astype(jnp.float32),
        lax.psum_scatter(
            grads[2].astype(jnp.bfloat16), "frames", scatter_dimension=1, tiled=True
        ).astype(jnp.float32),
        lax.psum_scatter(
            grads[3].astype(jnp.bfloat16), "frames", scatter_dimension=1, tiled=True
        ).astype(jnp.float32),
        lax.psum_scatter(
            grads[4].astype(jnp.bfloat16), "frames", scatter_dimension=1, tiled=True
        ).astype(jnp.float32),
        lax.psum_scatter(
            grads[5].astype(jnp.bfloat16), "frames", scatter_dimension=1, tiled=True
        ).astype(jnp.float32),
        lax.psum_scatter(
            grads[6].astype(jnp.bfloat16), "frames", scatter_dimension=1, tiled=True
        ).astype(jnp.float32),
        lax.psum_scatter(
            grads[7].astype(jnp.bfloat16), "frames", scatter_dimension=1, tiled=True
        ).astype(jnp.float32),
    )
    totals = (
        lax.psum_scatter(
            partial_sums[0].astype(jnp.bfloat16), "items", scatter_dimension=0, tiled=True
        ).astype(jnp.float32),
        lax.psum_scatter(
            partial_sums[1].astype(jnp.bfloat16), "items", scatter_dimension=0, tiled=True
        ).astype(jnp.float32),
        lax.psum_scatter(
            partial_sums[2].astype(jnp.bfloat16), "items", scatter_dimension=0, tiled=True
        ).astype(jnp.float32),
        lax.psum_scatter(
            partial_sums[3].astype(jnp.bfloat16), "items", scatter_dimension=0, tiled=True
        ).astype(jnp.float32),
        lax.psum_scatter(
            partial_sums[4].astype(jnp.bfloat16), "items", scatter_dimension=0, tiled=True
        ).astype(jnp.float32),
        lax.psum_scatter(
            partial_sums[5].astype(jnp.bfloat16), "items", scatter_dimension=0, tiled=True
        ).astype(jnp.float32),
        lax.psum_scatter(
            partial_sums[6].astype(jnp.bfloat16), "items", scatter_dimension=0, tiled=True
        ).astype(jnp.float32),
        lax.psum_scatter(
            partial_sums[7].astype(jnp.bfloat16), "items", scatter_dimension=0, tiled=True
        ).astype(jnp.float32),
    )
    return (
        layer_out,
        input_grad,
        text_grad,
        cond_grad,
        totals[0],
        totals[1],
        totals[2],
        totals[3],
        totals[4],
        totals[5],
        totals[6],
        totals[7],
    )


LOG2E = 1.4426950408889634
BF = jnp.bfloat16
F32 = jnp.float32
PACK = 384
FIN = 2
SUB = 128
BSUB = 256
CSUB = 256
LIMIT = 60 * 2**20


def nn(left, right):
    return jnp.dot(left, right, preferred_element_type=F32)


def nt(left, right):
    return lax.dot_general(left, right, (((1,), (1,)), ((), ())), preferred_element_type=F32)


def tn(left, right):
    return lax.dot_general(left, right, (((0,), (0,)), ((), ())), preferred_element_type=F32)


def ln_parts(rows):
    share = 1.0 / rows.shape[-1]
    centered = rows - jnp.sum(rows, -1, keepdims=True) * share
    inverse = lax.rsqrt(jnp.sum(centered * centered, -1, keepdims=True) * share + 1e-06)
    return centered * inverse, inverse


def ln_back(normed, inverse, incoming):
    share = 1.0 / normed.shape[-1]
    mean_in = jnp.sum(incoming, -1, keepdims=True) * share
    mean_dot = jnp.sum(incoming * normed, -1, keepdims=True) * share
    return inverse * (incoming - mean_in - normed * mean_dot)


def gelu_parts(value):
    size = jnp.abs(value)
    inner = 1.0 / (1.0 + (0.3275911 * 0.7071067811865476) * size)
    series = inner * (
        0.5 * 0.254829592
        + inner
        * (
            0.5 * -0.284496736
            + inner * (0.5 * 1.421413741 + inner * (0.5 * -1.453152027 + inner * (0.5 * 1.061405429)))
        )
    )
    bell = jnp.exp2(value * value * (-0.5 * LOG2E))
    tail = series * bell
    below = jnp.where(value >= 0.0, 1.0 - tail, tail)
    return below, below + value * bell * 0.3989422804014327


def strips(body, *arrays, rows=16):
    made = [body(*(array[at : at + rows] for array in arrays)) for at in range(0, arrays[0].shape[0], rows)]
    if not isinstance(made[0], tuple):
        return jnp.concatenate(made, 0)
    return tuple(jnp.concatenate(column, 0) for column in zip(*made))


def fold(rows):
    return jnp.sum(rows.reshape(rows.shape[0] // 8, 8, rows.shape[1]), 0)


def modulate(rows, shift, scale):
    normed, _ = ln_parts(rows.astype(F32))
    return (normed * (1.0 + scale) + shift).astype(BF)


class Columns:
    def __init__(self, count):
        self.parts = [None] * count

    def add(self, at, rows):
        made = fold(rows)
        self.parts[at] = made if self.parts[at] is None else self.parts[at] + made

    def total(self, at):
        return jnp.sum(self.parts[at], 0, keepdims=True)


def lane_half(half):
    lane = lax.broadcasted_iota(jnp.int32, (1, 128), 1)
    return lane < 64 if half == 0 else lane >= 64


def keep_half(rows, half):
    return jnp.where(lane_half(half), rows, jnp.zeros_like(rows))


def pack_square(acc, item, ra, cb, col):
    first = acc[pl.ds(pl.multiple_of(item * ra, 16), ra // 2), col : col + cb]
    second = acc[pl.ds(pl.multiple_of(item * ra + ra // 2, 16), ra // 2), col : col + cb]
    return jnp.concatenate([first, second], 1).astype(BF)


def store_block(value, part, frame, me, row, keep_ref, send_ref):
    place = frame ^ me

    @pl.when(place & 1 == 0)
    def _():
        keep_ref[part, place >> 1, row : row + value.shape[0]] = value

    @pl.when(place & 1 == 1)
    def _():
        send_ref[part, place >> 1, row : row + value.shape[0]] = value


def start_kernel(where, lengths, text_lengths, table, *, items, nf):
    per = items // nf
    me = where[0]
    table[0] = me
    table[1] = where[1]
    at = 2 + 3 * per
    for i in range(items):
        rank = jnp.int32(0)
        for j in range(items):
            if j < i:
                ahead = lengths[j] >= lengths[i]
            elif j > i:
                ahead = lengths[j] > lengths[i]
            else:
                continue
            rank = rank + ahead.astype(jnp.int32)
        turn, seat = rank // nf, rank % nf
        device = jnp.where(turn % 2 == 0, seat, nf - 1 - seat)
        table[at + i] = device
        table[at + items + i] = turn
        table[at + 2 * items + device * per + turn] = i
    for slot in range(per):
        item = table[at + 2 * items + me * per + slot]
        table[2 + slot] = item
        table[2 + per + slot] = lengths[item]
        table[2 + 2 * per + slot] = text_lengths[item]


def copy_kernel(table, source, out):
    out[...] = source[...]


def gather_kernel(table, *refs, per):
    rows, texts, cots, mixed, cot = refs[0], refs[1 : 1 + per], refs[1 + per : 1 + 2 * per], refs[-2], refs[-1]
    block, short = rows.shape[1], texts[0].shape[1]
    mixed[0, :block] = rows[0]
    for slot in range(per):
        mixed[0, block + slot * short : block + (slot + 1) * short] = texts[slot][0]
        cot[0, slot] = cots[slot][0]


def gate_kernel(*refs):
    pass


def ahead(work, make, use):
    made = make(*work[0])
    for number, item in enumerate(work):
        later = make(*work[number + 1]) if number + 1 < len(work) else None
        use(item, made)
        made = later


def soften(scores):
    top = jnp.max(scores, 1, keepdims=True)
    return jnp.exp2(scores - top).astype(BF), top


def soft_back(scores, d_prob, lse, delta):
    prob = jnp.exp2(scores - lse)
    return prob.astype(BF), (prob * (d_prob - delta)).astype(BF)


def self_fwd_kernel(
    table, x_ref, mod_ref, w_ref, *refs, blocks, qb, score_scale, length_at
):
    rows_ref, qkv_ref, att_ref, lse_ref, held = refs[-5:]
    step = pl.program_id(0)
    width = rows_ref.shape[-1]
    count = att_ref.shape[1]
    block = rows_ref.shape[1]
    pairs = H // 2

    @pl.when(step < blocks)
    def _():
        rows_ref[0] = x_ref[0]
        shift, scale = mod_ref[0, 0:1], mod_ref[0, 1:2]
        hidden = strips(lambda rows: modulate(rows, shift, scale), x_ref[0])
        at = pl.ds(pl.multiple_of(step * block, block), block)
        for part in range(3):
            made = nn(hidden, w_ref[:, part * width : (part + 1) * width])
            if part == 0:
                made = made * (score_scale * LOG2E)
            made = made.astype(BF)
            qkv_ref[0, :, part * width : (part + 1) * width] = made
            for pair in range(pairs):
                held[part * pairs + pair, at] = made[:, pair * 128 : pair * 128 + 128]

    for klen in (count // 4, count // 2, count):

        @pl.when((step >= blocks) & (table[length_at] == klen))
        def _(klen=klen):
            pair = step - blocks
            keys = held[pairs + pair, :klen]
            values = jnp.concatenate([held[2 * pairs + pair, :klen], jnp.ones((klen, 128), BF)], 1)

            def inner(position, carry):
                rows = pl.ds(pl.multiple_of(position * qb, qb), qb)
                queries = held[pair, rows]
                work = [(half, at) for at in range(0, qb, SUB) for half in (0, 1)]
                outs = [[], []]

                def score(half, at):
                    return nt(keep_half(queries[at : at + SUB], half), keys)

                def use(place, scores):
                    half, at = place
                    prob, top = strips(soften, scores)
                    mixed = nn(prob, values)
                    total = mixed[:, 128:]
                    cols = pl.ds(pl.multiple_of(position * qb + at, SUB), SUB)
                    lse_ref[0, 0, half : half + 1, cols] = (top + jnp.log2(total[:, :1])).T
                    outs[half].append(mixed[:, :128] / total)

                ahead(work, score, use)
                outs = [jnp.concatenate(out, 0) for out in outs]
                att_ref[0, rows] = jnp.where(lane_half(0), outs[0], outs[1]).astype(BF)
                return carry

            lax.fori_loop(0, count // qb, inner, 0)


def self_bwd_kernel(
    table, q_ref, k_ref, v_ref, o_ref, do_ref, lse_ref, x_ref, g1_ref, mod_ref, w_ref, *refs,
    slot, length_at, pairs, blocks, qb, score_scale, nf, ni, last,
):
    if last:
        d_early, x_early, mod_early, dx_ref, dmod_ref, keep_ref, send_ref, held, dk_acc, dv_acc, acc = refs
    else:
        text_ref, dx_ref, dmod_ref, d_out, held, dk_acc, dv_acc = refs
    step = pl.program_id(0)
    count = q_ref.shape[1]
    width = x_ref.shape[-1]
    block = x_ref.shape[1]
    used = table[length_at]
    for klen in (count // 4, count // 2, count):

        @pl.when((step < pairs) & (used == klen))
        def _(klen=klen):
            keys = k_ref[0, :klen]
            values = v_ref[0, :klen]
            dk_acc[:klen] = jnp.zeros((klen, 128), F32)
            dv_acc[:klen] = jnp.zeros((klen, 128), F32)

            def inner(position, carry):
                rows = pl.ds(pl.multiple_of(position * qb, qb), qb)
                queries = q_ref[0, rows]
                grad = do_ref[0, rows]
                dots = (grad.astype(F32) * o_ref[0, rows].astype(F32)).T
                d_queries = [[], []]
                work = [(half, at) for at in range(0, qb, BSUB) for half in (0, 1)]

                def score(half, at):
                    q_half = keep_half(queries[at : at + BSUB], half)
                    grad_half = keep_half(grad[at : at + BSUB], half)
                    return q_half, grad_half, nt(keys, q_half), nt(values, grad_half)

                def use(place, made):
                    half, at = place
                    q_half, grad_half, scores, d_prob = made
                    delta = jnp.sum(dots[64 * half : 64 * half + 64, at : at + BSUB], 0, keepdims=True)
                    cols = pl.ds(pl.multiple_of(position * qb + at, BSUB), BSUB)
                    lse = lse_ref[0, 0, half : half + 1, cols]
                    prob, d_scores = strips(partial(soft_back, lse=lse, delta=delta), scores, d_prob)
                    dv_acc[:klen] += nn(prob, grad_half)
                    dk_acc[:klen] += nn(d_scores, q_half)
                    d_queries[half].append(tn(d_scores, keys))

                ahead(work, score, use)
                d_queries = [jnp.concatenate(part, 0) for part in d_queries]
                held[step, rows] = (jnp.where(lane_half(0), d_queries[0], d_queries[1]) * score_scale).astype(BF)
                return carry

            lax.fori_loop(0, count // qb, inner, 0)
            held[pairs + step, :klen] = (dk_acc[:klen] * (1.0 / LOG2E)).astype(BF)
            held[2 * pairs + step, :klen] = dv_acc[:klen].astype(BF)
            if klen < count:
                held[pairs + step, klen:] = jnp.zeros((count - klen, 128), BF)
                held[2 * pairs + step, klen:] = jnp.zeros((count - klen, 128), BF)

    @pl.when(step == pairs)
    def _():
        dmod_ref[...] = jnp.zeros_like(dmod_ref)
        if last:
            acc[...] = jnp.zeros_like(acc)

    @pl.when((step >= pairs) & (step < pairs + blocks))
    def _():
        rows = pl.ds(pl.multiple_of((step - pairs) * block, block), block)
        d_qkv = jnp.concatenate([held[at, rows] for at in range(3 * pairs)], 1)
        shift, scale = mod_ref[0, 0:1], mod_ref[0, 1:2]
        d_hidden = nt(d_qkv, w_ref[...])
        sums = Columns(2)

        def leave(x, dh, upstream):
            normed, inverse = ln_parts(x.astype(F32))
            sums.add(0, dh)
            sums.add(1, dh * normed)
            out = upstream.astype(F32) + ln_back(normed, inverse, dh * (1.0 + scale))
            return out.astype(BF), (normed * (1.0 + scale) + shift).astype(BF)

        dx_ref[0, :block], hidden = strips(leave, x_ref[0], d_hidden, g1_ref[0])
        for at in range(2):
            dmod_ref[0, at : at + 1] += sums.total(at)
        if last:
            acc[...] += tn(hidden, d_qkv)
        else:
            d_out[...] = d_qkv
            short = text_ref.shape[2]
            for part in range(text_ref.shape[1]):
                dx_ref[0, block + part * short : block + (part + 1) * short] = text_ref[0, part]

    if last:

        @pl.when((step >= pairs + blocks) & (step < pairs + 2 * blocks))
        def _():
            shift, scale = mod_early[0, 0:1], mod_early[0, 1:2]
            hidden = strips(lambda rows: modulate(rows, shift, scale), x_early[0])
            acc[...] += tn(hidden, d_early[...])

        @pl.when(step >= pairs + 2 * blocks)
        def _():
            ra, cb = width // ni, 3 * width // nf
            for part in range(FIN):
                item = ((step - pairs - 2 * blocks) * FIN + part) ^ table[1]
                for frame in range(nf):
                    cut = acc[pl.ds(pl.multiple_of(item * ra, 16), ra), frame * cb : (frame + 1) * cb].astype(BF)
                    rest = jnp.concatenate([cut[: ra // 2, PACK:], cut[ra // 2 :, PACK:]], 1)
                    store_block(
                        jnp.concatenate([cut[:, :PACK], rest], 0), part, frame, table[0], 0, keep_ref, send_ref
                    )


def cross_kernel(
    table, att_ref, x_ref, mod_ref, text_ref, wkv_ref, wo_ref, wq_ref, wco_ref,
    kv_ref, text_rows, first_ref, second_ref, ba_ref, bb_ref, cq_ref, cr_ref, lse_ref, *, score_scale, length_at,
):
    width = x_ref.shape[-1]
    slots = kv_ref.shape[1]
    used = table[length_at + pl.program_id(0)]

    @pl.when(pl.program_id(1) == 0)
    def _():
        text_rows[0] = jnp.concatenate([text_ref[at] for at in range(text_ref.shape[0])], 0)
        kv_ref[0] = nn(text_rows[0], wkv_ref[...]).astype(BF)

    branch_a = nn(att_ref[0], wo_ref[...])
    gate_a, gate_b, shift, scale = mod_ref[0, 2:3], mod_ref[0, 5:6], mod_ref[0, 3:4], mod_ref[0, 4:5]

    def enter(rows, branch):
        first = rows.astype(F32) + gate_a * branch
        return branch.astype(BF), first, modulate(first, shift, scale)

    ba_ref[0], first, hidden = strips(enter, x_ref[0], branch_a)
    first_ref[0] = first.astype(BF)
    cq_ref[0] = (nn(hidden, wq_ref[...]) * (score_scale * LOG2E)).astype(BF)
    valid = lax.broadcasted_iota(jnp.int32, (1, slots), 1) < used
    ones = jnp.ones((slots, 128), BF)
    count = cq_ref.shape[1]
    outs = {}

    def score(pair, half, at):
        cols = slice(pair * 128, pair * 128 + 128)
        return nt(keep_half(cq_ref[0, at : at + CSUB, cols], half), kv_ref[0, :, cols])

    def use(place, scores):
        pair, half, at = place
        prob, top = strips(lambda part: soften(jnp.where(valid, part, -1e30)), scores)
        values = kv_ref[0, :, width + pair * 128 : width + pair * 128 + 128]
        mixed = nn(prob, jnp.concatenate([values, ones], 1))
        total = mixed[:, 128:]
        lse_ref[0, pair, half : half + 1, at : at + CSUB] = (top + jnp.log2(total[:, :1])).T
        outs[half] = mixed[:, :128] / total
        if half == 1:
            cr_ref[0, at : at + CSUB, pair * 128 : pair * 128 + 128] = jnp.where(
                lane_half(0), outs[0], outs[1]
            ).astype(BF)

    work = [(pair, half, at) for pair in range(H // 2) for at in range(0, count, CSUB) for half in (0, 1)]
    ahead(work, score, use)
    branch_b = nn(cr_ref[0], wco_ref[...])
    bb_ref[0], second_ref[0] = strips(
        lambda rows, branch: (branch.astype(BF), (rows + gate_b * branch).astype(BF)), first, branch_b
    )


def mlp_kernel(
    table, second_ref, cot_ref, mod_ref, wup_ref, wdn_ref,
    out_ref, g2_ref, dmod_ref, gw_ref, up_acc, dn_acc, *, blocks, total, chunk, nf, ni,
):
    step = pl.program_id(0)
    width = second_ref.shape[-1]
    ff = wup_ref.shape[-1]

    @pl.when(step == 0)
    def _():
        up_acc[...] = jnp.zeros_like(up_acc)
        dn_acc[...] = jnp.zeros_like(dn_acc)

    @pl.when(step < total)
    def _():
        shift, scale, gate = mod_ref[0, 6:7], mod_ref[0, 7:8], mod_ref[0, 8:9]
        hidden = strips(lambda rows: modulate(rows, shift, scale), second_ref[0])
        d_branch = strips(lambda rows: (rows.astype(F32) * gate).astype(BF), cot_ref[0, 0])
        branch = jnp.zeros(second_ref.shape[1:], F32)
        d_hidden = jnp.zeros(second_ref.shape[1:], F32)

        def middle(up_proj, d_act):
            below, slope = gelu_parts(up_proj)
            return (up_proj * below).astype(BF), (d_act * slope).astype(BF)

        sides = [branch, d_hidden]

        def make(at):
            cols = slice(at, at + chunk)
            return nn(hidden, wup_ref[:, cols]), nt(d_branch, wdn_ref[cols])

        def use(place, made):
            cols = slice(place[0], place[0] + chunk)
            act, d_up = strips(middle, *made)
            sides[0] += nn(act, wdn_ref[cols])
            sides[1] += nt(d_up, wup_ref[:, cols])
            dn_acc[cols] += tn(act, d_branch)
            up_acc[:, cols] += tn(hidden, d_up)

        ahead([(at,) for at in range(0, ff, chunk)], make, use)
        branch, d_hidden = sides

        @pl.when(step % blocks == 0)
        def _():
            dmod_ref[...] = jnp.zeros_like(dmod_ref)

        sums = Columns(3)

        def leave(second, cot, branch_rows, dh):
            second = second.astype(F32)
            normed, inverse = ln_parts(second)
            upstream = cot.astype(F32)
            sums.add(0, dh)
            sums.add(1, dh * normed)
            sums.add(2, upstream * branch_rows)
            upstream = upstream + ln_back(normed, inverse, dh * (1.0 + scale))
            return (second + gate * branch_rows).astype(BF), upstream.astype(BF)

        out_ref[0, 0], g2_ref[0] = strips(leave, second_ref[0], cot_ref[0, 0], branch, d_hidden)
        for at in range(3):
            dmod_ref[0, at : at + 1] += sums.total(at)

    @pl.when(step >= total)
    def _():
        ra, cb = width // ni, ff // nf
        for part in range(FIN):
            item = (step - total) * FIN + part
            for frame in range(nf):
                cut = up_acc[pl.ds(pl.multiple_of(item * ra, 16), ra), frame * cb : (frame + 1) * cb].astype(BF)
                gw_ref[part, frame, :ra] = cut[:, :PACK]
                gw_ref[part, frame, ra : 2 * ra] = cut[:, PACK:]
                gw_ref[part, frame, 2 * ra :] = pack_square(
                    dn_acc, item, ff // ni, width // nf, frame * (width // nf)
                )


def cross_back_kernel(
    table, g2_ref, bb_ref, cr_ref, cq_ref, att_ref, ba_ref, first_ref, mod_ref, kv_ref, lse_ref, text_ref,
    wo_ref, wq_ref, wco_ref, wkv_ref,
    g1_ref, datt_ref, text_out, dmod_ref, keep_ref, send_ref,
    o_acc, q_acc, co_acc, kv_acc, dtext, *, blocks, total, score_scale, nf, ni, length_at,
):
    step = pl.program_id(0)
    width = g2_ref.shape[-1]
    slots = kv_ref.shape[1]

    @pl.when(step == 0)
    def _():
        o_acc[...] = jnp.zeros_like(o_acc)
        q_acc[...] = jnp.zeros_like(q_acc)
        co_acc[...] = jnp.zeros_like(co_acc)
        kv_acc[...] = jnp.zeros_like(kv_acc)

    @pl.when(step < total)
    def _():
        @pl.when(step % blocks == 0)
        def _():
            dmod_ref[...] = jnp.zeros_like(dmod_ref)
            dtext[...] = jnp.zeros_like(dtext)

        used = table[length_at + step // blocks]
        gate_b = mod_ref[0, 5:6]
        sums = Columns(4)

        def enter(upstream, branch):
            upstream = upstream.astype(F32)
            sums.add(3, upstream * branch.astype(F32))
            return (upstream * gate_b).astype(BF)

        d_branch_b = strips(enter, g2_ref[0], bb_ref[0])
        co_acc[...] += tn(cr_ref[0], d_branch_b)
        d_crossed = nt(d_branch_b, wco_ref[...])
        slot_of = lax.broadcasted_iota(jnp.int32, (slots, 1), 0)
        parts = []
        kept = {}

        def score(pair, half):
            cols = slice(pair * 128, pair * 128 + 128)
            vcols = slice(width + pair * 128, width + pair * 128 + 128)
            grad = d_crossed[:, cols].astype(BF)
            q_half = keep_half(cq_ref[0, :, cols], half)
            grad_half = keep_half(grad, half)
            return grad, q_half, grad_half, nt(kv_ref[0, :, cols], q_half), nt(kv_ref[0, :, vcols], grad_half)

        def use(place, made):
            pair, half = place
            grad, q_half, grad_half, scores, d_prob = made
            cols = slice(pair * 128, pair * 128 + 128)
            vcols = slice(width + pair * 128, width + pair * 128 + 128)
            if half == 0:
                kept["dots"] = (grad.astype(F32) * cr_ref[0, :, cols].astype(F32)).T
            delta = jnp.sum(kept["dots"][64 * half : 64 * half + 64], 0, keepdims=True)
            lse = lse_ref[0, pair, half : half + 1]

            def back(part, d_part, at):
                return soft_back(jnp.where(at < used, part, -1e30), d_part, lse, delta)

            prob, d_scores = strips(back, scores, d_prob, slot_of)
            d_values = nn(prob, grad_half)
            d_keys = nn(d_scores, q_half)
            d_query = tn(d_scores, kv_ref[0, :, cols])
            if half == 0:
                kept["sums"] = d_keys, d_values, d_query
                return
            first_keys, first_values, first_query = kept["sums"]
            dtext[:, cols] += (first_keys + d_keys) * (1.0 / LOG2E)
            dtext[:, vcols] += first_values + d_values
            parts.append((jnp.where(lane_half(0), first_query, d_query) * score_scale).astype(BF))

        ahead([(pair, half) for pair in range(H // 2) for half in (0, 1)], score, use)
        d_cq = jnp.concatenate(parts, 1)
        shift, scale, gate = mod_ref[0, 3:4], mod_ref[0, 4:5], mod_ref[0, 2:3]
        d_hidden = nt(d_cq, wq_ref[...])

        def leave(first, dh, upstream, branch):
            normed, inverse = ln_parts(first.astype(F32))
            sums.add(1, dh)
            sums.add(2, dh * normed)
            upstream = upstream.astype(F32) + ln_back(normed, inverse, dh * (1.0 + scale))
            sums.add(0, upstream * branch.astype(F32))
            return (normed * (1.0 + scale) + shift).astype(BF), upstream.astype(BF), (upstream * gate).astype(BF)

        hidden, g1_ref[0], d_branch_a = strips(leave, first_ref[0], d_hidden, g2_ref[0], ba_ref[0])
        for at in range(4):
            dmod_ref[0, at : at + 1] += sums.total(at)
        datt_ref[0] = nt(d_branch_a, wo_ref[...]).astype(BF)
        q_acc[...] += tn(hidden, d_cq)
        o_acc[...] += tn(att_ref[0], d_branch_a)

        @pl.when(step % blocks == blocks - 1)
        def _():
            low = dtext[...].astype(BF)
            kv_acc[...] += tn(text_ref[0], low)
            made = nt(low, wkv_ref[...]).astype(BF)
            short = text_out.shape[2]
            for frame in range(nf):
                text_out[frame, 0] = made[frame * short : (frame + 1) * short]

    @pl.when(step >= total)
    def _():
        ra, cb = width // ni, width // nf
        half = ra // 2
        for part in range(FIN):
            item = ((step - total) * FIN + part) ^ table[1]
            for frame in range(nf):
                for place, acc in enumerate((o_acc, q_acc, co_acc)):
                    cut = pack_square(acc, item, ra, cb, frame * cb)
                    store_block(cut, part, frame, table[0], place * half, keep_ref, send_ref)
                cut = kv_acc[pl.ds(pl.multiple_of(item * ra, 16), ra), 2 * frame * cb : 2 * (frame + 1) * cb].astype(BF)
                store_block(cut, part, frame, table[0], 3 * half, keep_ref, send_ref)


def deal_kernel(table, *refs, at, items, group):
    out_ref = refs[-1]
    count = (len(refs) - 1) // group
    for part in range(group):
        sources = refs[part * count : (part + 1) * count]
        if count == 1:
            out_ref[part] = sources[0][0, 0].astype(out_ref.dtype)
            continue
        slot_of = table[at + items + pl.program_id(0) * group + part]
        for slot, ref in enumerate(sources):

            @pl.when(slot_of == slot)
            def _(ref=ref, part=part):
                out_ref[part] = ref[0, 0].astype(out_ref.dtype)


def land_kernel(keep, got, *refs):
    outs = refs[-2:]
    for half, out in enumerate(outs):
        out[...] = (keep[0, half].astype(F32) + got[0, half].astype(F32)).astype(BF)[None]


def finish_mlp_kernel(sum_ref, *refs):
    up, down = refs[-2:]
    ra, cb = up.shape
    up[:, : cb // 2] = sum_ref[:ra].astype(F32)
    up[:, cb // 2 :] = sum_ref[ra : 2 * ra].astype(F32)
    down[...] = untall(sum_ref[2 * ra :].astype(F32))


def finish_mid_kernel(keep, got, *refs):
    outs = refs[-4:]
    half = outs[0].shape[0] // 2
    total = keep[...].astype(F32) + got[...].astype(F32)
    for place in range(3):
        outs[place][...] = untall(total[place * half : (place + 1) * half])
    outs[3][...] = total[3 * half :]


def finish_qkv_kernel(keep, got, *refs):
    out = refs[-1]
    ra = out.shape[0]
    total = keep[...].astype(F32) + got[...].astype(F32)
    out[:, :PACK] = total[:ra]
    out[:, PACK:] = untall(total[ra:])


def untall(block):
    half = block.shape[1] // 2
    return jnp.concatenate([block[:, :half], block[:, half:]], 0)


def cost(flops, moved, exps=0):
    return pl.CostEstimate(flops=int(flops), bytes_accessed=int(moved), transcendentals=int(exps))


def params():
    return pltpu.CompilerParams(vmem_limit_bytes=LIMIT)


def whole(shape):
    return pl.BlockSpec(shape, lambda *_: (0,) * len(shape), pipeline_mode=pl.Buffered(1))


def run(kernel, name, grid, in_specs, args, out_specs, out_shape, scratch=(), deps=(), work=None, aliases=None):
    inputs = len(args)

    def body(*refs):
        kernel(*refs[:inputs], *refs[inputs + len(deps) :])

    return pl.pallas_call(
        body,
        grid_spec=pltpu.PrefetchScalarGridSpec(
            num_scalar_prefetch=1,
            grid=grid,
            in_specs=list(in_specs) + [pl.BlockSpec(memory_space=pl.ANY)] * len(deps),
            out_specs=out_specs,
            scratch_shapes=list(scratch),
        ),
        out_shape=out_shape,
        input_output_aliases=aliases or {},
        compiler_params=params(),
        cost_estimate=work,
        name=name,
    )(*args, *deps)


def any_spec(count):
    return [pl.BlockSpec(memory_space=pl.ANY)] * count


def struct(shape, dtype):
    return jax.ShapeDtypeStruct(shape, dtype)


def start_call(where, lengths, text_lengths, items, nf):
    size = 2 + 3 * (items // nf) + 3 * items
    smem = pl.BlockSpec(memory_space=pltpu.SMEM)
    return pl.pallas_call(
        partial(start_kernel, items=items, nf=nf),
        in_specs=[smem] * 3,
        out_specs=smem,
        out_shape=struct((size,), jnp.int32),
        name="start",
    )(where, lengths, text_lengths)


def gather_first_call(table, rows, nf):
    items, block, width = rows.shape
    per = items // nf
    at = 2 + 3 * per + 2 * items
    return run(
        copy_kernel,
        "gather_first",
        (nf,),
        [pl.BlockSpec((1, block, width), lambda t, s: (s[at + t * per], 0, 0))],
        (table, rows),
        pl.BlockSpec((1, block, width), lambda t, s: (t, 0, 0)),
        struct((nf, block, width), BF),
    )


def gather_call(table, rows, text, cot, nf):
    items, block, width = rows.shape
    per = items // nf
    at = 2 + 3 * per + 2 * items
    short = text.shape[1]

    def source(size, slot):
        return pl.BlockSpec((1, size, width), lambda t, s: (s[at + t * per + slot], 0, 0))

    return run(
        partial(gather_kernel, per=per),
        "gather",
        (nf,),
        [source(block, 1)] + [source(short, slot) for slot in range(per)] + [source(block, slot) for slot in range(per)],
        (table, rows) + (text,) * per + (cot,) * per,
        [
            pl.BlockSpec((1, block + per * short, width), lambda t, s: (t, 0, 0)),
            pl.BlockSpec((1, per, block, width), lambda t, s: (t, 0, 0, 0)),
        ],
        [struct((nf, block + per * short, width), BF), struct((nf, per, block, width), BF)],
    )


def gate_call(arrays, deps):
    return pl.pallas_call(
        gate_kernel,
        in_specs=any_spec(len(arrays) + len(deps)),
        out_specs=any_spec(len(arrays)),
        out_shape=[struct(array.shape, array.dtype) for array in arrays],
        input_output_aliases={at: at for at in range(len(arrays))},
        compiler_params=params(),
        name="gate",
    )(*arrays, *deps)


def halves(ni, nf, depth, total):
    spec = pl.BlockSpec((FIN, nf // 2, depth, PACK), lambda t, s: (jnp.maximum(t - total, 0), 0, 0, 0))
    return [spec] * 2, [struct((ni, nf // 2, depth, PACK), BF)] * 2


def self_fwd_call(table, slot, rows, mod, weight, kept, per, block, qb, score_scale, deps):
    blocks, _, width = rows.shape
    count = blocks * block
    pairs = H // 2

    def early(t):
        return jnp.minimum(t, blocks - 1)

    def late(t):
        return jnp.maximum(t - blocks, 0)

    return run(
        partial(self_fwd_kernel, blocks=blocks, qb=qb, score_scale=score_scale, length_at=2 + per + slot),
        "self_fwd",
        (blocks + pairs,),
        [pl.BlockSpec((1, block, width), lambda t, s: (early(t), 0, 0))]
        + [pl.BlockSpec((1, 9, width), lambda t, s: (slot, 0, 0)), whole(weight.shape)]
        + any_spec(len(kept)),
        (table, rows, mod, weight, *kept),
        [
            pl.BlockSpec((1, block, width), lambda t, s: (slot, early(t), 0)),
            pl.BlockSpec((1, block, 3 * width), lambda t, s: (slot, early(t), 0)),
            pl.BlockSpec((1, count, 128), lambda t, s: (slot, 0, late(t))),
            pl.BlockSpec((1, 1, 2, count), lambda t, s: (slot, late(t), 0, 0)),
        ],
        [
            struct((per, count, width), BF),
            struct((per, count, 3 * width), BF),
            struct((per, count, width), BF),
            struct((per, pairs, 2, count), F32),
        ],
        scratch=[pltpu.VMEM((3 * pairs, count, 128), BF)],
        deps=deps,
        work=cost(6 * count * width * width + 16 * count * count * width, count * width * 16, H * count * count),
        aliases={4 + at: at for at in range(len(kept))},
    )


def self_bwd_call(
    table, slot, qkv, att, d_att, lse, rows, g1, mod, weight, early, text, qb, score_scale, block, nf, ni, deps
):
    per, count, width = att.shape
    pairs = H // 2
    blocks = count // block
    last = early is not None
    steps = pairs + blocks
    lines = block if last else block + text.shape[1] * text.shape[2]

    def pair(t):
        return jnp.minimum(t, pairs - 1)

    def row(t):
        return jnp.clip(t - pairs, 0, blocks - 1)

    def row_early(t):
        return jnp.clip(t - pairs - blocks, 0, blocks - 1)

    column = pl.BlockSpec((1, count, 128), lambda t, s: (slot, 0, pair(t)))
    by_row = pl.BlockSpec((1, block, width), lambda t, s: (slot, row(t), 0))
    in_specs = [
        pl.BlockSpec((1, count, 128), lambda t, s, part=part: (slot, 0, part * pairs + pair(t))) for part in range(3)
    ] + [column, column, pl.BlockSpec((1, 1, 2, count), lambda t, s: (slot, pair(t), 0, 0))]
    in_specs += [by_row, by_row, pl.BlockSpec((1, 9, width), lambda t, s: (slot, 0, 0)), whole(weight.shape)]
    args = [table, qkv, qkv, qkv, att, d_att, lse, rows, g1, mod, weight]
    out_specs = [
        pl.BlockSpec((1, lines, width), lambda t, s: (row(t), 0, 0)),
        pl.BlockSpec((1, 2, width), lambda t, s: (0, 0, 0)),
    ]
    out_shape = [struct((blocks, lines, width), BF), struct((1, 2, width), F32)]
    scratch = [pltpu.VMEM((3 * pairs, count, 128), BF)] + [pltpu.VMEM((count, 128), F32)] * 2
    if last:
        in_specs += [
            pl.BlockSpec((block, 3 * width), lambda t, s: (row_early(t), 0)),
            pl.BlockSpec((1, block, width), lambda t, s: (slot - 1, row_early(t), 0)),
            pl.BlockSpec((1, 9, width), lambda t, s: (slot - 1, 0, 0)),
        ]
        args += [early, rows, mod]
        specs, shapes = halves(ni, nf, 3 * width * width // (nf * ni * PACK), steps + blocks)
        out_specs += specs
        out_shape += shapes
        scratch += [pltpu.VMEM((width, 3 * width), F32)]
        steps += blocks + ni // FIN
    else:
        in_specs += [pl.BlockSpec((1,) + text.shape[1:], lambda t, s: (row(t), 0, 0, 0))]
        args += [text]
        out_specs += [pl.BlockSpec((block, 3 * width), lambda t, s: (row(t), 0))]
        out_shape += [struct((count, 3 * width), BF)]
    return run(
        partial(
            self_bwd_kernel,
            slot=slot,
            length_at=2 + per + slot,
            pairs=pairs,
            blocks=blocks,
            qb=qb,
            score_scale=score_scale,
            nf=nf,
            ni=ni,
            last=last,
        ),
        "self_bwd",
        (steps,),
        in_specs,
        args,
        out_specs,
        out_shape,
        scratch=scratch,
        deps=deps,
        work=cost(40 * count * count * width + 12 * count * width * width, count * width * 30, H * count * count),
    )


def cross_call(table, att, rows, mod, text, short, wkv, wo, wq, wco, score_scale, block, deps):
    items, count, width = rows.shape
    nf, lines, _ = text.shape
    skip = lines // short - items
    slots = nf * short
    row = pl.BlockSpec((1, block, width), lambda i, j, s: (i, j, 0))
    return run(
        partial(cross_kernel, score_scale=score_scale, length_at=2 + 2 * items),
        "cross_fwd",
        (items, count // block),
        [
            row,
            row,
            pl.BlockSpec((1, 9, width), lambda i, j, s: (i, 0, 0)),
            pl.BlockSpec((nf, short, width), lambda i, j, s: (0, skip + i, 0)),
            whole(wkv.shape),
            whole(wo.shape),
            whole(wq.shape),
            whole(wco.shape),
        ],
        (table, att, rows, mod, text, wkv, wo, wq, wco),
        [pl.BlockSpec((1, slots, 2 * width), lambda i, j, s: (i, 0, 0))]
        + [pl.BlockSpec((1, slots, width), lambda i, j, s: (i, 0, 0))]
        + [row] * 6
        + [pl.BlockSpec((1, H // 2, 2, block), lambda i, j, s: (i, 0, 0, j))],
        [struct((items, slots, 2 * width), BF), struct((items, slots, width), BF)]
        + [struct(rows.shape, BF)] * 6
        + [struct((items, H // 2, 2, count), F32)],
        deps=deps,
        work=cost(
            items * count * (6 * width * width + 16 * slots * width), items * count * width * 20, items * H * count * slots
        ),
    )


def back_grid(items, count, block):
    blocks = count // block
    total = items * blocks

    def at(t):
        return jnp.minimum(t, total - 1)

    def by_item(t, s):
        return (at(t) // blocks, 0, 0)

    def by_row(t, s):
        return (at(t) // blocks, at(t) % blocks, 0)

    return blocks, total, by_item, by_row


def mlp_call(table, second, cot, mod, wup, wdn, block, chunk, nf, ni, deps):
    items, count, width = second.shape
    ff = wup.shape[1]
    blocks, total, by_item, by_row = back_grid(items, count, block)
    row = pl.BlockSpec((1, block, width), by_row)
    shard = pl.BlockSpec((1, 1, block, width), lambda t, s: (by_row(t, s)[1], by_row(t, s)[0], 0, 0))
    depth = 2 * width * ff // (nf * ni * PACK)
    return run(
        partial(mlp_kernel, blocks=blocks, total=total, chunk=chunk, nf=nf, ni=ni),
        "mlp",
        (total + ni // FIN,),
        [row, shard, pl.BlockSpec((1, 9, width), by_item), whole(wup.shape), whole(wdn.shape)],
        (table, second, cot, mod, wup, wdn),
        [shard, row, pl.BlockSpec((1, 3, width), by_item)]
        + [pl.BlockSpec((FIN, nf, depth, PACK), lambda t, s: (jnp.maximum(t - total, 0), 0, 0, 0))],
        [struct(cot.shape, BF), struct(second.shape, BF), struct((items, 3, width), F32)]
        + [struct((ni, nf, depth, PACK), BF)],
        scratch=[pltpu.VMEM((width, ff), F32), pltpu.VMEM((ff, width), F32)],
        deps=deps,
        work=cost(12 * items * count * width * ff, items * count * width * 16, items * count * ff * 2),
    )


def cross_back_call(
    table, g2, bb, cr, cq, att, ba, first, mod, kv, lse, text, wo, wq, wco, wkv, score_scale, block, nf, ni, deps
):
    items, count, width = g2.shape
    slots = kv.shape[1]
    short = slots // nf
    blocks, total, by_item, by_row = back_grid(items, count, block)
    row = pl.BlockSpec((1, block, width), by_row)
    by_slot = pl.BlockSpec((nf, 1, short, width), lambda t, s: (0, by_item(t, s)[0], 0, 0))
    specs, shapes = halves(ni, nf, 5 * width * width // (nf * ni * PACK), total)
    lse_spec = pl.BlockSpec((1, H // 2, 2, block), lambda t, s: (by_row(t, s)[0], 0, 0, by_row(t, s)[1]))
    return run(
        partial(
            cross_back_kernel,
            blocks=blocks,
            total=total,
            score_scale=score_scale,
            nf=nf,
            ni=ni,
            length_at=2 + 2 * items,
        ),
        "cross_bwd",
        (total + ni // FIN,),
        [row] * 7
        + [pl.BlockSpec((1, 9, width), by_item), pl.BlockSpec((1, slots, 2 * width), by_item), lse_spec]
        + [pl.BlockSpec((1, slots, width), by_item)]
        + [whole(weight.shape) for weight in (wo, wq, wco, wkv)],
        (table, g2, bb, cr, cq, att, ba, first, mod, kv, lse, text, wo, wq, wco, wkv),
        [row, row, by_slot, pl.BlockSpec((1, 4, width), by_item)] + specs,
        [struct(g2.shape, BF)] * 2 + [struct((nf, items, short, width), BF), struct((items, 4, width), F32)] + shapes,
        scratch=[pltpu.VMEM((width, width), F32)] * 3
        + [pltpu.VMEM((width, 2 * width), F32), pltpu.VMEM((slots, 2 * width), F32)],
        deps=deps,
        work=cost(
            items * count * (12 * width * width + 40 * slots * width), items * count * width * 24, items * H * count * slots
        ),
    )


def deal_call(table, jobs, per, name, deps=(), group=2):
    nf, _, _, width = jobs[0][0][0].shape
    items = nf * per
    at = 2 + 3 * per
    specs, args, counts = [], [], []
    for got, block, skip, _ in jobs:
        counts.append(len(got) * group)
        args += list(got) * group
        for part in range(group):
            if len(got) == 1:
                specs.append(
                    pl.BlockSpec(
                        (1, 1, block, width),
                        lambda t, s, part=part, skip=skip: (
                            s[at + t * group + part], 0, skip + s[at + items + t * group + part], 0
                        ),
                    )
                )
            else:
                specs += [
                    pl.BlockSpec((1, 1, block, width), lambda t, s, part=part: (s[at + t * group + part], 0, 0, 0))
                ] * len(got)

    def body(table, *refs):
        outs = refs[sum(counts) :]
        first = 0
        for count, out in zip(counts, outs):
            deal_kernel(table, *refs[first : first + count], out, at=at, items=items, group=group)
            first += count

    return run(
        body,
        name,
        (items // group,),
        specs,
        (table, *args),
        [pl.BlockSpec((group, job[1], width), lambda t, s: (t, 0, 0)) for job in jobs],
        [struct((items, job[1], width), job[3]) for job in jobs],
        deps=deps,
        work=cost(0, items * jobs[0][1] * width * 6),
    )


def small_call(kernel, name, args, out_shape, deps=()):
    return pl.pallas_call(
        kernel,
        in_specs=[pl.BlockSpec(arg.shape, lambda: (0,) * arg.ndim) for arg in args] + any_spec(len(deps)),
        out_specs=[pl.BlockSpec(out.shape, lambda: (0,) * len(out.shape)) for out in out_shape],
        out_shape=out_shape,
        compiler_params=params(),
        name=name,
    )(*args, *deps)


def exchange(blocks):
    return lax.all_to_all(blocks, "frames", 0, 0, tiled=True)


def swap(block, offset, nf):
    if offset == 0:
        return block
    return lax.ppermute(block, "frames", [(i, i ^ offset) for i in range(nf)])


def bits_of(count):
    return count.bit_length() - 1


class Sum:
    def __init__(self, keep, send, order, sizes):
        self.sizes = sizes
        ni, nf = sizes["items"], sizes["frames"]
        self.dims = [("items", bit) for bit in reversed(range(bits_of(ni)))]
        self.dims += [("frames", bit) for bit in reversed(range(1, bits_of(nf)))]
        shape = (2,) * len(self.dims) + keep.shape[2:]
        self.keep, self.send = keep.reshape(shape), send
        self.shape = shape
        self.steps = [("frames", 0)] + list(order)
        self.got = None

    def launch(self):
        name, bit = self.steps.pop(0)
        self.got = lax.ppermute(self.send, name, [(i, i ^ (1 << bit)) for i in range(self.sizes[name])])

    def land(self, deps=()):
        got = self.got.reshape(self.keep.shape)
        if not self.steps:
            return self.keep, got
        dim = self.dims.index(self.steps[0])
        self.dims.remove(self.steps[0])
        shape = self.keep.shape
        outer, inner = 2**dim, 2 ** (len(shape) - 3 - dim)
        view = (outer, 2, inner) + shape[-2:]
        out = struct((outer, inner) + shape[-2:], BF)
        source = pl.BlockSpec((1,) + view[1:], lambda t: (t, 0, 0, 0, 0))
        target = pl.BlockSpec((1,) + out.shape[1:], lambda t: (t, 0, 0, 0))
        self.keep, self.send = pl.pallas_call(
            land_kernel,
            grid=(outer,),
            in_specs=[source] * 2 + any_spec(len(deps)),
            out_specs=[target] * 2,
            out_shape=[out] * 2,
            compiler_params=params(),
            name="land",
        )(self.keep.reshape(view), got.reshape(view), *deps)
        left = shape[:dim] + shape[dim + 1 :]
        self.keep = self.keep.reshape(left)
        return None


def collect_items(rows, ni):
    for bit in range(bits_of(ni)):
        rows = jnp.concatenate([rows, lax.ppermute(rows, "items", [(i, i ^ (1 << bit)) for i in range(ni)])], 0)
    return rows


def items_whole(
    ni, nf, frames_in, cond, text, item_lengths, text_lengths, ada_weight, qkv_weight, out_weight,
    cross_q_weight, cross_kv_weight, cross_out_weight, up_weight, down_weight, cotangent,
):
    items, block, width = frames_in.shape
    per = items // nf
    ff = up_weight.shape[1]
    sizes = {"items": ni, "frames": nf}
    score_scale = (width // H) ** (-0.5)
    me = lax.axis_index("frames")
    row_item = lax.axis_index("items")
    x_first = [("items", bit) for bit in range(bits_of(ni))] + [("frames", bit) for bit in range(1, bits_of(nf))]

    table = start_call(jnp.stack([me, row_item]), item_lengths, text_lengths, items, nf)
    rows_first = exchange(gather_first_call(table, frames_in, nf))
    mixed_send, cot_send = gather_call(table, frames_in, text, cotangent, nf)

    cond_f = cond.astype(F32)
    low_cond = jax.nn.silu(cond_f).astype(BF)
    modulation = nn(low_cond, ada_weight)
    pick = table[2 : 2 + per, None] == jnp.arange(items, dtype=jnp.int32)[None, :]
    mod = jnp.sum(jnp.where(pick[:, :, None], modulation[None], 0.0), 1).reshape(per, 9, width)

    (mixed_send,) = gate_call([mixed_send], [rows_first, mod])
    mixed = exchange(mixed_send)
    kept = self_fwd_call(table, 0, rows_first, mod, qkv_weight, (), per, block, 512, score_scale, [mixed_send])
    (cot_send,) = gate_call([cot_send], [mixed])
    cot = exchange(cot_send)
    kept = self_fwd_call(table, 1, mixed, mod, qkv_weight, kept, per, block, 512, score_scale, [cot_send])
    rows, qkv, attended, self_lse = kept
    text_kv, text_rows, first, second, branch_a, branch_b, cross_q, crossed, cross_lse = cross_call(
        table, attended, rows, mod, mixed, text.shape[1], cross_kv_weight, out_weight, cross_q_weight, cross_out_weight,
        score_scale, 2 * block, [],
    )
    layer_send, g2, dmod_c, g_mlp = mlp_call(
        table, second, cot, mod, up_weight, down_weight, block, 768, nf, ni, []
    )
    layer_got = exchange(layer_send)
    sum_mlp = lax.psum_scatter(
        g_mlp.reshape((ni * nf,) + g_mlp.shape[2:]), ("items", "frames"), scatter_dimension=0, tiled=True
    )[0]
    g1, d_att, text_back, dmod_b, mid_keep, mid_send = cross_back_call(
        table, g2, branch_b, crossed, cross_q, attended, branch_a, first, mod, text_kv, cross_lse, text_rows,
        out_weight, cross_q_weight, cross_out_weight, cross_kv_weight, score_scale, 2 * block, nf, ni, [],
    )
    mid = Sum(mid_keep, mid_send, x_first, sizes)
    mid.launch()
    made_0, dmod_0, early = self_bwd_call(
        table, 0, qkv, attended, d_att, self_lse, rows, g1, mod, qkv_weight, None, text_back, 1024, score_scale, block, nf, ni,
        [layer_got],
    )
    mid.land()
    mid.launch()
    got_0 = exchange(made_0)
    made_1, dmod_1, grad_keep, grad_send = self_bwd_call(
        table, 1, qkv, attended, d_att, self_lse, rows, g1, mod, qkv_weight, early, None, 1024, score_scale, block, nf, ni,
        [mid.send],
    )
    made_1, grad_send = gate_call([made_1, grad_send], [mid.got, got_0, sum_mlp])
    grad = Sum(grad_keep, grad_send, x_first, sizes)
    grad.launch()
    d_mod = jnp.concatenate([jnp.concatenate([dmod_0, dmod_1], 0), dmod_b, dmod_c], 1).reshape(per, 9 * width)
    ada_rows, ada_cols, cond_cols = width // ni, 9 * width // nf, width // nf
    high = d_mod.astype(BF)
    rest = (d_mod - high.astype(F32)).astype(BF)
    parts = nt(jnp.concatenate([high, rest], 0), ada_weight)
    parts = jnp.concatenate(
        [d_mod.reshape(per, nf, ada_cols), (parts[:per] + parts[per:]).reshape(per, nf, cond_cols)], 2
    ).transpose(1, 0, 2)
    parts = exchange(parts)
    (made_1,) = gate_call([made_1], [parts])
    got_1 = exchange(made_1)
    grad.land([parts])
    grad.launch()
    mid.land([grad.send])
    mid.launch()
    layer_out, text_grad = deal_call(
        table,
        [
            ([layer_got.reshape(nf, 1, per * block, width)], block, 0, BF),
            ([got_0[:, None]], text.shape[1], block // text.shape[1], F32),
        ],
        per,
        "deal_out",
        [grad.send, mid.send],
    )
    mid.land([layer_out])
    mid.launch()
    grad.land([mid.send])
    grad.launch()
    (input_grad,) = deal_call(
        table, [([got_0[:, None], got_1[:, None]], block, 0, F32)], per, "deal_in", [grad.send, mid.send]
    )
    mid.land([input_grad])
    mid.launch()
    grad.land([mid.send])
    grad.launch()
    (parts,) = gate_call([parts], [grad.send])
    parts = parts.reshape(items, ada_cols + cond_cols)
    at = 2 + 3 * per
    spot = table[at : at + items] * per + table[at + items : at + 2 * items]
    pick_row = spot[:, None] == jnp.arange(items, dtype=jnp.int32)[None, :]
    parts = jnp.sum(jnp.where(pick_row[:, :, None], parts[None], 0.0), 1)
    every = collect_items(jnp.concatenate([parts[:, :ada_cols], low_cond.astype(F32)], 1), ni)
    grad_ada = lax.dot_general(
        lax.dynamic_slice(every, (0, ada_cols + row_item * ada_rows), (items * ni, ada_rows), allow_negative_indices=False),
        every[:, :ada_cols],
        (((0,), (0,)), ((), ())),
        precision=lax.Precision.HIGHEST,
        preferred_element_type=F32,
    )
    cond_mine = lax.dynamic_slice(cond_f, (0, me * cond_cols), (items, cond_cols), allow_negative_indices=False)
    sigmoid_c = jax.nn.sigmoid(cond_mine)
    cond_grad = parts[:, ada_cols:] * (sigmoid_c * (1.0 + cond_mine * (1.0 - sigmoid_c)))

    grad_up, grad_down = small_call(
        finish_mlp_kernel,
        "finish_mlp",
        [sum_mlp],
        [struct((width // ni, ff // nf), F32), struct((ff // ni, width // nf), F32)],
        [grad.send],
    )
    while grad.steps:
        grad.land()
        grad.launch()
    mid_sum = mid.land()
    square = struct((ada_rows, cond_cols), F32)
    grad_out, grad_cross_q, grad_cross_out, grad_cross_kv = small_call(
        finish_mid_kernel, "finish_mid", mid_sum, [square] * 3 + [struct((ada_rows, 2 * cond_cols), F32)]
    )
    (grad_qkv,) = small_call(finish_qkv_kernel, "finish_qkv", grad.land(), [struct((ada_rows, 3 * cond_cols), F32)])
    return (
        layer_out,
        input_grad,
        text_grad,
        cond_grad,
        grad_ada,
        grad_qkv,
        grad_out,
        grad_cross_q,
        grad_cross_kv,
        grad_cross_out,
        grad_up,
        grad_down,
    )


def on_device(mesh, *args):
    ni, nf = mesh.shape["items"], mesh.shape["frames"]
    if nf == 4 and args[0].shape[0] == 2 * nf and args[0].shape[-1] == 768 and 768 % (32 * ni) == 0:
        return items_whole(ni, nf, *args)
    return frames_split(*args)


def solution(mesh):
    in_specs = (
        P("items", "frames", None),
        P("items", None),
        P("items", "frames", None),
        P("items"),
        P("items"),
        P(),
        P(),
        P(),
        P(),
        P(),
        P(),
        P(),
        P(),
        P("items", "frames", None),
    )
    out_specs = (
        P("items", "frames", None),
        P("items", "frames", None),
        P("items", "frames", None),
        P("items", "frames"),
        P("items", "frames"),
        P("items", "frames"),
        P("items", "frames"),
        P("items", "frames"),
        P("items", "frames"),
        P("items", "frames"),
        P("items", "frames"),
        P("items", "frames"),
    )
    return jax.shard_map(
        partial(on_device, mesh), mesh=mesh, in_specs=in_specs, out_specs=out_specs, check_vma=False
    )
```

```python
import functools
from functools import partial

import jax
import jax.numpy as jnp
from jax import lax
from jax.experimental import pallas as pl
from jax.experimental.pallas import tpu as pltpu
from jax.sharding import PartitionSpec as P

H = 12


def norm_parts(tensor):
    centered = tensor - jnp.mean(tensor, -1, keepdims=True)
    inverse = lax.rsqrt(jnp.mean(centered * centered, -1, keepdims=True) + 1e-06)
    return (centered * inverse, inverse)


def norm_back(normed, inverse, incoming):
    return inverse * (
        incoming
        - jnp.mean(incoming, -1, keepdims=True)
        - normed * jnp.mean(incoming * normed, -1, keepdims=True)
    )


def split_heads(tensor):
    return tensor.reshape(tensor.shape[0], tensor.shape[1], H, -1)


def attend(queries, keys_in, values_in, key_valid, score_scale):
    scores = (
        jnp.einsum(
            "ifhd,ijhd->ihfj",
            split_heads(queries),
            split_heads(keys_in),
            preferred_element_type=jnp.float32,
        )
        * score_scale
    )
    scores = jnp.where(key_valid[:, None, None, :], scores, -1e30)
    attn_prob = jax.nn.softmax(scores, axis=-1)
    log_total = jax.nn.logsumexp(scores, axis=-1)
    low_prob = attn_prob.astype(jnp.bfloat16)
    mixed = jnp.einsum(
        "ihfj,ijhd->ifhd", low_prob, split_heads(values_in), preferred_element_type=jnp.float32
    )
    return (attn_prob, low_prob, mixed.astype(jnp.bfloat16).reshape(queries.shape), log_total)


def attend_back(grad_mixed, queries, keys_in, values_in, attn_prob, low_prob, score_scale):
    grad_heads = split_heads(grad_mixed)
    grad_prob = jnp.einsum(
        "ifhd,ijhd->ihfj", grad_heads, split_heads(values_in), preferred_element_type=jnp.float32
    )
    grad_values = jnp.einsum(
        "ihfj,ifhd->ijhd", low_prob, grad_heads, preferred_element_type=jnp.float32
    )
    grad_scores = (
        attn_prob * (grad_prob - jnp.sum(attn_prob * grad_prob, -1, keepdims=True))
    ).astype(jnp.bfloat16)
    grad_queries = (
        jnp.einsum(
            "ihfj,ijhd->ifhd", grad_scores, split_heads(keys_in), preferred_element_type=jnp.float32
        )
        * score_scale
    )
    grad_keys = (
        jnp.einsum(
            "ihfj,ifhd->ijhd", grad_scores, split_heads(queries), preferred_element_type=jnp.float32
        )
        * score_scale
    )
    return (
        grad_queries.reshape(queries.shape),
        grad_keys.reshape(keys_in.shape),
        grad_values.reshape(values_in.shape),
    )


def project(tensor, weight):
    return jnp.einsum("ifd,de->ife", tensor, weight, preferred_element_type=jnp.float32)


def project_back(tensor, weight):
    return jnp.einsum("ife,de->ifd", tensor, weight, preferred_element_type=jnp.float32)


def weight_grad(left, right):
    return jnp.einsum("ifd,ife->de", left, right, preferred_element_type=jnp.float32)


def frames_split(
    frames_in,
    cond,
    text,
    item_lengths,
    text_lengths,
    ada_weight,
    qkv_weight,
    out_weight,
    cross_q_weight,
    cross_kv_weight,
    cross_out_weight,
    up_weight,
    down_weight,
    cotangent,
):
    model_width = frames_in.shape[-1]
    score_scale = (model_width // H) ** (-0.5)
    cond_f = cond.astype(jnp.float32)
    low_cond = jax.nn.silu(cond_f).astype(jnp.bfloat16)
    modulation = jnp.dot(low_cond, ada_weight, preferred_element_type=jnp.float32)
    pieces = [
        modulation[:, None, position * model_width : (position + 1) * model_width]
        for position in range(9)
    ]
    shift_a, scale_a, gate_a, shift_b, scale_b, gate_b, shift_c, scale_c, gate_c = pieces
    residual_in = frames_in.astype(jnp.float32)
    normed_a, inverse_a = norm_parts(residual_in)
    hidden_a = (normed_a * (1.0 + scale_a) + shift_a).astype(jnp.bfloat16)
    qkv = project(hidden_a, qkv_weight).astype(jnp.bfloat16)
    queries = qkv[..., :model_width]
    keys_own = qkv[..., model_width : 2 * model_width]
    values_own = qkv[..., 2 * model_width :]
    keys_all, values_all = (
        lax.all_gather(keys_own, "frames", axis=1, tiled=True),
        lax.all_gather(values_own, "frames", axis=1, tiled=True),
    )
    key_valid = jnp.arange(keys_all.shape[1], dtype=jnp.int32)[None, :] < item_lengths[:, None]
    attn_prob, low_prob, attended, self_total = attend(
        queries, keys_all, values_all, key_valid, score_scale
    )
    branch_a = project(attended, out_weight)
    first = residual_in + gate_a * branch_a
    normed_b, inverse_b = norm_parts(first)
    hidden_b = (normed_b * (1.0 + scale_b) + shift_b).astype(jnp.bfloat16)
    cross_q = project(hidden_b, cross_q_weight).astype(jnp.bfloat16)
    text_own = project(text, cross_kv_weight).astype(jnp.bfloat16)
    text_kv = lax.all_gather(text_own, "frames", axis=1, tiled=True)
    text_keys = text_kv[..., :model_width]
    text_values = text_kv[..., model_width:]
    text_valid = jnp.arange(text_kv.shape[1], dtype=jnp.int32)[None, :] < text_lengths[:, None]
    cross_prob, cross_low, crossed, cross_total = attend(
        cross_q, text_keys, text_values, text_valid, score_scale
    )
    branch_b = project(crossed, cross_out_weight)
    second = first + gate_b * branch_b
    normed_c, inverse_c = norm_parts(second)
    hidden_c = (normed_c * (1.0 + scale_c) + shift_c).astype(jnp.bfloat16)
    up_proj = project(hidden_c, up_weight)
    activated, gelu_back = jax.vjp(partial(jax.nn.gelu, approximate=False), up_proj)
    low_act = activated.astype(jnp.bfloat16)
    branch_c = project(low_act, down_weight)
    layer_out = (second + gate_c * branch_c).astype(jnp.bfloat16)
    upstream = cotangent.astype(jnp.float32)
    d_gate_c = jnp.sum(upstream * branch_c, 1)
    d_branch_c = (upstream * gate_c).astype(jnp.bfloat16)
    grad_down = weight_grad(low_act, d_branch_c)
    d_up = gelu_back(project_back(d_branch_c, down_weight))[0].astype(jnp.bfloat16)
    grad_up = weight_grad(hidden_c, d_up)
    d_hidden_c = project_back(d_up, up_weight)
    d_shift_c = jnp.sum(d_hidden_c, 1)
    d_scale_c = jnp.sum(d_hidden_c * normed_c, 1)
    upstream = upstream + norm_back(normed_c, inverse_c, d_hidden_c * (1.0 + scale_c))
    d_gate_b = jnp.sum(upstream * branch_b, 1)
    d_branch_b = (upstream * gate_b).astype(jnp.bfloat16)
    grad_cross_out = weight_grad(crossed, d_branch_b)
    d_crossed = project_back(d_branch_b, cross_out_weight).astype(jnp.bfloat16)
    d_cross_q, d_text_keys, d_text_values = attend_back(
        d_crossed, cross_q, text_keys, text_values, cross_prob, cross_low, score_scale
    )
    d_cross_q = d_cross_q.astype(jnp.bfloat16)
    grad_cross_q = weight_grad(hidden_b, d_cross_q)
    d_hidden_b = project_back(d_cross_q, cross_q_weight)
    d_text_local = jnp.concatenate([d_text_keys, d_text_values], -1)
    d_shift_b = jnp.sum(d_hidden_b, 1)
    d_scale_b = jnp.sum(d_hidden_b * normed_b, 1)
    upstream = upstream + norm_back(normed_b, inverse_b, d_hidden_b * (1.0 + scale_b))
    d_gate_a = jnp.sum(upstream * branch_a, 1)
    d_branch_a = (upstream * gate_a).astype(jnp.bfloat16)
    grad_out = weight_grad(attended, d_branch_a)
    d_attended = project_back(d_branch_a, out_weight).astype(jnp.bfloat16)
    keys_back, values_back = (
        lax.all_gather(keys_own, "frames", axis=1, tiled=True),
        lax.all_gather(values_own, "frames", axis=1, tiled=True),
    )
    d_queries, d_keys_all, d_values_all = attend_back(
        d_attended, queries, keys_back, values_back, attn_prob, low_prob, score_scale
    )
    d_keys, d_values = (
        lax.psum_scatter(
            d_keys_all.astype(jnp.bfloat16), "frames", scatter_dimension=1, tiled=True
        ).astype(jnp.float32),
        lax.psum_scatter(
            d_values_all.astype(jnp.bfloat16), "frames", scatter_dimension=1, tiled=True
        ).astype(jnp.float32),
    )
    d_qkv = jnp.concatenate(
        [
            d_queries.astype(jnp.bfloat16),
            d_keys.astype(jnp.bfloat16),
            d_values.astype(jnp.bfloat16),
        ],
        -1,
    )
    grad_qkv = weight_grad(hidden_a, d_qkv)
    d_hidden_a = project_back(d_qkv, qkv_weight)
    d_shift_a = jnp.sum(d_hidden_a, 1)
    d_scale_a = jnp.sum(d_hidden_a * normed_a, 1)
    input_grad = upstream + norm_back(normed_a, inverse_a, d_hidden_a * (1.0 + scale_a))
    d_modulation = jnp.concatenate(
        [
            d_shift_a,
            d_scale_a,
            d_gate_a,
            d_shift_b,
            d_scale_b,
            d_gate_b,
            d_shift_c,
            d_scale_c,
            d_gate_c,
        ],
        -1,
    )
    grad_ada = jnp.dot(
        low_cond.astype(jnp.float32).T,
        d_modulation,
        precision=lax.Precision.HIGHEST,
        preferred_element_type=jnp.float32,
    )
    sigmoid_c = jax.nn.sigmoid(cond_f)
    cond_part = jnp.dot(
        d_modulation,
        ada_weight.T,
        precision=lax.Precision.HIGHEST,
        preferred_element_type=jnp.float32,
    ) * (sigmoid_c * (1.0 + cond_f * (1.0 - sigmoid_c)))
    d_text_kv, cond_grad = (
        lax.psum_scatter(d_text_local, "frames", scatter_dimension=1, tiled=True),
        lax.psum_scatter(cond_part, "frames", scatter_dimension=1, tiled=True),
    )
    low_text_kv = d_text_kv.astype(jnp.bfloat16)
    grad_cross_kv = weight_grad(text, low_text_kv)
    text_grad = project_back(low_text_kv, cross_kv_weight)
    grads = (
        grad_ada,
        grad_qkv,
        grad_out,
        grad_cross_q,
        grad_cross_kv,
        grad_cross_out,
        grad_up,
        grad_down,
    )
    partial_sums = (
        lax.psum_scatter(
            grads[0].astype(jnp.bfloat16), "frames", scatter_dimension=1, tiled=True
        ).astype(jnp.float32),
        lax.psum_scatter(
            grads[1].astype(jnp.bfloat16), "frames", scatter_dimension=1, tiled=True
        ).astype(jnp.float32),
        lax.psum_scatter(
            grads[2].astype(jnp.bfloat16), "frames", scatter_dimension=1, tiled=True
        ).astype(jnp.float32),
        lax.psum_scatter(
            grads[3].astype(jnp.bfloat16), "frames", scatter_dimension=1, tiled=True
        ).astype(jnp.float32),
        lax.psum_scatter(
            grads[4].astype(jnp.bfloat16), "frames", scatter_dimension=1, tiled=True
        ).astype(jnp.float32),
        lax.psum_scatter(
            grads[5].astype(jnp.bfloat16), "frames", scatter_dimension=1, tiled=True
        ).astype(jnp.float32),
        lax.psum_scatter(
            grads[6].astype(jnp.bfloat16), "frames", scatter_dimension=1, tiled=True
        ).astype(jnp.float32),
        lax.psum_scatter(
            grads[7].astype(jnp.bfloat16), "frames", scatter_dimension=1, tiled=True
        ).astype(jnp.float32),
    )
    totals = (
        lax.psum_scatter(
            partial_sums[0].astype(jnp.bfloat16), "items", scatter_dimension=0, tiled=True
        ).astype(jnp.float32),
        lax.psum_scatter(
            partial_sums[1].astype(jnp.bfloat16), "items", scatter_dimension=0, tiled=True
        ).astype(jnp.float32),
        lax.psum_scatter(
            partial_sums[2].astype(jnp.bfloat16), "items", scatter_dimension=0, tiled=True
        ).astype(jnp.float32),
        lax.psum_scatter(
            partial_sums[3].astype(jnp.bfloat16), "items", scatter_dimension=0, tiled=True
        ).astype(jnp.float32),
        lax.psum_scatter(
            partial_sums[4].astype(jnp.bfloat16), "items", scatter_dimension=0, tiled=True
        ).astype(jnp.float32),
        lax.psum_scatter(
            partial_sums[5].astype(jnp.bfloat16), "items", scatter_dimension=0, tiled=True
        ).astype(jnp.float32),
        lax.psum_scatter(
            partial_sums[6].astype(jnp.bfloat16), "items", scatter_dimension=0, tiled=True
        ).astype(jnp.float32),
        lax.psum_scatter(
            partial_sums[7].astype(jnp.bfloat16), "items", scatter_dimension=0, tiled=True
        ).astype(jnp.float32),
    )
    return (
        layer_out,
        input_grad,
        text_grad,
        cond_grad,
        totals[0],
        totals[1],
        totals[2],
        totals[3],
        totals[4],
        totals[5],
        totals[6],
        totals[7],
    )


LOG2E = 1.4426950408889634
BF = jnp.bfloat16
F32 = jnp.float32
PACK = 384
FIN = 2
SUB = 128
BSUB = 256
CSUB = 256
LIMIT = 127 * 2**19


def nn(left, right):
    return jnp.dot(left, right, preferred_element_type=F32)


def nt(left, right):
    return lax.dot_general(left, right, (((1,), (1,)), ((), ())), preferred_element_type=F32)


def tn(left, right):
    return lax.dot_general(left, right, (((0,), (0,)), ((), ())), preferred_element_type=F32)


def ln_parts(rows):
    share = 1.0 / rows.shape[-1]
    centered = rows - jnp.sum(rows, -1, keepdims=True) * share
    inverse = lax.rsqrt(jnp.sum(centered * centered, -1, keepdims=True) * share + 1e-06)
    return centered * inverse, inverse


def ln_back(normed, inverse, incoming):
    share = 1.0 / normed.shape[-1]
    mean_in = jnp.sum(incoming, -1, keepdims=True) * share
    mean_dot = jnp.sum(incoming * normed, -1, keepdims=True) * share
    return inverse * (incoming - mean_in - normed * mean_dot)


def gelu_parts(value):
    size = jnp.abs(value)
    inner = 1.0 / (1.0 + (0.3275911 * 0.7071067811865476) * size)
    series = inner * (
        0.5 * 0.254829592
        + inner
        * (
            0.5 * -0.284496736
            + inner * (0.5 * 1.421413741 + inner * (0.5 * -1.453152027 + inner * (0.5 * 1.061405429)))
        )
    )
    bell = jnp.exp2(value * value * (-0.5 * LOG2E))
    tail = series * bell
    below = jnp.where(value >= 0.0, 1.0 - tail, tail)
    return below, below + value * bell * 0.3989422804014327


def strips(body, *arrays, rows=16):
    made = [body(*(array[at : at + rows] for array in arrays)) for at in range(0, arrays[0].shape[0], rows)]
    if not isinstance(made[0], tuple):
        return jnp.concatenate(made, 0)
    return tuple(jnp.concatenate(column, 0) for column in zip(*made))


def fold(rows):
    return jnp.sum(rows.reshape(rows.shape[0] // 8, 8, rows.shape[1]), 0)


def modulate(rows, shift, scale):
    normed, _ = ln_parts(rows.astype(F32))
    return (normed * (1.0 + scale) + shift).astype(BF)


class Columns:
    def __init__(self, count):
        self.parts = [None] * count

    def add(self, at, rows):
        made = fold(rows)
        self.parts[at] = made if self.parts[at] is None else self.parts[at] + made

    def total(self, at):
        return jnp.sum(self.parts[at], 0, keepdims=True)


def lane_half(half):
    lane = lax.broadcasted_iota(jnp.int32, (1, 128), 1)
    return lane < 64 if half == 0 else lane >= 64


def keep_half(rows, half):
    return jnp.where(lane_half(half), rows, jnp.zeros_like(rows))


def pack_square(acc, item, ra, cb, col):
    first = acc[pl.ds(pl.multiple_of(item * ra, 16), ra // 2), col : col + cb]
    second = acc[pl.ds(pl.multiple_of(item * ra + ra // 2, 16), ra // 2), col : col + cb]
    return jnp.concatenate([first, second], 1).astype(BF)


def store_block(value, part, frame, me, row, keep_ref, send_ref):
    place = frame ^ me

    @pl.when(place & 1 == 0)
    def _():
        keep_ref[part, place >> 1, row : row + value.shape[0]] = value

    @pl.when(place & 1 == 1)
    def _():
        send_ref[part, place >> 1, row : row + value.shape[0]] = value


def start_kernel(where, lengths, text_lengths, table, *, items, nf):
    per = items // nf
    me = where[0]
    table[0] = me
    table[1] = where[1]
    at = 2 + 3 * per
    for i in range(items):
        rank = jnp.int32(0)
        for j in range(items):
            if j < i:
                ahead = lengths[j] >= lengths[i]
            elif j > i:
                ahead = lengths[j] > lengths[i]
            else:
                continue
            rank = rank + ahead.astype(jnp.int32)
        turn, seat = rank // nf, rank % nf
        device = jnp.where(turn % 2 == 0, seat, nf - 1 - seat)
        table[at + i] = device
        table[at + items + i] = turn
        table[at + 2 * items + device * per + turn] = i
    for slot in range(per):
        item = table[at + 2 * items + me * per + slot]
        table[2 + slot] = item
        table[2 + per + slot] = lengths[item]
        table[2 + 2 * per + slot] = text_lengths[item]


def gather_first_kernel(table, *refs):
    for to, source in enumerate(refs[:-1]):
        refs[-1][to] = source[0]


def gather_kernel(table, *refs, per):
    rows, texts, cots, mixed, cot = refs[0], refs[1 : 1 + per], refs[1 + per : 1 + 2 * per], refs[-2], refs[-1]
    block, short = rows.shape[1], texts[0].shape[1]
    mixed[0, :block] = rows[0]
    for slot in range(per):
        mixed[0, block + slot * short : block + (slot + 1) * short] = texts[slot][0]
        cot[0, slot] = cots[slot][0]


def gate_kernel(*refs):
    pass


def ahead(work, make, use):
    made = make(*work[0])
    for number, item in enumerate(work):
        later = make(*work[number + 1]) if number + 1 < len(work) else None
        use(item, made)
        made = later


def soften(scores):
    top = jnp.max(scores, 1, keepdims=True)
    return jnp.exp2(scores - top).astype(BF), top


def soft_back(scores, d_prob, lse, delta):
    prob = jnp.exp2(scores - lse)
    return prob.astype(BF), (prob * (d_prob - delta)).astype(BF)


def self_fwd_kernel(
    table, x_ref, mod_ref, w_ref, *refs, blocks, qb, score_scale, length_at
):
    rows_ref, qkv_ref, att_ref, lse_ref, held = refs[-5:]
    step = pl.program_id(0)
    width = rows_ref.shape[-1]
    count = att_ref.shape[1]
    block = rows_ref.shape[1]
    pairs = H // 2

    @pl.when(step < blocks)
    def _():
        rows_ref[0] = x_ref[0]
        shift, scale = mod_ref[0, 0:1], mod_ref[0, 1:2]
        hidden = strips(lambda rows: modulate(rows, shift, scale), x_ref[0])
        at = pl.ds(pl.multiple_of(step * block, block), block)
        for part in range(3):
            made = nn(hidden, w_ref[:, part * width : (part + 1) * width])
            if part == 0:
                made = made * (score_scale * LOG2E)
            made = made.astype(BF)
            qkv_ref[0, :, part * width : (part + 1) * width] = made
            for pair in range(pairs):
                held[part * pairs + pair, at] = made[:, pair * 128 : pair * 128 + 128]

    for klen in (count // 4, count // 2, count):

        @pl.when((step >= blocks) & (table[length_at] == klen))
        def _(klen=klen):
            pair = step - blocks
            keys = held[pairs + pair, :klen]
            values = jnp.concatenate([held[2 * pairs + pair, :klen], jnp.ones((klen, 128), BF)], 1)

            def inner(position, carry):
                rows = pl.ds(pl.multiple_of(position * qb, qb), qb)
                queries = held[pair, rows]
                work = [(half, at) for at in range(0, qb, SUB) for half in (0, 1)]
                outs = [[], []]

                def score(half, at):
                    return nt(keep_half(queries[at : at + SUB], half), keys)

                def use(place, scores):
                    half, at = place
                    prob, top = strips(soften, scores)
                    mixed = nn(prob, values)
                    total = mixed[:, 128:]
                    cols = pl.ds(pl.multiple_of(position * qb + at, SUB), SUB)
                    lse_ref[0, 0, half : half + 1, cols] = (top + jnp.log2(total[:, :1])).T
                    outs[half].append(mixed[:, :128] / total)

                ahead(work, score, use)
                outs = [jnp.concatenate(out, 0) for out in outs]
                att_ref[0, rows] = jnp.where(lane_half(0), outs[0], outs[1]).astype(BF)
                return carry

            lax.fori_loop(0, count // qb, inner, 0)


def self_bwd_kernel(
    table, q_ref, k_ref, v_ref, o_ref, do_ref, lse_ref, x_ref, g1_ref, mod_ref, w_ref, *refs,
    slot, length_at, pairs, blocks, qb, score_scale, nf, ni, last,
):
    if last:
        d_early, x_early, mod_early, dx_ref, dmod_ref, keep_ref, send_ref, held, dk_acc, dv_acc, acc = refs
    else:
        text_ref, dx_ref, dmod_ref, d_out, held, dk_acc, dv_acc = refs
    step = pl.program_id(0)
    count = q_ref.shape[1]
    width = x_ref.shape[-1]
    block = x_ref.shape[1]
    used = table[length_at]
    for klen in (count // 4, count // 2, count):

        @pl.when((step < pairs) & (used == klen))
        def _(klen=klen):
            keys = k_ref[0, :klen]
            values = v_ref[0, :klen]
            dk_acc[:klen] = jnp.zeros((klen, 128), F32)
            dv_acc[:klen] = jnp.zeros((klen, 128), F32)

            def inner(position, carry):
                rows = pl.ds(pl.multiple_of(position * qb, qb), qb)
                queries = q_ref[0, rows]
                grad = do_ref[0, rows]
                dots = (grad.astype(F32) * o_ref[0, rows].astype(F32)).T
                d_queries = [[], []]
                work = [(half, at) for at in range(0, qb, BSUB) for half in (0, 1)]

                def score(half, at):
                    q_half = keep_half(queries[at : at + BSUB], half)
                    grad_half = keep_half(grad[at : at + BSUB], half)
                    return q_half, grad_half, nt(keys, q_half), nt(values, grad_half)

                def use(place, made):
                    half, at = place
                    q_half, grad_half, scores, d_prob = made
                    delta = jnp.sum(dots[64 * half : 64 * half + 64, at : at + BSUB], 0, keepdims=True)
                    cols = pl.ds(pl.multiple_of(position * qb + at, BSUB), BSUB)
                    lse = lse_ref[0, 0, half : half + 1, cols]
                    prob, d_scores = strips(partial(soft_back, lse=lse, delta=delta), scores, d_prob)
                    dv_acc[:klen] += nn(prob, grad_half)
                    dk_acc[:klen] += nn(d_scores, q_half)
                    d_queries[half].append(tn(d_scores, keys))

                ahead(work, score, use)
                d_queries = [jnp.concatenate(part, 0) for part in d_queries]
                held[step, rows] = (jnp.where(lane_half(0), d_queries[0], d_queries[1]) * score_scale).astype(BF)
                return carry

            lax.fori_loop(0, count // qb, inner, 0)
            held[pairs + step, :klen] = (dk_acc[:klen] * (1.0 / LOG2E)).astype(BF)
            held[2 * pairs + step, :klen] = dv_acc[:klen].astype(BF)
            if klen < count:
                held[pairs + step, klen:] = jnp.zeros((count - klen, 128), BF)
                held[2 * pairs + step, klen:] = jnp.zeros((count - klen, 128), BF)

    @pl.when(step == pairs)
    def _():
        dmod_ref[...] = jnp.zeros_like(dmod_ref)
        if last:
            acc[...] = jnp.zeros_like(acc)

    @pl.when((step >= pairs) & (step < pairs + blocks))
    def _():
        rows = pl.ds(pl.multiple_of((step - pairs) * block, block), block)
        d_qkv = jnp.concatenate([held[at, rows] for at in range(3 * pairs)], 1)
        shift, scale = mod_ref[0, 0:1], mod_ref[0, 1:2]
        d_hidden = nt(d_qkv, w_ref[...])
        sums = Columns(2)

        def leave(x, dh, upstream):
            normed, inverse = ln_parts(x.astype(F32))
            sums.add(0, dh)
            sums.add(1, dh * normed)
            out = upstream.astype(F32) + ln_back(normed, inverse, dh * (1.0 + scale))
            return out.astype(BF), (normed * (1.0 + scale) + shift).astype(BF)

        dx_ref[0, :block], hidden = strips(leave, x_ref[0], d_hidden, g1_ref[0])
        for at in range(2):
            dmod_ref[0, at : at + 1] += sums.total(at)
        if last:
            acc[...] += tn(hidden, d_qkv)
        else:
            d_out[...] = d_qkv
            short = text_ref.shape[2]
            for part in range(text_ref.shape[1]):
                dx_ref[0, block + part * short : block + (part + 1) * short] = text_ref[0, part]

    if last:

        @pl.when((step >= pairs + blocks) & (step < pairs + 2 * blocks))
        def _():
            shift, scale = mod_early[0, 0:1], mod_early[0, 1:2]
            hidden = strips(lambda rows: modulate(rows, shift, scale), x_early[0])
            acc[...] += tn(hidden, d_early[...])

        @pl.when(step >= pairs + 2 * blocks)
        def _():
            ra, cb = width // ni, 3 * width // nf
            for part in range(FIN):
                item = ((step - pairs - 2 * blocks) * FIN + part) ^ table[1]
                for frame in range(nf):
                    cut = acc[pl.ds(pl.multiple_of(item * ra, 16), ra), frame * cb : (frame + 1) * cb].astype(BF)
                    rest = jnp.concatenate([cut[: ra // 2, PACK:], cut[ra // 2 :, PACK:]], 1)
                    store_block(
                        jnp.concatenate([cut[:, :PACK], rest], 0), part, frame, table[0], 0, keep_ref, send_ref
                    )


def cross_kernel(
    table, att_ref, x_ref, mod_ref, text_ref, wkv_ref, wo_ref, wq_ref, wco_ref,
    kv_ref, text_rows, first_ref, second_ref, ba_ref, bb_ref, cq_ref, cr_ref, lse_ref, *, score_scale, length_at,
):
    width = x_ref.shape[-1]
    slots = kv_ref.shape[1]
    used = table[length_at + pl.program_id(0)]

    @pl.when(pl.program_id(1) == 0)
    def _():
        text_rows[0] = jnp.concatenate([text_ref[at] for at in range(text_ref.shape[0])], 0)
        kv_ref[0] = nn(text_rows[0], wkv_ref[...]).astype(BF)

    branch_a = nn(att_ref[0], wo_ref[...])
    gate_a, gate_b, shift, scale = mod_ref[0, 2:3], mod_ref[0, 5:6], mod_ref[0, 3:4], mod_ref[0, 4:5]

    def enter(rows, branch):
        first = rows.astype(F32) + gate_a * branch
        return branch.astype(BF), first, modulate(first, shift, scale)

    ba_ref[0], first, hidden = strips(enter, x_ref[0], branch_a)
    first_ref[0] = first.astype(BF)
    cq_ref[0] = (nn(hidden, wq_ref[...]) * (score_scale * LOG2E)).astype(BF)
    valid = lax.broadcasted_iota(jnp.int32, (1, slots), 1) < used
    ones = jnp.ones((slots, 128), BF)
    count = cq_ref.shape[1]
    outs = {}

    def score(pair, half, at):
        cols = slice(pair * 128, pair * 128 + 128)
        return nt(keep_half(cq_ref[0, at : at + CSUB, cols], half), kv_ref[0, :, cols])

    def use(place, scores):
        pair, half, at = place
        prob, top = strips(lambda part: soften(jnp.where(valid, part, -1e30)), scores)
        values = kv_ref[0, :, width + pair * 128 : width + pair * 128 + 128]
        mixed = nn(prob, jnp.concatenate([values, ones], 1))
        total = mixed[:, 128:]
        lse_ref[0, pair, half : half + 1, at : at + CSUB] = (top + jnp.log2(total[:, :1])).T
        outs[half] = mixed[:, :128] / total
        if half == 1:
            cr_ref[0, at : at + CSUB, pair * 128 : pair * 128 + 128] = jnp.where(
                lane_half(0), outs[0], outs[1]
            ).astype(BF)

    work = [(pair, half, at) for pair in range(H // 2) for at in range(0, count, CSUB) for half in (0, 1)]
    ahead(work, score, use)
    branch_b = nn(cr_ref[0], wco_ref[...])
    bb_ref[0], second_ref[0] = strips(
        lambda rows, branch: (branch.astype(BF), (rows + gate_b * branch).astype(BF)), first, branch_b
    )


def mlp_kernel(
    table, second_ref, cot_ref, mod_ref, wup_ref, wdn_ref,
    out_ref, g2_ref, dmod_ref, gw_ref, up_acc, dn_acc, *, blocks, total, chunk, nf, ni,
):
    step = pl.program_id(0)
    width = second_ref.shape[-1]
    ff = wup_ref.shape[-1]

    @pl.when(step == 0)
    def _():
        up_acc[...] = jnp.zeros_like(up_acc)
        dn_acc[...] = jnp.zeros_like(dn_acc)

    @pl.when(step < total)
    def _():
        shift, scale, gate = mod_ref[0, 6:7], mod_ref[0, 7:8], mod_ref[0, 8:9]
        hidden = strips(lambda rows: modulate(rows, shift, scale), second_ref[0])
        cot = jnp.concatenate([cot_ref[at, 0] for at in range(cot_ref.shape[0])], 0)
        d_branch = strips(lambda rows: (rows.astype(F32) * gate).astype(BF), cot)
        def middle(up_proj, d_act):
            below, slope = gelu_parts(up_proj)
            return (up_proj * below).astype(BF), (d_act * slope).astype(BF)

        third = chunk // 3
        span = width // 3
        count = ff // chunk
        made, done = {}, {}
        branches = [jnp.zeros((second_ref.shape[1], span), F32)] * 3
        d_hiddens = [jnp.zeros((second_ref.shape[1], span), F32)] * 3
        for at in range(count + 2):
            for part in range(3):
                sub = slice(part * span, (part + 1) * span)
                if at < count:
                    cols = slice(at * chunk + part * third, at * chunk + (part + 1) * third)
                    made[at, part] = nn(hidden, wup_ref[:, cols]), nt(d_branch, wdn_ref[cols])
                if 1 <= at <= count:
                    done[at - 1, part] = strips(middle, *made.pop((at - 1, part)))
                if at >= 2:
                    cols = slice((at - 2) * chunk, (at - 1) * chunk)
                    act, d_up = (jnp.concatenate([done[at - 2, p][side] for p in range(3)], 1) for side in (0, 1))
                    branches[part] += nn(act, wdn_ref[cols, sub])
                    d_hiddens[part] += nt(d_up, wup_ref[sub, cols])
                    cols = slice((at - 2) * chunk + part * third, (at - 2) * chunk + (part + 1) * third)
                    dn_acc[cols] += tn(done[at - 2, part][0], d_branch)
                    up_acc[:, cols] += tn(hidden, done[at - 2, part][1])
        branch, d_hidden = jnp.concatenate(branches, 1), jnp.concatenate(d_hiddens, 1)

        @pl.when(step % blocks == 0)
        def _():
            dmod_ref[...] = jnp.zeros_like(dmod_ref)

        sums = Columns(3)

        def leave(second, cot, branch_rows, dh):
            second = second.astype(F32)
            normed, inverse = ln_parts(second)
            upstream = cot.astype(F32)
            sums.add(0, dh)
            sums.add(1, dh * normed)
            sums.add(2, upstream * branch_rows)
            upstream = upstream + ln_back(normed, inverse, dh * (1.0 + scale))
            return (second + gate * branch_rows).astype(BF), upstream.astype(BF)

        out, g2_ref[0] = strips(leave, second_ref[0], cot, branch, d_hidden)
        rows = out_ref.shape[2]
        for at in range(out_ref.shape[0]):
            out_ref[at, 0] = out[at * rows : (at + 1) * rows]
        for at in range(3):
            dmod_ref[0, at : at + 1] += sums.total(at)

    @pl.when(step >= total)
    def _():
        ra, cb = width // ni, ff // nf
        for part in range(FIN):
            item = (step - total) * FIN + part
            for frame in range(nf):
                cut = up_acc[pl.ds(pl.multiple_of(item * ra, 16), ra), frame * cb : (frame + 1) * cb].astype(BF)
                gw_ref[part, frame, :ra] = cut[:, :PACK]
                gw_ref[part, frame, ra : 2 * ra] = cut[:, PACK:]
                gw_ref[part, frame, 2 * ra :] = pack_square(
                    dn_acc, item, ff // ni, width // nf, frame * (width // nf)
                )


def cross_back_kernel(
    table, g2_ref, bb_ref, cr_ref, cq_ref, att_ref, ba_ref, first_ref, mod_ref, kv_ref, lse_ref, text_ref,
    wo_ref, wq_ref, wco_ref, wkv_ref, _,
    g1_ref, datt_ref, text_out, dmod_ref, all_ref,
    o_acc, q_acc, co_acc, kv_acc, dtext, staged, sems, *, blocks, total, score_scale, nf, ni, length_at,
):
    step = pl.program_id(0)
    width = g2_ref.shape[-1]
    slots = kv_ref.shape[1]

    @pl.when(step == 0)
    def _():
        o_acc[...] = jnp.zeros_like(o_acc)
        q_acc[...] = jnp.zeros_like(q_acc)
        co_acc[...] = jnp.zeros_like(co_acc)
        kv_acc[...] = jnp.zeros_like(kv_acc)

    @pl.when(step < total)
    def _():
        @pl.when(step % blocks == 0)
        def _():
            dmod_ref[...] = jnp.zeros_like(dmod_ref)
            dtext[...] = jnp.zeros_like(dtext)

        used = table[length_at + step // blocks]
        gate_b = mod_ref[0, 5:6]
        sums = Columns(4)

        def enter(upstream, branch):
            upstream = upstream.astype(F32)
            sums.add(3, upstream * branch.astype(F32))
            return (upstream * gate_b).astype(BF)

        d_branch_b = strips(enter, g2_ref[0], bb_ref[0])
        co_acc[...] += tn(cr_ref[0], d_branch_b)
        d_crossed = nt(d_branch_b, wco_ref[...])
        slot_of = lax.broadcasted_iota(jnp.int32, (slots, 1), 0)
        parts = []
        kept = {}

        def score(pair, half):
            cols = slice(pair * 128, pair * 128 + 128)
            vcols = slice(width + pair * 128, width + pair * 128 + 128)
            grad = d_crossed[:, cols].astype(BF)
            q_half = keep_half(cq_ref[0, :, cols], half)
            grad_half = keep_half(grad, half)
            return grad, q_half, grad_half, nt(kv_ref[0, :, cols], q_half), nt(kv_ref[0, :, vcols], grad_half)

        def use(place, made):
            pair, half = place
            grad, q_half, grad_half, scores, d_prob = made
            cols = slice(pair * 128, pair * 128 + 128)
            vcols = slice(width + pair * 128, width + pair * 128 + 128)
            if half == 0:
                kept["dots"] = (grad.astype(F32) * cr_ref[0, :, cols].astype(F32)).T
            delta = jnp.sum(kept["dots"][64 * half : 64 * half + 64], 0, keepdims=True)
            lse = lse_ref[0, pair, half : half + 1]

            def back(part, d_part, at):
                return soft_back(jnp.where(at < used, part, -1e30), d_part, lse, delta)

            prob, d_scores = strips(back, scores, d_prob, slot_of)
            d_values = nn(prob, grad_half)
            d_keys = nn(d_scores, q_half)
            d_query = tn(d_scores, kv_ref[0, :, cols])
            if half == 0:
                kept["sums"] = d_keys, d_values, d_query
                return
            first_keys, first_values, first_query = kept["sums"]
            dtext[:, cols] += (first_keys + d_keys) * (1.0 / LOG2E)
            dtext[:, vcols] += first_values + d_values
            parts.append((jnp.where(lane_half(0), first_query, d_query) * score_scale).astype(BF))

        ahead([(pair, half) for pair in range(H // 2) for half in (0, 1)], score, use)
        d_cq = jnp.concatenate(parts, 1)
        shift, scale, gate = mod_ref[0, 3:4], mod_ref[0, 4:5], mod_ref[0, 2:3]
        d_hidden = nt(d_cq, wq_ref[...])

        def leave(first, dh, upstream, branch):
            normed, inverse = ln_parts(first.astype(F32))
            sums.add(1, dh)
            sums.add(2, dh * normed)
            upstream = upstream.astype(F32) + ln_back(normed, inverse, dh * (1.0 + scale))
            sums.add(0, upstream * branch.astype(F32))
            return (normed * (1.0 + scale) + shift).astype(BF), upstream.astype(BF), (upstream * gate).astype(BF)

        hidden, g1_ref[0], d_branch_a = strips(leave, first_ref[0], d_hidden, g2_ref[0], ba_ref[0])
        for at in range(4):
            dmod_ref[0, at : at + 1] += sums.total(at)
        datt_ref[0] = nt(d_branch_a, wo_ref[...]).astype(BF)
        q_acc[...] += tn(hidden, d_cq)
        o_acc[...] += tn(att_ref[0], d_branch_a)

        @pl.when(step % blocks == blocks - 1)
        def _():
            low = dtext[...].astype(BF)
            kv_acc[...] += tn(text_ref[0], low)
            made = nt(low, wkv_ref[...]).astype(BF)
            short = text_out.shape[2]
            for frame in range(nf):
                text_out[frame, 0] = made[frame * short : (frame + 1) * short]

    @pl.when(step >= total)
    def _():
        ra, cb = width // ni, width // nf
        half = ra // 2
        depth = staged.shape[3]
        number = step - total
        side = number % 2

        def moved(at):
            place = pl.ds(at * FIN, FIN)
            return pltpu.make_async_copy(
                staged.at[at % 2], all_ref.at[place, :, pl.ds(all_ref.shape[2] - depth, depth)], sems.at[at % 2]
            )

        @pl.when(number >= 2)
        def _():
            moved(number - 2).wait()

        for part in range(FIN):
            item = number * FIN + part
            for frame in range(nf):
                for place, acc in enumerate((o_acc, q_acc, co_acc)):
                    cut = pack_square(acc, item, ra, cb, frame * cb)
                    staged[side, part, frame, place * half : (place + 1) * half] = cut
                cut = kv_acc[pl.ds(pl.multiple_of(item * ra, 16), ra), 2 * frame * cb : 2 * (frame + 1) * cb]
                staged[side, part, frame, 3 * half :] = cut.astype(BF)
        moved(number).start()

        @pl.when(number == ni // FIN - 1)
        def _():
            moved(number - 1).wait()
            moved(number).wait()


def deal_kernel(table, *refs, at, items, group):
    out_ref = refs[-1]
    count = (len(refs) - 1) // group
    for part in range(group):
        sources = refs[part * count : (part + 1) * count]
        if count == 1:
            out_ref[part] = sources[0][0, 0].astype(out_ref.dtype)
            continue
        slot_of = table[at + items + pl.program_id(0) * group + part]
        for slot, ref in enumerate(sources):

            @pl.when(slot_of == slot)
            def _(ref=ref, part=part):
                out_ref[part] = ref[0, 0].astype(out_ref.dtype)


def land_kernel(keep, got, *refs):
    outs = refs[-2:]
    for half, out in enumerate(outs):
        out[...] = (keep[0, half].astype(F32) + got[0, half].astype(F32)).astype(BF)[None]


def finish_kernel(sum_ref, *refs):
    up, down, squares, kv = refs[-6], refs[-5], refs[-4:-1], refs[-1]
    ra, cb = up.shape
    up[:, : cb // 2] = sum_ref[:ra].astype(F32)
    up[:, cb // 2 :] = sum_ref[ra : 2 * ra].astype(F32)
    at = 2 * ra + down.shape[0] // 2
    down[...] = untall(sum_ref[2 * ra : at].astype(F32))
    half = ra // 2
    for out in squares:
        out[...] = untall(sum_ref[at : at + half].astype(F32))
        at += half
    kv[...] = sum_ref[at:].astype(F32)


def finish_qkv_kernel(keep, got, *refs):
    out = refs[-1]
    ra = out.shape[0]
    total = keep[...].astype(F32) + got[...].astype(F32)
    out[:, :PACK] = total[:ra]
    out[:, PACK:] = untall(total[ra:])


def untall(block):
    half = block.shape[1] // 2
    return jnp.concatenate([block[:, :half], block[:, half:]], 0)


def cost(flops, moved, exps=0):
    return pl.CostEstimate(flops=int(flops), bytes_accessed=int(moved), transcendentals=int(exps))


def params():
    return pltpu.CompilerParams(vmem_limit_bytes=LIMIT)


def whole(shape):
    return pl.BlockSpec(shape, lambda *_: (0,) * len(shape), pipeline_mode=pl.Buffered(1))


def run(kernel, name, grid, in_specs, args, out_specs, out_shape, scratch=(), deps=(), work=None, aliases=None):
    inputs = len(args)

    def body(*refs):
        kernel(*refs[:inputs], *refs[inputs + len(deps) :])

    return pl.pallas_call(
        body,
        grid_spec=pltpu.PrefetchScalarGridSpec(
            num_scalar_prefetch=1,
            grid=grid,
            in_specs=list(in_specs) + [pl.BlockSpec(memory_space=pl.ANY)] * len(deps),
            out_specs=out_specs,
            scratch_shapes=list(scratch),
        ),
        out_shape=out_shape,
        input_output_aliases=aliases or {},
        compiler_params=params(),
        cost_estimate=work,
        name=name,
    )(*args, *deps)


def any_spec(count):
    return [pl.BlockSpec(memory_space=pl.ANY)] * count


def struct(shape, dtype):
    return jax.ShapeDtypeStruct(shape, dtype)


def start_call(where, lengths, text_lengths, items, nf):
    size = 2 + 3 * (items // nf) + 3 * items
    smem = pl.BlockSpec(memory_space=pltpu.SMEM)
    return pl.pallas_call(
        partial(start_kernel, items=items, nf=nf),
        in_specs=[smem] * 3,
        out_specs=smem,
        out_shape=struct((size,), jnp.int32),
        name="start",
    )(where, lengths, text_lengths)


def gather_first_call(table, rows, nf):
    items, block, width = rows.shape
    per = items // nf
    at = 2 + 3 * per + 2 * items
    return run(
        gather_first_kernel,
        "gather_first",
        (1,),
        [pl.BlockSpec((1, block, width), lambda t, s, to=to: (s[at + to * per], 0, 0)) for to in range(nf)],
        (table,) + (rows,) * nf,
        pl.BlockSpec((nf, block, width), lambda t, s: (0, 0, 0)),
        struct((nf, block, width), BF),
    )


def gather_call(table, rows, text, cot, nf):
    items, block, width = rows.shape
    per = items // nf
    at = 2 + 3 * per + 2 * items
    short = text.shape[1]

    def source(size, slot):
        return pl.BlockSpec((1, size, width), lambda t, s: (s[at + t * per + slot], 0, 0))

    return run(
        partial(gather_kernel, per=per),
        "gather",
        (nf,),
        [source(block, 1)] + [source(short, slot) for slot in range(per)] + [source(block, slot) for slot in range(per)],
        (table, rows) + (text,) * per + (cot,) * per,
        [
            pl.BlockSpec((1, block + per * short, width), lambda t, s: (t, 0, 0)),
            pl.BlockSpec((1, per, block, width), lambda t, s: (t, 0, 0, 0)),
        ],
        [struct((nf, block + per * short, width), BF), struct((nf, per, block, width), BF)],
    )


def gate_call(arrays, deps):
    return pl.pallas_call(
        gate_kernel,
        in_specs=any_spec(len(arrays) + len(deps)),
        out_specs=any_spec(len(arrays)),
        out_shape=[struct(array.shape, array.dtype) for array in arrays],
        input_output_aliases={at: at for at in range(len(arrays))},
        compiler_params=params(),
        name="gate",
    )(*arrays, *deps)


def halves(ni, nf, depth, total):
    spec = pl.BlockSpec((FIN, nf // 2, depth, PACK), lambda t, s: (jnp.maximum(t - total, 0), 0, 0, 0))
    return [spec] * 2, [struct((ni, nf // 2, depth, PACK), BF)] * 2


def self_fwd_call(table, slot, rows, mod, weight, kept, per, block, qb, score_scale, deps):
    blocks, _, width = rows.shape
    count = blocks * block
    pairs = H // 2

    def early(t):
        return jnp.minimum(t, blocks - 1)

    def late(t):
        return jnp.maximum(t - blocks, 0)

    return run(
        partial(self_fwd_kernel, blocks=blocks, qb=qb, score_scale=score_scale, length_at=2 + per + slot),
        "self_fwd",
        (blocks + pairs,),
        [pl.BlockSpec((1, block, width), lambda t, s: (early(t), 0, 0))]
        + [pl.BlockSpec((1, 9, width), lambda t, s: (slot, 0, 0)), whole(weight.shape)]
        + any_spec(len(kept)),
        (table, rows, mod, weight, *kept),
        [
            pl.BlockSpec((1, block, width), lambda t, s: (slot, early(t), 0)),
            pl.BlockSpec((1, block, 3 * width), lambda t, s: (slot, early(t), 0)),
            pl.BlockSpec((1, count, 128), lambda t, s: (slot, 0, late(t))),
            pl.BlockSpec((1, 1, 2, count), lambda t, s: (slot, late(t), 0, 0)),
        ],
        [
            struct((per, count, width), BF),
            struct((per, count, 3 * width), BF),
            struct((per, count, width), BF),
            struct((per, pairs, 2, count), F32),
        ],
        scratch=[pltpu.VMEM((3 * pairs, count, 128), BF)],
        deps=deps,
        work=cost(6 * count * width * width + 16 * count * count * width, count * width * 16, H * count * count),
        aliases={4 + at: at for at in range(len(kept))},
    )


def self_bwd_call(
    table, slot, qkv, att, d_att, lse, rows, g1, mod, weight, early, text, qb, score_scale, block, nf, ni, deps
):
    per, count, width = att.shape
    pairs = H // 2
    blocks = count // block
    last = early is not None
    steps = pairs + blocks
    lines = block if last else block + text.shape[1] * text.shape[2]

    def pair(t):
        return jnp.minimum(t, pairs - 1)

    def row(t):
        return jnp.clip(t - pairs, 0, blocks - 1)

    def row_early(t):
        return jnp.clip(t - pairs - blocks, 0, blocks - 1)

    column = pl.BlockSpec((1, count, 128), lambda t, s: (slot, 0, pair(t)))
    by_row = pl.BlockSpec((1, block, width), lambda t, s: (slot, row(t), 0))
    in_specs = [
        pl.BlockSpec((1, count, 128), lambda t, s, part=part: (slot, 0, part * pairs + pair(t))) for part in range(3)
    ] + [column, column, pl.BlockSpec((1, 1, 2, count), lambda t, s: (slot, pair(t), 0, 0))]
    in_specs += [by_row, by_row, pl.BlockSpec((1, 9, width), lambda t, s: (slot, 0, 0)), whole(weight.shape)]
    args = [table, qkv, qkv, qkv, att, d_att, lse, rows, g1, mod, weight]
    out_specs = [
        pl.BlockSpec((1, lines, width), lambda t, s: (row(t), 0, 0)),
        pl.BlockSpec((1, 2, width), lambda t, s: (0, 0, 0)),
    ]
    out_shape = [struct((blocks, lines, width), BF), struct((1, 2, width), F32)]
    scratch = [pltpu.VMEM((3 * pairs, count, 128), BF)] + [pltpu.VMEM((count, 128), F32)] * 2
    if last:
        in_specs += [
            pl.BlockSpec((block, 3 * width), lambda t, s: (row_early(t), 0)),
            pl.BlockSpec((1, block, width), lambda t, s: (slot - 1, row_early(t), 0)),
            pl.BlockSpec((1, 9, width), lambda t, s: (slot - 1, 0, 0)),
        ]
        args += [early, rows, mod]
        specs, shapes = halves(ni, nf, 3 * width * width // (nf * ni * PACK), steps + blocks)
        out_specs += specs
        out_shape += shapes
        scratch += [pltpu.VMEM((width, 3 * width), F32)]
        steps += blocks + ni // FIN
    else:
        in_specs += [pl.BlockSpec((1,) + text.shape[1:], lambda t, s: (row(t), 0, 0, 0))]
        args += [text]
        out_specs += [pl.BlockSpec((block, 3 * width), lambda t, s: (row(t), 0))]
        out_shape += [struct((count, 3 * width), BF)]
    return run(
        partial(
            self_bwd_kernel,
            slot=slot,
            length_at=2 + per + slot,
            pairs=pairs,
            blocks=blocks,
            qb=qb,
            score_scale=score_scale,
            nf=nf,
            ni=ni,
            last=last,
        ),
        "self_bwd",
        (steps,),
        in_specs,
        args,
        out_specs,
        out_shape,
        scratch=scratch,
        deps=deps,
        work=cost(40 * count * count * width + 12 * count * width * width, count * width * 30, H * count * count),
    )


def cross_call(table, att, rows, mod, text, short, wkv, wo, wq, wco, score_scale, block, deps):
    items, count, width = rows.shape
    nf, lines, _ = text.shape
    skip = lines // short - items
    slots = nf * short
    row = pl.BlockSpec((1, block, width), lambda i, j, s: (i, j, 0))
    return run(
        partial(cross_kernel, score_scale=score_scale, length_at=2 + 2 * items),
        "cross_fwd",
        (items, count // block),
        [
            row,
            row,
            pl.BlockSpec((1, 9, width), lambda i, j, s: (i, 0, 0)),
            pl.BlockSpec((nf, short, width), lambda i, j, s: (0, skip + i, 0)),
            whole(wkv.shape),
            whole(wo.shape),
            whole(wq.shape),
            whole(wco.shape),
        ],
        (table, att, rows, mod, text, wkv, wo, wq, wco),
        [pl.BlockSpec((1, slots, 2 * width), lambda i, j, s: (i, 0, 0))]
        + [pl.BlockSpec((1, slots, width), lambda i, j, s: (i, 0, 0))]
        + [row] * 6
        + [pl.BlockSpec((1, H // 2, 2, block), lambda i, j, s: (i, 0, 0, j))],
        [struct((items, slots, 2 * width), BF), struct((items, slots, width), BF)]
        + [struct(rows.shape, BF)] * 6
        + [struct((items, H // 2, 2, count), F32)],
        deps=deps,
        work=cost(
            items * count * (6 * width * width + 16 * slots * width), items * count * width * 20, items * H * count * slots
        ),
    )


def back_grid(items, count, block):
    blocks = count // block
    total = items * blocks

    def at(t):
        return jnp.minimum(t, total - 1)

    def by_item(t, s):
        return (at(t) // blocks, 0, 0)

    def by_row(t, s):
        return (at(t) // blocks, at(t) % blocks, 0)

    return blocks, total, by_item, by_row


def mlp_call(table, second, cot, mod, wup, wdn, block, chunk, nf, ni, deps):
    items, count, width = second.shape
    ff = wup.shape[1]
    blocks, total, by_item, by_row = back_grid(items, count, block)
    row = pl.BlockSpec((1, block, width), by_row)
    shard = pl.BlockSpec(
        (block // cot.shape[2], 1, cot.shape[2], width), lambda t, s: (by_row(t, s)[1], by_row(t, s)[0], 0, 0)
    )
    depth = 2 * width * ff // (nf * ni * PACK)
    return run(
        partial(mlp_kernel, blocks=blocks, total=total, chunk=chunk, nf=nf, ni=ni),
        "mlp",
        (total + ni // FIN,),
        [row, shard, pl.BlockSpec((1, 9, width), by_item), whole(wup.shape), whole(wdn.shape)],
        (table, second, cot, mod, wup, wdn),
        [shard, row, pl.BlockSpec((1, 3, width), by_item)]
        + [pl.BlockSpec((FIN, nf, depth, PACK), lambda t, s: (jnp.maximum(t - total, 0), 0, 0, 0))],
        [struct(cot.shape, BF), struct(second.shape, BF), struct((items, 3, width), F32)]
        + [struct((ni, nf, depth + 5 * width * width // (nf * ni * PACK), PACK), BF)],
        scratch=[pltpu.VMEM((width, ff), F32), pltpu.VMEM((ff, width), F32)],
        deps=deps,
        work=cost(12 * items * count * width * ff, items * count * width * 16, items * count * ff * 2),
    )


def cross_back_call(
    table, g2, bb, cr, cq, att, ba, first, mod, kv, lse, text, wo, wq, wco, wkv, blocks_all, score_scale, block, nf, ni, deps
):
    items, count, width = g2.shape
    slots = kv.shape[1]
    short = slots // nf
    blocks, total, by_item, by_row = back_grid(items, count, block)
    row = pl.BlockSpec((1, block, width), by_row)
    by_slot = pl.BlockSpec((nf, 1, short, width), lambda t, s: (0, by_item(t, s)[0], 0, 0))
    depth = 5 * width * width // (nf * ni * PACK)
    lse_spec = pl.BlockSpec((1, H // 2, 2, block), lambda t, s: (by_row(t, s)[0], 0, 0, by_row(t, s)[1]))
    return run(
        partial(
            cross_back_kernel,
            blocks=blocks,
            total=total,
            score_scale=score_scale,
            nf=nf,
            ni=ni,
            length_at=2 + 2 * items,
        ),
        "cross_bwd",
        (total + ni // FIN,),
        [row] * 7
        + [pl.BlockSpec((1, 9, width), by_item), pl.BlockSpec((1, slots, 2 * width), by_item), lse_spec]
        + [pl.BlockSpec((1, slots, width), by_item)]
        + [whole(weight.shape) for weight in (wo, wq, wco, wkv)]
        + any_spec(1),
        (table, g2, bb, cr, cq, att, ba, first, mod, kv, lse, text, wo, wq, wco, wkv, blocks_all),
        [row, row, by_slot, pl.BlockSpec((1, 4, width), by_item)] + any_spec(1),
        [struct(g2.shape, BF)] * 2
        + [struct((nf, items, short, width), BF), struct((items, 4, width), F32), struct(blocks_all.shape, BF)],
        scratch=[pltpu.VMEM((width, width), F32)] * 3
        + [pltpu.VMEM((width, 2 * width), F32), pltpu.VMEM((slots, 2 * width), F32)]
        + [pltpu.VMEM((2, FIN, nf, depth, PACK), BF), pltpu.SemaphoreType.DMA((2,))],
        aliases={16: 4},
        deps=deps,
        work=cost(
            items * count * (12 * width * width + 40 * slots * width), items * count * width * 24, items * H * count * slots
        ),
    )


def deal_call(table, jobs, per, name, deps=(), group=2):
    nf, _, _, width = jobs[0][0][0].shape
    items = nf * per
    at = 2 + 3 * per
    specs, args, counts = [], [], []
    for got, block, skip, _ in jobs:
        counts.append(len(got) * group)
        args += list(got) * group
        for part in range(group):
            if len(got) == 1:
                specs.append(
                    pl.BlockSpec(
                        (1, 1, block, width),
                        lambda t, s, part=part, skip=skip: (
                            s[at + t * group + part], 0, skip + s[at + items + t * group + part], 0
                        ),
                    )
                )
            else:
                specs += [
                    pl.BlockSpec((1, 1, block, width), lambda t, s, part=part: (s[at + t * group + part], 0, 0, 0))
                ] * len(got)

    def body(table, *refs):
        outs = refs[sum(counts) :]
        first = 0
        for count, out in zip(counts, outs):
            deal_kernel(table, *refs[first : first + count], out, at=at, items=items, group=group)
            first += count

    return run(
        body,
        name,
        (items // group,),
        specs,
        (table, *args),
        [pl.BlockSpec((group, job[1], width), lambda t, s: (t, 0, 0)) for job in jobs],
        [struct((items, job[1], width), job[3]) for job in jobs],
        deps=deps,
        work=cost(0, items * jobs[0][1] * width * 6),
    )


def small_call(kernel, name, args, out_shape, deps=()):
    return pl.pallas_call(
        kernel,
        in_specs=[pl.BlockSpec(arg.shape, lambda: (0,) * arg.ndim) for arg in args] + any_spec(len(deps)),
        out_specs=[pl.BlockSpec(out.shape, lambda: (0,) * len(out.shape)) for out in out_shape],
        out_shape=out_shape,
        compiler_params=params(),
        name=name,
    )(*args, *deps)


def exchange(blocks):
    return lax.all_to_all(blocks, "frames", 0, 0, tiled=True)


def swap(block, offset, nf):
    if offset == 0:
        return block
    return lax.ppermute(block, "frames", [(i, i ^ offset) for i in range(nf)])


def bits_of(count):
    return count.bit_length() - 1


class Sum:
    def __init__(self, keep, send, order, sizes):
        self.sizes = sizes
        ni, nf = sizes["items"], sizes["frames"]
        self.dims = [("items", bit) for bit in reversed(range(bits_of(ni)))]
        self.dims += [("frames", bit) for bit in reversed(range(1, bits_of(nf)))]
        shape = (2,) * len(self.dims) + keep.shape[2:]
        self.keep, self.send = keep.reshape(shape), send
        self.shape = shape
        self.steps = [("frames", 0)] + list(order)
        self.got = None

    def launch(self):
        name, bit = self.steps.pop(0)
        self.got = lax.ppermute(self.send, name, [(i, i ^ (1 << bit)) for i in range(self.sizes[name])])

    def land(self, deps=()):
        got = self.got.reshape(self.keep.shape)
        if not self.steps:
            return self.keep, got
        dim = self.dims.index(self.steps[0])
        self.dims.remove(self.steps[0])
        shape = self.keep.shape
        outer, inner = 2**dim, 2 ** (len(shape) - 3 - dim)
        view = (outer, 2, inner) + shape[-2:]
        out = struct((outer, inner) + shape[-2:], BF)
        source = pl.BlockSpec((1,) + view[1:], lambda t: (t, 0, 0, 0, 0))
        target = pl.BlockSpec((1,) + out.shape[1:], lambda t: (t, 0, 0, 0))
        self.keep, self.send = pl.pallas_call(
            land_kernel,
            grid=(outer,),
            in_specs=[source] * 2 + any_spec(len(deps)),
            out_specs=[target] * 2,
            out_shape=[out] * 2,
            compiler_params=params(),
            name="land",
        )(self.keep.reshape(view), got.reshape(view), *deps)
        left = shape[:dim] + shape[dim + 1 :]
        self.keep = self.keep.reshape(left)
        return None


def collect_items(rows, ni):
    for bit in range(bits_of(ni)):
        rows = jnp.concatenate([rows, lax.ppermute(rows, "items", [(i, i ^ (1 << bit)) for i in range(ni)])], 0)
    return rows


def total_here(blocks):
    flat = blocks.reshape((-1,) + blocks.shape[2:])
    return lax.psum_scatter(flat, ("items", "frames"), scatter_dimension=0, tiled=True)[0]


def items_whole(
    ni, nf, frames_in, cond, text, item_lengths, text_lengths, ada_weight, qkv_weight, out_weight,
    cross_q_weight, cross_kv_weight, cross_out_weight, up_weight, down_weight, cotangent,
):
    items, block, width = frames_in.shape
    per = items // nf
    ff = up_weight.shape[1]
    sizes = {"items": ni, "frames": nf}
    score_scale = (width // H) ** (-0.5)
    me = lax.axis_index("frames")
    row_item = lax.axis_index("items")
    x_first = [("items", bit) for bit in range(bits_of(ni))] + [("frames", bit) for bit in range(1, bits_of(nf))]

    table = start_call(jnp.stack([me, row_item]), item_lengths, text_lengths, items, nf)
    rows_first = exchange(gather_first_call(table, frames_in, nf))
    mixed_send, cot_send = gather_call(table, frames_in, text, cotangent, nf)

    cond_f = cond.astype(F32)
    low_cond = jax.nn.silu(cond_f).astype(BF)
    modulation = nn(low_cond, ada_weight)
    pick = table[2 : 2 + per, None] == jnp.arange(items, dtype=jnp.int32)[None, :]
    mod = jnp.sum(jnp.where(pick[:, :, None], modulation[None], 0.0), 1).reshape(per, 9, width)

    (mixed_send,) = gate_call([mixed_send], [rows_first, mod])
    mixed = exchange(mixed_send)
    kept = self_fwd_call(table, 0, rows_first, mod, qkv_weight, (), per, block, 512, score_scale, [mixed_send])
    (cot_send,) = gate_call([cot_send], [mixed])
    cot = exchange(cot_send)
    kept = self_fwd_call(table, 1, mixed, mod, qkv_weight, kept, per, block, 512, score_scale, [cot_send])
    rows, qkv, attended, self_lse = kept
    text_kv, text_rows, first, second, branch_a, branch_b, cross_q, crossed, cross_lse = cross_call(
        table, attended, rows, mod, mixed, text.shape[1], cross_kv_weight, out_weight, cross_q_weight, cross_out_weight,
        score_scale, 2 * block, [],
    )
    layer_send, g2, dmod_c, g_mlp = mlp_call(
        table, second, cot, mod, up_weight, down_weight, block, 768, nf, ni, []
    )
    layer_got = exchange(layer_send)
    g1, d_att, text_back, dmod_b, g_all = cross_back_call(
        table, g2, branch_b, crossed, cross_q, attended, branch_a, first, mod, text_kv, cross_lse, text_rows,
        out_weight, cross_q_weight, cross_out_weight, cross_kv_weight, g_mlp, score_scale, 2 * block, nf, ni, [],
    )
    sum_all = total_here(g_all)
    made_0, dmod_0, early = self_bwd_call(
        table, 0, qkv, attended, d_att, self_lse, rows, g1, mod, qkv_weight, None, text_back, 1024, score_scale, block, nf, ni,
        [],
    )
    got_0 = exchange(made_0)
    made_1, dmod_1, grad_keep, grad_send = self_bwd_call(
        table, 1, qkv, attended, d_att, self_lse, rows, g1, mod, qkv_weight, early, None, 1024, score_scale, block, nf, ni,
        [layer_got],
    )
    made_1, grad_send = gate_call([made_1, grad_send], [got_0])
    grad = Sum(grad_keep, grad_send, x_first, sizes)
    grad.launch()
    d_mod = jnp.concatenate([jnp.concatenate([dmod_0, dmod_1], 0), dmod_b, dmod_c], 1).reshape(per, 9 * width)
    ada_rows, ada_cols, cond_cols = width // ni, 9 * width // nf, width // nf
    high = d_mod.astype(BF)
    rest = (d_mod - high.astype(F32)).astype(BF)
    parts = nt(jnp.concatenate([high, rest], 0), ada_weight)
    parts = jnp.concatenate(
        [d_mod.reshape(per, nf, ada_cols), (parts[:per] + parts[per:]).reshape(per, nf, cond_cols)], 2
    ).transpose(1, 0, 2)
    parts = exchange(parts)
    (made_1,) = gate_call([made_1], [parts])
    got_1 = exchange(made_1)
    grad.land([parts])
    grad.launch()
    layer_out, text_grad = deal_call(
        table,
        [
            ([layer_got.reshape(nf, 1, per * block, width)], block, 0, BF),
            ([got_0[:, None]], text.shape[1], block // text.shape[1], F32),
        ],
        per,
        "deal_out",
        [grad.send],
    )
    grad.land([layer_out])
    grad.launch()
    (input_grad,) = deal_call(
        table, [([got_0[:, None], got_1[:, None]], block, 0, F32)], per, "deal_in", [grad.send]
    )
    grad.land([input_grad])
    grad.launch()
    (parts,) = gate_call([parts], [grad.send])
    parts = parts.reshape(items, ada_cols + cond_cols)
    at = 2 + 3 * per
    spot = table[at : at + items] * per + table[at + items : at + 2 * items]
    pick_row = spot[:, None] == jnp.arange(items, dtype=jnp.int32)[None, :]
    parts = jnp.sum(jnp.where(pick_row[:, :, None], parts[None], 0.0), 1)
    every = collect_items(jnp.concatenate([parts[:, :ada_cols], low_cond.astype(F32)], 1), ni)
    grad_ada = lax.dot_general(
        lax.dynamic_slice(every, (0, ada_cols + row_item * ada_rows), (items * ni, ada_rows), allow_negative_indices=False),
        every[:, :ada_cols],
        (((0,), (0,)), ((), ())),
        precision=lax.Precision.HIGHEST,
        preferred_element_type=F32,
    )
    cond_mine = lax.dynamic_slice(cond_f, (0, me * cond_cols), (items, cond_cols), allow_negative_indices=False)
    sigmoid_c = jax.nn.sigmoid(cond_mine)
    cond_grad = parts[:, ada_cols:] * (sigmoid_c * (1.0 + cond_mine * (1.0 - sigmoid_c)))

    while grad.steps:
        grad.land()
        grad.launch()
    square = struct((ada_rows, cond_cols), F32)
    grad_up, grad_down, grad_out, grad_cross_q, grad_cross_out, grad_cross_kv = small_call(
        finish_kernel,
        "finish",
        [sum_all],
        [struct((ada_rows, ff // nf), F32), struct((ff // ni, cond_cols), F32)]
        + [square] * 3
        + [struct((ada_rows, 2 * cond_cols), F32)],
    )
    (grad_qkv,) = small_call(finish_qkv_kernel, "finish_qkv", grad.land(), [struct((ada_rows, 3 * cond_cols), F32)])
    return (
        layer_out,
        input_grad,
        text_grad,
        cond_grad,
        grad_ada,
        grad_qkv,
        grad_out,
        grad_cross_q,
        grad_cross_kv,
        grad_cross_out,
        grad_up,
        grad_down,
    )


def on_device(mesh, *args):
    ni, nf = mesh.shape["items"], mesh.shape["frames"]
    if nf == 4 and args[0].shape[0] == 2 * nf and args[0].shape[-1] == 768 and 768 % (32 * ni) == 0:
        return items_whole(ni, nf, *args)
    return frames_split(*args)


def solution(mesh):
    in_specs = (
        P("items", "frames", None),
        P("items", None),
        P("items", "frames", None),
        P("items"),
        P("items"),
        P(),
        P(),
        P(),
        P(),
        P(),
        P(),
        P(),
        P(),
        P("items", "frames", None),
    )
    out_specs = (
        P("items", "frames", None),
        P("items", "frames", None),
        P("items", "frames", None),
        P("items", "frames"),
        P("items", "frames"),
        P("items", "frames"),
        P("items", "frames"),
        P("items", "frames"),
        P("items", "frames"),
        P("items", "frames"),
        P("items", "frames"),
        P("items", "frames"),
    )
    return jax.shard_map(
        partial(on_device, mesh), mesh=mesh, in_specs=in_specs, out_specs=out_specs, check_vma=False
    )
```

```python
import functools
from functools import partial

import jax
import jax.numpy as jnp
from jax import lax
from jax.experimental import pallas as pl
from jax.experimental.pallas import tpu as pltpu
from jax.sharding import PartitionSpec as P

H = 12


def norm_parts(tensor):
    centered = tensor - jnp.mean(tensor, -1, keepdims=True)
    inverse = lax.rsqrt(jnp.mean(centered * centered, -1, keepdims=True) + 1e-06)
    return (centered * inverse, inverse)


def norm_back(normed, inverse, incoming):
    return inverse * (
        incoming
        - jnp.mean(incoming, -1, keepdims=True)
        - normed * jnp.mean(incoming * normed, -1, keepdims=True)
    )


def split_heads(tensor):
    return tensor.reshape(tensor.shape[0], tensor.shape[1], H, -1)


def attend(queries, keys_in, values_in, key_valid, score_scale):
    scores = (
        jnp.einsum(
            "ifhd,ijhd->ihfj",
            split_heads(queries),
            split_heads(keys_in),
            preferred_element_type=jnp.float32,
        )
        * score_scale
    )
    scores = jnp.where(key_valid[:, None, None, :], scores, -1e30)
    attn_prob = jax.nn.softmax(scores, axis=-1)
    log_total = jax.nn.logsumexp(scores, axis=-1)
    low_prob = attn_prob.astype(jnp.bfloat16)
    mixed = jnp.einsum(
        "ihfj,ijhd->ifhd", low_prob, split_heads(values_in), preferred_element_type=jnp.float32
    )
    return (attn_prob, low_prob, mixed.astype(jnp.bfloat16).reshape(queries.shape), log_total)


def attend_back(grad_mixed, queries, keys_in, values_in, attn_prob, low_prob, score_scale):
    grad_heads = split_heads(grad_mixed)
    grad_prob = jnp.einsum(
        "ifhd,ijhd->ihfj", grad_heads, split_heads(values_in), preferred_element_type=jnp.float32
    )
    grad_values = jnp.einsum(
        "ihfj,ifhd->ijhd", low_prob, grad_heads, preferred_element_type=jnp.float32
    )
    grad_scores = (
        attn_prob * (grad_prob - jnp.sum(attn_prob * grad_prob, -1, keepdims=True))
    ).astype(jnp.bfloat16)
    grad_queries = (
        jnp.einsum(
            "ihfj,ijhd->ifhd", grad_scores, split_heads(keys_in), preferred_element_type=jnp.float32
        )
        * score_scale
    )
    grad_keys = (
        jnp.einsum(
            "ihfj,ifhd->ijhd", grad_scores, split_heads(queries), preferred_element_type=jnp.float32
        )
        * score_scale
    )
    return (
        grad_queries.reshape(queries.shape),
        grad_keys.reshape(keys_in.shape),
        grad_values.reshape(values_in.shape),
    )


def project(tensor, weight):
    return jnp.einsum("ifd,de->ife", tensor, weight, preferred_element_type=jnp.float32)


def project_back(tensor, weight):
    return jnp.einsum("ife,de->ifd", tensor, weight, preferred_element_type=jnp.float32)


def weight_grad(left, right):
    return jnp.einsum("ifd,ife->de", left, right, preferred_element_type=jnp.float32)


def frames_split(
    frames_in,
    cond,
    text,
    item_lengths,
    text_lengths,
    ada_weight,
    qkv_weight,
    out_weight,
    cross_q_weight,
    cross_kv_weight,
    cross_out_weight,
    up_weight,
    down_weight,
    cotangent,
):
    model_width = frames_in.shape[-1]
    score_scale = (model_width // H) ** (-0.5)
    cond_f = cond.astype(jnp.float32)
    low_cond = jax.nn.silu(cond_f).astype(jnp.bfloat16)
    modulation = jnp.dot(low_cond, ada_weight, preferred_element_type=jnp.float32)
    pieces = [
        modulation[:, None, position * model_width : (position + 1) * model_width]
        for position in range(9)
    ]
    shift_a, scale_a, gate_a, shift_b, scale_b, gate_b, shift_c, scale_c, gate_c = pieces
    residual_in = frames_in.astype(jnp.float32)
    normed_a, inverse_a = norm_parts(residual_in)
    hidden_a = (normed_a * (1.0 + scale_a) + shift_a).astype(jnp.bfloat16)
    qkv = project(hidden_a, qkv_weight).astype(jnp.bfloat16)
    queries = qkv[..., :model_width]
    keys_own = qkv[..., model_width : 2 * model_width]
    values_own = qkv[..., 2 * model_width :]
    keys_all, values_all = (
        lax.all_gather(keys_own, "frames", axis=1, tiled=True),
        lax.all_gather(values_own, "frames", axis=1, tiled=True),
    )
    key_valid = jnp.arange(keys_all.shape[1], dtype=jnp.int32)[None, :] < item_lengths[:, None]
    attn_prob, low_prob, attended, self_total = attend(
        queries, keys_all, values_all, key_valid, score_scale
    )
    branch_a = project(attended, out_weight)
    first = residual_in + gate_a * branch_a
    normed_b, inverse_b = norm_parts(first)
    hidden_b = (normed_b * (1.0 + scale_b) + shift_b).astype(jnp.bfloat16)
    cross_q = project(hidden_b, cross_q_weight).astype(jnp.bfloat16)
    text_own = project(text, cross_kv_weight).astype(jnp.bfloat16)
    text_kv = lax.all_gather(text_own, "frames", axis=1, tiled=True)
    text_keys = text_kv[..., :model_width]
    text_values = text_kv[..., model_width:]
    text_valid = jnp.arange(text_kv.shape[1], dtype=jnp.int32)[None, :] < text_lengths[:, None]
    cross_prob, cross_low, crossed, cross_total = attend(
        cross_q, text_keys, text_values, text_valid, score_scale
    )
    branch_b = project(crossed, cross_out_weight)
    second = first + gate_b * branch_b
    normed_c, inverse_c = norm_parts(second)
    hidden_c = (normed_c * (1.0 + scale_c) + shift_c).astype(jnp.bfloat16)
    up_proj = project(hidden_c, up_weight)
    activated, gelu_back = jax.vjp(partial(jax.nn.gelu, approximate=False), up_proj)
    low_act = activated.astype(jnp.bfloat16)
    branch_c = project(low_act, down_weight)
    layer_out = (second + gate_c * branch_c).astype(jnp.bfloat16)
    upstream = cotangent.astype(jnp.float32)
    d_gate_c = jnp.sum(upstream * branch_c, 1)
    d_branch_c = (upstream * gate_c).astype(jnp.bfloat16)
    grad_down = weight_grad(low_act, d_branch_c)
    d_up = gelu_back(project_back(d_branch_c, down_weight))[0].astype(jnp.bfloat16)
    grad_up = weight_grad(hidden_c, d_up)
    d_hidden_c = project_back(d_up, up_weight)
    d_shift_c = jnp.sum(d_hidden_c, 1)
    d_scale_c = jnp.sum(d_hidden_c * normed_c, 1)
    upstream = upstream + norm_back(normed_c, inverse_c, d_hidden_c * (1.0 + scale_c))
    d_gate_b = jnp.sum(upstream * branch_b, 1)
    d_branch_b = (upstream * gate_b).astype(jnp.bfloat16)
    grad_cross_out = weight_grad(crossed, d_branch_b)
    d_crossed = project_back(d_branch_b, cross_out_weight).astype(jnp.bfloat16)
    d_cross_q, d_text_keys, d_text_values = attend_back(
        d_crossed, cross_q, text_keys, text_values, cross_prob, cross_low, score_scale
    )
    d_cross_q = d_cross_q.astype(jnp.bfloat16)
    grad_cross_q = weight_grad(hidden_b, d_cross_q)
    d_hidden_b = project_back(d_cross_q, cross_q_weight)
    d_text_local = jnp.concatenate([d_text_keys, d_text_values], -1)
    d_shift_b = jnp.sum(d_hidden_b, 1)
    d_scale_b = jnp.sum(d_hidden_b * normed_b, 1)
    upstream = upstream + norm_back(normed_b, inverse_b, d_hidden_b * (1.0 + scale_b))
    d_gate_a = jnp.sum(upstream * branch_a, 1)
    d_branch_a = (upstream * gate_a).astype(jnp.bfloat16)
    grad_out = weight_grad(attended, d_branch_a)
    d_attended = project_back(d_branch_a, out_weight).astype(jnp.bfloat16)
    keys_back, values_back = (
        lax.all_gather(keys_own, "frames", axis=1, tiled=True),
        lax.all_gather(values_own, "frames", axis=1, tiled=True),
    )
    d_queries, d_keys_all, d_values_all = attend_back(
        d_attended, queries, keys_back, values_back, attn_prob, low_prob, score_scale
    )
    d_keys, d_values = (
        lax.psum_scatter(
            d_keys_all.astype(jnp.bfloat16), "frames", scatter_dimension=1, tiled=True
        ).astype(jnp.float32),
        lax.psum_scatter(
            d_values_all.astype(jnp.bfloat16), "frames", scatter_dimension=1, tiled=True
        ).astype(jnp.float32),
    )
    d_qkv = jnp.concatenate(
        [
            d_queries.astype(jnp.bfloat16),
            d_keys.astype(jnp.bfloat16),
            d_values.astype(jnp.bfloat16),
        ],
        -1,
    )
    grad_qkv = weight_grad(hidden_a, d_qkv)
    d_hidden_a = project_back(d_qkv, qkv_weight)
    d_shift_a = jnp.sum(d_hidden_a, 1)
    d_scale_a = jnp.sum(d_hidden_a * normed_a, 1)
    input_grad = upstream + norm_back(normed_a, inverse_a, d_hidden_a * (1.0 + scale_a))
    d_modulation = jnp.concatenate(
        [
            d_shift_a,
            d_scale_a,
            d_gate_a,
            d_shift_b,
            d_scale_b,
            d_gate_b,
            d_shift_c,
            d_scale_c,
            d_gate_c,
        ],
        -1,
    )
    grad_ada = jnp.dot(
        low_cond.astype(jnp.float32).T,
        d_modulation,
        precision=lax.Precision.HIGHEST,
        preferred_element_type=jnp.float32,
    )
    sigmoid_c = jax.nn.sigmoid(cond_f)
    cond_part = jnp.dot(
        d_modulation,
        ada_weight.T,
        precision=lax.Precision.HIGHEST,
        preferred_element_type=jnp.float32,
    ) * (sigmoid_c * (1.0 + cond_f * (1.0 - sigmoid_c)))
    d_text_kv, cond_grad = (
        lax.psum_scatter(d_text_local, "frames", scatter_dimension=1, tiled=True),
        lax.psum_scatter(cond_part, "frames", scatter_dimension=1, tiled=True),
    )
    low_text_kv = d_text_kv.astype(jnp.bfloat16)
    grad_cross_kv = weight_grad(text, low_text_kv)
    text_grad = project_back(low_text_kv, cross_kv_weight)
    grads = (
        grad_ada,
        grad_qkv,
        grad_out,
        grad_cross_q,
        grad_cross_kv,
        grad_cross_out,
        grad_up,
        grad_down,
    )
    partial_sums = (
        lax.psum_scatter(
            grads[0].astype(jnp.bfloat16), "frames", scatter_dimension=1, tiled=True
        ).astype(jnp.float32),
        lax.psum_scatter(
            grads[1].astype(jnp.bfloat16), "frames", scatter_dimension=1, tiled=True
        ).astype(jnp.float32),
        lax.psum_scatter(
            grads[2].astype(jnp.bfloat16), "frames", scatter_dimension=1, tiled=True
        ).astype(jnp.float32),
        lax.psum_scatter(
            grads[3].astype(jnp.bfloat16), "frames", scatter_dimension=1, tiled=True
        ).astype(jnp.float32),
        lax.psum_scatter(
            grads[4].astype(jnp.bfloat16), "frames", scatter_dimension=1, tiled=True
        ).astype(jnp.float32),
        lax.psum_scatter(
            grads[5].astype(jnp.bfloat16), "frames", scatter_dimension=1, tiled=True
        ).astype(jnp.float32),
        lax.psum_scatter(
            grads[6].astype(jnp.bfloat16), "frames", scatter_dimension=1, tiled=True
        ).astype(jnp.float32),
        lax.psum_scatter(
            grads[7].astype(jnp.bfloat16), "frames", scatter_dimension=1, tiled=True
        ).astype(jnp.float32),
    )
    totals = (
        lax.psum_scatter(
            partial_sums[0].astype(jnp.bfloat16), "items", scatter_dimension=0, tiled=True
        ).astype(jnp.float32),
        lax.psum_scatter(
            partial_sums[1].astype(jnp.bfloat16), "items", scatter_dimension=0, tiled=True
        ).astype(jnp.float32),
        lax.psum_scatter(
            partial_sums[2].astype(jnp.bfloat16), "items", scatter_dimension=0, tiled=True
        ).astype(jnp.float32),
        lax.psum_scatter(
            partial_sums[3].astype(jnp.bfloat16), "items", scatter_dimension=0, tiled=True
        ).astype(jnp.float32),
        lax.psum_scatter(
            partial_sums[4].astype(jnp.bfloat16), "items", scatter_dimension=0, tiled=True
        ).astype(jnp.float32),
        lax.psum_scatter(
            partial_sums[5].astype(jnp.bfloat16), "items", scatter_dimension=0, tiled=True
        ).astype(jnp.float32),
        lax.psum_scatter(
            partial_sums[6].astype(jnp.bfloat16), "items", scatter_dimension=0, tiled=True
        ).astype(jnp.float32),
        lax.psum_scatter(
            partial_sums[7].astype(jnp.bfloat16), "items", scatter_dimension=0, tiled=True
        ).astype(jnp.float32),
    )
    return (
        layer_out,
        input_grad,
        text_grad,
        cond_grad,
        totals[0],
        totals[1],
        totals[2],
        totals[3],
        totals[4],
        totals[5],
        totals[6],
        totals[7],
    )


LOG2E = 1.4426950408889634
BF = jnp.bfloat16
F32 = jnp.float32
PACK = 384
FIN = 2
SUB = 128
BSUB = 256
CSUB = 256
LIMIT = 127 * 2**19


def nn(left, right):
    return jnp.dot(left, right, preferred_element_type=F32)


def nt(left, right):
    return lax.dot_general(left, right, (((1,), (1,)), ((), ())), preferred_element_type=F32)


def tn(left, right):
    return lax.dot_general(left, right, (((0,), (0,)), ((), ())), preferred_element_type=F32)


def ln_parts(rows):
    share = 1.0 / rows.shape[-1]
    centered = rows - jnp.sum(rows, -1, keepdims=True) * share
    inverse = lax.rsqrt(jnp.sum(centered * centered, -1, keepdims=True) * share + 1e-06)
    return centered * inverse, inverse


def ln_back(normed, inverse, incoming):
    share = 1.0 / normed.shape[-1]
    mean_in = jnp.sum(incoming, -1, keepdims=True) * share
    mean_dot = jnp.sum(incoming * normed, -1, keepdims=True) * share
    return inverse * (incoming - mean_in - normed * mean_dot)


def gelu_parts(value):
    size = jnp.abs(value)
    inner = 1.0 / (1.0 + (0.3275911 * 0.7071067811865476) * size)
    series = inner * (
        0.5 * 0.254829592
        + inner
        * (
            0.5 * -0.284496736
            + inner * (0.5 * 1.421413741 + inner * (0.5 * -1.453152027 + inner * (0.5 * 1.061405429)))
        )
    )
    bell = jnp.exp2(value * value * (-0.5 * LOG2E))
    tail = series * bell
    below = jnp.where(value >= 0.0, 1.0 - tail, tail)
    return below, below + value * bell * 0.3989422804014327


def strips(body, *arrays, rows=16):
    made = [body(*(array[at : at + rows] for array in arrays)) for at in range(0, arrays[0].shape[0], rows)]
    if not isinstance(made[0], tuple):
        return jnp.concatenate(made, 0)
    return tuple(jnp.concatenate(column, 0) for column in zip(*made))


def fold(rows):
    return jnp.sum(rows.reshape(rows.shape[0] // 8, 8, rows.shape[1]), 0)


def modulate(rows, shift, scale):
    normed, _ = ln_parts(rows.astype(F32))
    return (normed * (1.0 + scale) + shift).astype(BF)


class Columns:
    def __init__(self, count):
        self.parts = [None] * count

    def add(self, at, rows):
        made = fold(rows)
        self.parts[at] = made if self.parts[at] is None else self.parts[at] + made

    def total(self, at):
        return jnp.sum(self.parts[at], 0, keepdims=True)


def lane_half(half):
    lane = lax.broadcasted_iota(jnp.int32, (1, 128), 1)
    return lane < 64 if half == 0 else lane >= 64


def keep_half(rows, half):
    return jnp.where(lane_half(half), rows, jnp.zeros_like(rows))


def pack_square(acc, item, ra, cb, col):
    first = acc[pl.ds(pl.multiple_of(item * ra, 16), ra // 2), col : col + cb]
    second = acc[pl.ds(pl.multiple_of(item * ra + ra // 2, 16), ra // 2), col : col + cb]
    return jnp.concatenate([first, second], 1).astype(BF)


def store_block(value, part, frame, me, row, keep_ref, send_ref):
    place = frame ^ me

    @pl.when(place & 1 == 0)
    def _():
        keep_ref[part, place >> 1, row : row + value.shape[0]] = value

    @pl.when(place & 1 == 1)
    def _():
        send_ref[part, place >> 1, row : row + value.shape[0]] = value


def start_kernel(where, lengths, text_lengths, table, *, items, nf):
    per = items // nf
    me = where[0]
    table[0] = me
    table[1] = where[1]
    at = 2 + 3 * per
    for i in range(items):
        rank = jnp.int32(0)
        for j in range(items):
            if j < i:
                ahead = lengths[j] >= lengths[i]
            elif j > i:
                ahead = lengths[j] > lengths[i]
            else:
                continue
            rank = rank + ahead.astype(jnp.int32)
        turn, seat = rank // nf, rank % nf
        device = jnp.where(turn % 2 == 0, seat, nf - 1 - seat)
        table[at + i] = device
        table[at + items + i] = turn
        table[at + 2 * items + device * per + turn] = i
    for slot in range(per):
        item = table[at + 2 * items + me * per + slot]
        table[2 + slot] = item
        table[2 + per + slot] = lengths[item]
        table[2 + 2 * per + slot] = text_lengths[item]


def gather_first_kernel(table, *refs):
    for to, source in enumerate(refs[:-1]):
        refs[-1][to] = source[0]


def gather_kernel(table, *refs, per):
    rows, texts, cots, mixed, cot = refs[0], refs[1 : 1 + per], refs[1 + per : 1 + 2 * per], refs[-2], refs[-1]
    block, short = rows.shape[1], texts[0].shape[1]
    mixed[0, :block] = rows[0]
    for slot in range(per):
        mixed[0, block + slot * short : block + (slot + 1) * short] = texts[slot][0]
        cot[0, slot] = cots[slot][0]


def gate_kernel(*refs):
    pass


def ahead(work, make, use):
    made = make(*work[0])
    for number, item in enumerate(work):
        later = make(*work[number + 1]) if number + 1 < len(work) else None
        use(item, made)
        made = later


def soften(scores):
    top = jnp.max(scores, 1, keepdims=True)
    return jnp.exp2(scores - top).astype(BF), top


def soft_back(scores, d_prob, lse, delta):
    prob = jnp.exp2(scores - lse)
    return prob.astype(BF), (prob * (d_prob - delta)).astype(BF)


def self_fwd_kernel(
    table, x_ref, mod_ref, w_ref, *refs, blocks, qb, score_scale, length_at
):
    rows_ref, qkv_ref, att_ref, lse_ref, held = refs[-5:]
    step = pl.program_id(0)
    width = rows_ref.shape[-1]
    count = att_ref.shape[1]
    block = rows_ref.shape[1]
    pairs = H // 2

    @pl.when(step < blocks)
    def _():
        rows_ref[0] = x_ref[0]
        shift, scale = mod_ref[0, 0:1], mod_ref[0, 1:2]
        hidden = strips(lambda rows: modulate(rows, shift, scale), x_ref[0])
        at = pl.ds(pl.multiple_of(step * block, block), block)
        for part in range(3):
            made = nn(hidden, w_ref[:, part * width : (part + 1) * width])
            if part == 0:
                made = made * (score_scale * LOG2E)
            made = made.astype(BF)
            qkv_ref[0, :, part * width : (part + 1) * width] = made
            for pair in range(pairs):
                held[part * pairs + pair, at] = made[:, pair * 128 : pair * 128 + 128]

    for klen in (count // 4, count // 2, count):

        @pl.when((step >= blocks) & (table[length_at] == klen))
        def _(klen=klen):
            pair = step - blocks
            keys = held[pairs + pair, :klen]
            values = jnp.concatenate([held[2 * pairs + pair, :klen], jnp.ones((klen, 128), BF)], 1)

            def inner(position, carry):
                rows = pl.ds(pl.multiple_of(position * qb, qb), qb)
                queries = held[pair, rows]
                work = [(half, at) for at in range(0, qb, SUB) for half in (0, 1)]
                outs = [[], []]

                def score(half, at):
                    return nt(keep_half(queries[at : at + SUB], half), keys)

                def use(place, scores):
                    half, at = place
                    prob, top = strips(soften, scores)
                    mixed = nn(prob, values)
                    total = mixed[:, 128:]
                    cols = pl.ds(pl.multiple_of(position * qb + at, SUB), SUB)
                    lse_ref[0, 0, half : half + 1, cols] = (top + jnp.log2(total[:, :1])).T
                    outs[half].append(mixed[:, :128] / total)

                ahead(work, score, use)
                outs = [jnp.concatenate(out, 0) for out in outs]
                att_ref[0, rows] = jnp.where(lane_half(0), outs[0], outs[1]).astype(BF)
                return carry

            lax.fori_loop(0, count // qb, inner, 0)


def self_bwd_kernel(
    table, q_ref, k_ref, v_ref, o_ref, do_ref, lse_ref, x_ref, g1_ref, mod_ref, w_ref, *refs,
    slot, length_at, pairs, blocks, qb, score_scale, nf, ni, last,
):
    if last:
        d_early, x_early, mod_early, dx_ref, dmod_ref, keep_ref, send_ref, held, dk_acc, dv_acc, acc = refs
    else:
        text_ref, dx_ref, dmod_ref, d_out, held, dk_acc, dv_acc = refs
    step = pl.program_id(0)
    count = q_ref.shape[1]
    width = x_ref.shape[-1]
    block = x_ref.shape[1]
    used = table[length_at]
    for klen in (count // 4, count // 2, count):

        @pl.when((step < pairs) & (used == klen))
        def _(klen=klen):
            keys = k_ref[0, :klen]
            values = v_ref[0, :klen]
            dk_acc[:klen] = jnp.zeros((klen, 128), F32)
            dv_acc[:klen] = jnp.zeros((klen, 128), F32)

            def inner(position, carry):
                rows = pl.ds(pl.multiple_of(position * qb, qb), qb)
                queries = q_ref[0, rows]
                grad = do_ref[0, rows]
                dots = (grad.astype(F32) * o_ref[0, rows].astype(F32)).T
                d_queries = [[], []]
                work = [(half, at) for at in range(0, qb, BSUB) for half in (0, 1)]

                def score(half, at):
                    q_half = keep_half(queries[at : at + BSUB], half)
                    grad_half = keep_half(grad[at : at + BSUB], half)
                    return q_half, grad_half, nt(keys, q_half), nt(values, grad_half)

                def use(place, made):
                    half, at = place
                    q_half, grad_half, scores, d_prob = made
                    delta = jnp.sum(dots[64 * half : 64 * half + 64, at : at + BSUB], 0, keepdims=True)
                    cols = pl.ds(pl.multiple_of(position * qb + at, BSUB), BSUB)
                    lse = lse_ref[0, 0, half : half + 1, cols]
                    prob, d_scores = strips(partial(soft_back, lse=lse, delta=delta), scores, d_prob)
                    dv_acc[:klen] += nn(prob, grad_half)
                    dk_acc[:klen] += nn(d_scores, q_half)
                    d_queries[half].append(tn(d_scores, keys))

                ahead(work, score, use)
                d_queries = [jnp.concatenate(part, 0) for part in d_queries]
                held[step, rows] = (jnp.where(lane_half(0), d_queries[0], d_queries[1]) * score_scale).astype(BF)
                return carry

            lax.fori_loop(0, count // qb, inner, 0)
            held[pairs + step, :klen] = (dk_acc[:klen] * (1.0 / LOG2E)).astype(BF)
            held[2 * pairs + step, :klen] = dv_acc[:klen].astype(BF)
            if klen < count:
                held[pairs + step, klen:] = jnp.zeros((count - klen, 128), BF)
                held[2 * pairs + step, klen:] = jnp.zeros((count - klen, 128), BF)

    @pl.when(step == pairs)
    def _():
        dmod_ref[...] = jnp.zeros_like(dmod_ref)
        if last:
            acc[...] = jnp.zeros_like(acc)

    @pl.when((step >= pairs) & (step < pairs + blocks))
    def _():
        rows = pl.ds(pl.multiple_of((step - pairs) * block, block), block)
        d_qkv = jnp.concatenate([held[at, rows] for at in range(3 * pairs)], 1)
        shift, scale = mod_ref[0, 0:1], mod_ref[0, 1:2]
        d_hidden = nt(d_qkv, w_ref[...])
        sums = Columns(2)

        def leave(x, dh, upstream):
            normed, inverse = ln_parts(x.astype(F32))
            sums.add(0, dh)
            sums.add(1, dh * normed)
            out = upstream.astype(F32) + ln_back(normed, inverse, dh * (1.0 + scale))
            return out.astype(BF), (normed * (1.0 + scale) + shift).astype(BF)

        dx_ref[0, :block], hidden = strips(leave, x_ref[0], d_hidden, g1_ref[0])
        for at in range(2):
            dmod_ref[0, at : at + 1] += sums.total(at)
        if last:
            acc[...] += tn(hidden, d_qkv)
        else:
            d_out[...] = d_qkv
            short = text_ref.shape[2]
            for part in range(text_ref.shape[1]):
                dx_ref[0, block + part * short : block + (part + 1) * short] = text_ref[0, part]

    if last:

        @pl.when((step >= pairs + blocks) & (step < pairs + 2 * blocks))
        def _():
            shift, scale = mod_early[0, 0:1], mod_early[0, 1:2]
            hidden = strips(lambda rows: modulate(rows, shift, scale), x_early[0])
            acc[...] += tn(hidden, d_early[...])

        @pl.when(step >= pairs + 2 * blocks)
        def _():
            ra, cb = width // ni, 3 * width // nf
            for part in range(FIN):
                item = ((step - pairs - 2 * blocks) * FIN + part) ^ table[1]
                for frame in range(nf):
                    cut = acc[pl.ds(pl.multiple_of(item * ra, 16), ra), frame * cb : (frame + 1) * cb].astype(BF)
                    rest = jnp.concatenate([cut[: ra // 2, PACK:], cut[ra // 2 :, PACK:]], 1)
                    store_block(
                        jnp.concatenate([cut[:, :PACK], rest], 0), part, frame, table[0], 0, keep_ref, send_ref
                    )


def cross_kernel(
    table, att_ref, x_ref, mod_ref, text_ref, wkv_ref, wo_ref, wq_ref, wco_ref,
    kv_ref, text_rows, first_ref, second_ref, ba_ref, bb_ref, cq_ref, cr_ref, lse_ref, *, score_scale, length_at,
):
    width = x_ref.shape[-1]
    slots = kv_ref.shape[1]
    used = table[length_at + pl.program_id(0)]

    @pl.when(pl.program_id(1) == 0)
    def _():
        text_rows[0] = jnp.concatenate([text_ref[at] for at in range(text_ref.shape[0])], 0)
        kv_ref[0] = nn(text_rows[0], wkv_ref[...]).astype(BF)

    branch_a = nn(att_ref[0], wo_ref[...])
    gate_a, gate_b, shift, scale = mod_ref[0, 2:3], mod_ref[0, 5:6], mod_ref[0, 3:4], mod_ref[0, 4:5]

    def enter(rows, branch):
        first = rows.astype(F32) + gate_a * branch
        return branch.astype(BF), first, modulate(first, shift, scale)

    ba_ref[0], first, hidden = strips(enter, x_ref[0], branch_a)
    first_ref[0] = first.astype(BF)
    cq_ref[0] = (nn(hidden, wq_ref[...]) * (score_scale * LOG2E)).astype(BF)
    valid = lax.broadcasted_iota(jnp.int32, (1, slots), 1) < used
    ones = jnp.ones((slots, 128), BF)
    count = cq_ref.shape[1]
    outs = {}

    def score(pair, half, at):
        cols = slice(pair * 128, pair * 128 + 128)
        return nt(keep_half(cq_ref[0, at : at + CSUB, cols], half), kv_ref[0, :, cols])

    def use(place, scores):
        pair, half, at = place
        prob, top = strips(lambda part: soften(jnp.where(valid, part, -1e30)), scores)
        values = kv_ref[0, :, width + pair * 128 : width + pair * 128 + 128]
        mixed = nn(prob, jnp.concatenate([values, ones], 1))
        total = mixed[:, 128:]
        lse_ref[0, pair, half : half + 1, at : at + CSUB] = (top + jnp.log2(total[:, :1])).T
        outs[half] = mixed[:, :128] / total
        if half == 1:
            cr_ref[0, at : at + CSUB, pair * 128 : pair * 128 + 128] = jnp.where(
                lane_half(0), outs[0], outs[1]
            ).astype(BF)

    work = [(pair, half, at) for pair in range(H // 2) for at in range(0, count, CSUB) for half in (0, 1)]
    ahead(work, score, use)
    branch_b = nn(cr_ref[0], wco_ref[...])
    bb_ref[0], second_ref[0] = strips(
        lambda rows, branch: (branch.astype(BF), (rows + gate_b * branch).astype(BF)), first, branch_b
    )


def mlp_kernel(
    table, second_ref, cot_ref, mod_ref, wup_ref, wdn_ref,
    out_ref, g2_ref, dmod_ref, gw_ref, up_acc, dn_acc, *, blocks, total, chunk, nf, ni,
):
    step = pl.program_id(0)
    width = second_ref.shape[-1]
    ff = wup_ref.shape[-1]

    @pl.when(step == 0)
    def _():
        up_acc[...] = jnp.zeros_like(up_acc)
        dn_acc[...] = jnp.zeros_like(dn_acc)

    @pl.when(step < total)
    def _():
        shift, scale, gate = mod_ref[0, 6:7], mod_ref[0, 7:8], mod_ref[0, 8:9]
        hidden = strips(lambda rows: modulate(rows, shift, scale), second_ref[0])
        cot = jnp.concatenate([cot_ref[at, 0] for at in range(cot_ref.shape[0])], 0)
        d_branch = strips(lambda rows: (rows.astype(F32) * gate).astype(BF), cot)
        def middle(up_proj, d_act):
            below, slope = gelu_parts(up_proj)
            return (up_proj * below).astype(BF), (d_act * slope).astype(BF)

        third = chunk // 3
        span = width // 3
        count = ff // chunk
        made, done = {}, {}
        branches = [jnp.zeros((second_ref.shape[1], span), F32)] * 3
        d_hiddens = [jnp.zeros((second_ref.shape[1], span), F32)] * 3
        for at in range(count + 2):
            for part in range(3):
                sub = slice(part * span, (part + 1) * span)
                if at < count:
                    cols = slice(at * chunk + part * third, at * chunk + (part + 1) * third)
                    made[at, part] = nn(hidden, wup_ref[:, cols]), nt(d_branch, wdn_ref[cols])
                if 1 <= at <= count:
                    done[at - 1, part] = strips(middle, *made.pop((at - 1, part)))
                if at >= 2:
                    cols = slice((at - 2) * chunk, (at - 1) * chunk)
                    act, d_up = (jnp.concatenate([done[at - 2, p][side] for p in range(3)], 1) for side in (0, 1))
                    branches[part] += nn(act, wdn_ref[cols, sub])
                    d_hiddens[part] += nt(d_up, wup_ref[sub, cols])
                    cols = slice((at - 2) * chunk + part * third, (at - 2) * chunk + (part + 1) * third)
                    dn_acc[cols] += tn(done[at - 2, part][0], d_branch)
                    up_acc[:, cols] += tn(hidden, done[at - 2, part][1])
        branch, d_hidden = jnp.concatenate(branches, 1), jnp.concatenate(d_hiddens, 1)

        @pl.when(step % blocks == 0)
        def _():
            dmod_ref[...] = jnp.zeros_like(dmod_ref)

        sums = Columns(3)

        def leave(second, cot, branch_rows, dh):
            second = second.astype(F32)
            normed, inverse = ln_parts(second)
            upstream = cot.astype(F32)
            sums.add(0, dh)
            sums.add(1, dh * normed)
            sums.add(2, upstream * branch_rows)
            upstream = upstream + ln_back(normed, inverse, dh * (1.0 + scale))
            return (second + gate * branch_rows).astype(BF), upstream.astype(BF)

        out, g2_ref[0] = strips(leave, second_ref[0], cot, branch, d_hidden)
        rows = out_ref.shape[2]
        for at in range(out_ref.shape[0]):
            out_ref[at, 0] = out[at * rows : (at + 1) * rows]
        for at in range(3):
            dmod_ref[0, at : at + 1] += sums.total(at)

    @pl.when(step >= total)
    def _():
        ra, cb = width // ni, ff // nf
        for part in range(FIN):
            item = (step - total) * FIN + part
            for frame in range(nf):
                cut = up_acc[pl.ds(pl.multiple_of(item * ra, 16), ra), frame * cb : (frame + 1) * cb].astype(BF)
                gw_ref[part, frame, :ra] = cut[:, :PACK]
                gw_ref[part, frame, ra : 2 * ra] = cut[:, PACK:]
                gw_ref[part, frame, 2 * ra :] = pack_square(
                    dn_acc, item, ff // ni, width // nf, frame * (width // nf)
                )


def cross_back_kernel(
    table, g2_ref, bb_ref, cr_ref, cq_ref, att_ref, ba_ref, first_ref, mod_ref, kv_ref, lse_ref, text_ref,
    wo_ref, wq_ref, wco_ref, wkv_ref, _,
    g1_ref, datt_ref, text_out, dmod_ref, all_ref,
    o_acc, q_acc, co_acc, kv_acc, dtext, staged, sems, *, blocks, total, score_scale, nf, ni, length_at,
):
    step = pl.program_id(0)
    width = g2_ref.shape[-1]
    slots = kv_ref.shape[1]

    @pl.when(step == 0)
    def _():
        o_acc[...] = jnp.zeros_like(o_acc)
        q_acc[...] = jnp.zeros_like(q_acc)
        co_acc[...] = jnp.zeros_like(co_acc)
        kv_acc[...] = jnp.zeros_like(kv_acc)

    @pl.when(step < total)
    def _():
        @pl.when(step % blocks == 0)
        def _():
            dmod_ref[...] = jnp.zeros_like(dmod_ref)
            dtext[...] = jnp.zeros_like(dtext)

        used = table[length_at + step // blocks]
        gate_b = mod_ref[0, 5:6]
        sums = Columns(4)

        def enter(upstream, branch):
            upstream = upstream.astype(F32)
            sums.add(3, upstream * branch.astype(F32))
            return (upstream * gate_b).astype(BF)

        d_branch_b = strips(enter, g2_ref[0], bb_ref[0])
        co_acc[...] += tn(cr_ref[0], d_branch_b)
        d_crossed = nt(d_branch_b, wco_ref[...])
        slot_of = lax.broadcasted_iota(jnp.int32, (slots, 1), 0)
        parts = []
        kept = {}

        def score(pair, half):
            cols = slice(pair * 128, pair * 128 + 128)
            vcols = slice(width + pair * 128, width + pair * 128 + 128)
            grad = d_crossed[:, cols].astype(BF)
            q_half = keep_half(cq_ref[0, :, cols], half)
            grad_half = keep_half(grad, half)
            return grad, q_half, grad_half, nt(kv_ref[0, :, cols], q_half), nt(kv_ref[0, :, vcols], grad_half)

        def use(place, made):
            pair, half = place
            grad, q_half, grad_half, scores, d_prob = made
            cols = slice(pair * 128, pair * 128 + 128)
            vcols = slice(width + pair * 128, width + pair * 128 + 128)
            if half == 0:
                kept["dots"] = (grad.astype(F32) * cr_ref[0, :, cols].astype(F32)).T
            delta = jnp.sum(kept["dots"][64 * half : 64 * half + 64], 0, keepdims=True)
            lse = lse_ref[0, pair, half : half + 1]

            def back(part, d_part, at):
                return soft_back(jnp.where(at < used, part, -1e30), d_part, lse, delta)

            prob, d_scores = strips(back, scores, d_prob, slot_of)
            d_values = nn(prob, grad_half)
            d_keys = nn(d_scores, q_half)
            d_query = tn(d_scores, kv_ref[0, :, cols])
            if half == 0:
                kept["sums"] = d_keys, d_values, d_query
                return
            first_keys, first_values, first_query = kept["sums"]
            dtext[:, cols] += (first_keys + d_keys) * (1.0 / LOG2E)
            dtext[:, vcols] += first_values + d_values
            parts.append((jnp.where(lane_half(0), first_query, d_query) * score_scale).astype(BF))

        ahead([(pair, half) for pair in range(H // 2) for half in (0, 1)], score, use)
        d_cq = jnp.concatenate(parts, 1)
        shift, scale, gate = mod_ref[0, 3:4], mod_ref[0, 4:5], mod_ref[0, 2:3]
        d_hidden = nt(d_cq, wq_ref[...])

        def leave(first, dh, upstream, branch):
            normed, inverse = ln_parts(first.astype(F32))
            sums.add(1, dh)
            sums.add(2, dh * normed)
            upstream = upstream.astype(F32) + ln_back(normed, inverse, dh * (1.0 + scale))
            sums.add(0, upstream * branch.astype(F32))
            return (normed * (1.0 + scale) + shift).astype(BF), upstream.astype(BF), (upstream * gate).astype(BF)

        hidden, g1_ref[0], d_branch_a = strips(leave, first_ref[0], d_hidden, g2_ref[0], ba_ref[0])
        for at in range(4):
            dmod_ref[0, at : at + 1] += sums.total(at)
        datt_ref[0] = nt(d_branch_a, wo_ref[...]).astype(BF)
        q_acc[...] += tn(hidden, d_cq)
        o_acc[...] += tn(att_ref[0], d_branch_a)

        @pl.when(step % blocks == blocks - 1)
        def _():
            low = dtext[...].astype(BF)
            kv_acc[...] += tn(text_ref[0], low)
            made = nt(low, wkv_ref[...]).astype(BF)
            short = text_out.shape[2]
            for frame in range(nf):
                text_out[frame, 0] = made[frame * short : (frame + 1) * short]

    @pl.when(step >= total)
    def _():
        ra, cb = width // ni, width // nf
        half = ra // 2
        depth = staged.shape[3]
        number = step - total
        side = number % 2

        def moved(at):
            place = pl.ds(at * FIN, FIN)
            return pltpu.make_async_copy(
                staged.at[at % 2], all_ref.at[place, :, pl.ds(all_ref.shape[2] - depth, depth)], sems.at[at % 2]
            )

        @pl.when(number >= 2)
        def _():
            moved(number - 2).wait()

        for part in range(FIN):
            item = number * FIN + part
            for frame in range(nf):
                for place, acc in enumerate((o_acc, q_acc, co_acc)):
                    cut = pack_square(acc, item, ra, cb, frame * cb)
                    staged[side, part, frame, place * half : (place + 1) * half] = cut
                cut = kv_acc[pl.ds(pl.multiple_of(item * ra, 16), ra), 2 * frame * cb : 2 * (frame + 1) * cb]
                staged[side, part, frame, 3 * half :] = cut.astype(BF)
        moved(number).start()

        @pl.when(number == ni // FIN - 1)
        def _():
            moved(number - 1).wait()
            moved(number).wait()


def deal_kernel(table, *refs, at, items, group):
    out_ref = refs[-1]
    count = (len(refs) - 1) // group
    for part in range(group):
        sources = refs[part * count : (part + 1) * count]
        if count == 1:
            out_ref[part] = sources[0][0, 0].astype(out_ref.dtype)
            continue
        slot_of = table[at + items + pl.program_id(0) * group + part]
        for slot, ref in enumerate(sources):

            @pl.when(slot_of == slot)
            def _(ref=ref, part=part):
                out_ref[part] = ref[0, 0].astype(out_ref.dtype)


def land_kernel(keep, got, *refs):
    outs = refs[-2:]
    for half, out in enumerate(outs):
        out[...] = (keep[0, half].astype(F32) + got[0, half].astype(F32)).astype(BF)[None]


def finish_kernel(sum_ref, *refs):
    up, down, squares, kv = refs[-6], refs[-5], refs[-4:-1], refs[-1]
    ra, cb = up.shape
    up[:, : cb // 2] = sum_ref[:ra].astype(F32)
    up[:, cb // 2 :] = sum_ref[ra : 2 * ra].astype(F32)
    at = 2 * ra + down.shape[1] // 2
    down[...] = untall(sum_ref[2 * ra : at].astype(F32)).T
    half = ra // 2
    for out in squares:
        out[...] = untall(sum_ref[at : at + half].astype(F32))
        at += half
    kv[...] = sum_ref[at:].astype(F32)


def finish_qkv_kernel(keep, got, *refs):
    out = refs[-1]
    ra = out.shape[0]
    total = keep[...].astype(F32) + got[...].astype(F32)
    out[:, :PACK] = total[:ra]
    out[:, PACK:] = untall(total[ra:])


def untall(block):
    half = block.shape[1] // 2
    return jnp.concatenate([block[:, :half], block[:, half:]], 0)


def cost(flops, moved, exps=0):
    return pl.CostEstimate(flops=int(flops), bytes_accessed=int(moved), transcendentals=int(exps))


def params():
    return pltpu.CompilerParams(vmem_limit_bytes=LIMIT)


def whole(shape):
    return pl.BlockSpec(shape, lambda *_: (0,) * len(shape), pipeline_mode=pl.Buffered(1))


def run(kernel, name, grid, in_specs, args, out_specs, out_shape, scratch=(), deps=(), work=None, aliases=None):
    inputs = len(args)

    def body(*refs):
        kernel(*refs[:inputs], *refs[inputs + len(deps) :])

    return pl.pallas_call(
        body,
        grid_spec=pltpu.PrefetchScalarGridSpec(
            num_scalar_prefetch=1,
            grid=grid,
            in_specs=list(in_specs) + [pl.BlockSpec(memory_space=pl.ANY)] * len(deps),
            out_specs=out_specs,
            scratch_shapes=list(scratch),
        ),
        out_shape=out_shape,
        input_output_aliases=aliases or {},
        compiler_params=params(),
        cost_estimate=work,
        name=name,
    )(*args, *deps)


def any_spec(count):
    return [pl.BlockSpec(memory_space=pl.ANY)] * count


def struct(shape, dtype):
    return jax.ShapeDtypeStruct(shape, dtype)


def start_call(where, lengths, text_lengths, items, nf):
    size = 2 + 3 * (items // nf) + 3 * items
    smem = pl.BlockSpec(memory_space=pltpu.SMEM)
    return pl.pallas_call(
        partial(start_kernel, items=items, nf=nf),
        in_specs=[smem] * 3,
        out_specs=smem,
        out_shape=struct((size,), jnp.int32),
        name="start",
    )(where, lengths, text_lengths)


def gather_first_call(table, rows, nf):
    items, block, width = rows.shape
    per = items // nf
    at = 2 + 3 * per + 2 * items
    return run(
        gather_first_kernel,
        "gather_first",
        (1,),
        [pl.BlockSpec((1, block, width), lambda t, s, to=to: (s[at + to * per], 0, 0)) for to in range(nf)],
        (table,) + (rows,) * nf,
        pl.BlockSpec((nf, block, width), lambda t, s: (0, 0, 0)),
        struct((nf, block, width), BF),
    )


def gather_call(table, rows, text, cot, nf):
    items, block, width = rows.shape
    per = items // nf
    at = 2 + 3 * per + 2 * items
    short = text.shape[1]

    def source(size, slot):
        return pl.BlockSpec((1, size, width), lambda t, s: (s[at + t * per + slot], 0, 0))

    return run(
        partial(gather_kernel, per=per),
        "gather",
        (nf,),
        [source(block, 1)] + [source(short, slot) for slot in range(per)] + [source(block, slot) for slot in range(per)],
        (table, rows) + (text,) * per + (cot,) * per,
        [
            pl.BlockSpec((1, block + per * short, width), lambda t, s: (t, 0, 0)),
            pl.BlockSpec((1, per, block, width), lambda t, s: (t, 0, 0, 0)),
        ],
        [struct((nf, block + per * short, width), BF), struct((nf, per, block, width), BF)],
    )


def gate_call(arrays, deps):
    return pl.pallas_call(
        gate_kernel,
        in_specs=any_spec(len(arrays) + len(deps)),
        out_specs=any_spec(len(arrays)),
        out_shape=[struct(array.shape, array.dtype) for array in arrays],
        input_output_aliases={at: at for at in range(len(arrays))},
        compiler_params=params(),
        name="gate",
    )(*arrays, *deps)


def halves(ni, nf, depth, total):
    spec = pl.BlockSpec((FIN, nf // 2, depth, PACK), lambda t, s: (jnp.maximum(t - total, 0), 0, 0, 0))
    return [spec] * 2, [struct((ni, nf // 2, depth, PACK), BF)] * 2


def self_fwd_call(table, slot, rows, mod, weight, kept, per, block, qb, score_scale, deps):
    blocks, _, width = rows.shape
    count = blocks * block
    pairs = H // 2

    def early(t):
        return jnp.minimum(t, blocks - 1)

    def late(t):
        return jnp.maximum(t - blocks, 0)

    return run(
        partial(self_fwd_kernel, blocks=blocks, qb=qb, score_scale=score_scale, length_at=2 + per + slot),
        "self_fwd",
        (blocks + pairs,),
        [pl.BlockSpec((1, block, width), lambda t, s: (early(t), 0, 0))]
        + [pl.BlockSpec((1, 9, width), lambda t, s: (slot, 0, 0)), whole(weight.shape)]
        + any_spec(len(kept)),
        (table, rows, mod, weight, *kept),
        [
            pl.BlockSpec((1, block, width), lambda t, s: (slot, early(t), 0)),
            pl.BlockSpec((1, block, 3 * width), lambda t, s: (slot, early(t), 0)),
            pl.BlockSpec((1, count, 128), lambda t, s: (slot, 0, late(t))),
            pl.BlockSpec((1, 1, 2, count), lambda t, s: (slot, late(t), 0, 0)),
        ],
        [
            struct((per, count, width), BF),
            struct((per, count, 3 * width), BF),
            struct((per, count, width), BF),
            struct((per, pairs, 2, count), F32),
        ],
        scratch=[pltpu.VMEM((3 * pairs, count, 128), BF)],
        deps=deps,
        work=cost(6 * count * width * width + 16 * count * count * width, count * width * 16, H * count * count),
        aliases={4 + at: at for at in range(len(kept))},
    )


def self_bwd_call(
    table, slot, qkv, att, d_att, lse, rows, g1, mod, weight, early, text, qb, score_scale, block, nf, ni, deps
):
    per, count, width = att.shape
    pairs = H // 2
    blocks = count // block
    last = early is not None
    steps = pairs + blocks
    lines = block if last else block + text.shape[1] * text.shape[2]

    def pair(t):
        return jnp.minimum(t, pairs - 1)

    def row(t):
        return jnp.clip(t - pairs, 0, blocks - 1)

    def row_early(t):
        return jnp.clip(t - pairs - blocks, 0, blocks - 1)

    column = pl.BlockSpec((1, count, 128), lambda t, s: (slot, 0, pair(t)))
    by_row = pl.BlockSpec((1, block, width), lambda t, s: (slot, row(t), 0))
    in_specs = [
        pl.BlockSpec((1, count, 128), lambda t, s, part=part: (slot, 0, part * pairs + pair(t))) for part in range(3)
    ] + [column, column, pl.BlockSpec((1, 1, 2, count), lambda t, s: (slot, pair(t), 0, 0))]
    in_specs += [by_row, by_row, pl.BlockSpec((1, 9, width), lambda t, s: (slot, 0, 0)), whole(weight.shape)]
    args = [table, qkv, qkv, qkv, att, d_att, lse, rows, g1, mod, weight]
    out_specs = [
        pl.BlockSpec((1, lines, width), lambda t, s: (row(t), 0, 0)),
        pl.BlockSpec((1, 2, width), lambda t, s: (0, 0, 0)),
    ]
    out_shape = [struct((blocks, lines, width), BF), struct((1, 2, width), F32)]
    scratch = [pltpu.VMEM((3 * pairs, count, 128), BF)] + [pltpu.VMEM((count, 128), F32)] * 2
    if last:
        in_specs += [
            pl.BlockSpec((block, 3 * width), lambda t, s: (row_early(t), 0)),
            pl.BlockSpec((1, block, width), lambda t, s: (slot - 1, row_early(t), 0)),
            pl.BlockSpec((1, 9, width), lambda t, s: (slot - 1, 0, 0)),
        ]
        args += [early, rows, mod]
        specs, shapes = halves(ni, nf, 3 * width * width // (nf * ni * PACK), steps + blocks)
        out_specs += specs
        out_shape += shapes
        scratch += [pltpu.VMEM((width, 3 * width), F32)]
        steps += blocks + ni // FIN
    else:
        in_specs += [pl.BlockSpec((1,) + text.shape[1:], lambda t, s: (row(t), 0, 0, 0))]
        args += [text]
        out_specs += [pl.BlockSpec((block, 3 * width), lambda t, s: (row(t), 0))]
        out_shape += [struct((count, 3 * width), BF)]
    return run(
        partial(
            self_bwd_kernel,
            slot=slot,
            length_at=2 + per + slot,
            pairs=pairs,
            blocks=blocks,
            qb=qb,
            score_scale=score_scale,
            nf=nf,
            ni=ni,
            last=last,
        ),
        "self_bwd",
        (steps,),
        in_specs,
        args,
        out_specs,
        out_shape,
        scratch=scratch,
        deps=deps,
        work=cost(40 * count * count * width + 12 * count * width * width, count * width * 30, H * count * count),
    )


def cross_call(table, att, rows, mod, text, short, wkv, wo, wq, wco, score_scale, block, deps):
    items, count, width = rows.shape
    nf, lines, _ = text.shape
    skip = lines // short - items
    slots = nf * short
    row = pl.BlockSpec((1, block, width), lambda i, j, s: (i, j, 0))
    return run(
        partial(cross_kernel, score_scale=score_scale, length_at=2 + 2 * items),
        "cross_fwd",
        (items, count // block),
        [
            row,
            row,
            pl.BlockSpec((1, 9, width), lambda i, j, s: (i, 0, 0)),
            pl.BlockSpec((nf, short, width), lambda i, j, s: (0, skip + i, 0)),
            whole(wkv.shape),
            whole(wo.shape),
            whole(wq.shape),
            whole(wco.shape),
        ],
        (table, att, rows, mod, text, wkv, wo, wq, wco),
        [pl.BlockSpec((1, slots, 2 * width), lambda i, j, s: (i, 0, 0))]
        + [pl.BlockSpec((1, slots, width), lambda i, j, s: (i, 0, 0))]
        + [row] * 6
        + [pl.BlockSpec((1, H // 2, 2, block), lambda i, j, s: (i, 0, 0, j))],
        [struct((items, slots, 2 * width), BF), struct((items, slots, width), BF)]
        + [struct(rows.shape, BF)] * 6
        + [struct((items, H // 2, 2, count), F32)],
        deps=deps,
        work=cost(
            items * count * (6 * width * width + 16 * slots * width), items * count * width * 20, items * H * count * slots
        ),
    )


def back_grid(items, count, block):
    blocks = count // block
    total = items * blocks

    def at(t):
        return jnp.minimum(t, total - 1)

    def by_item(t, s):
        return (at(t) // blocks, 0, 0)

    def by_row(t, s):
        return (at(t) // blocks, at(t) % blocks, 0)

    return blocks, total, by_item, by_row


def mlp_call(table, second, cot, mod, wup, wdn, block, chunk, nf, ni, deps):
    items, count, width = second.shape
    ff = wup.shape[1]
    blocks, total, by_item, by_row = back_grid(items, count, block)
    row = pl.BlockSpec((1, block, width), by_row)
    shard = pl.BlockSpec(
        (block // cot.shape[2], 1, cot.shape[2], width), lambda t, s: (by_row(t, s)[1], by_row(t, s)[0], 0, 0)
    )
    depth = 2 * width * ff // (nf * ni * PACK)
    return run(
        partial(mlp_kernel, blocks=blocks, total=total, chunk=chunk, nf=nf, ni=ni),
        "mlp",
        (total + ni // FIN,),
        [row, shard, pl.BlockSpec((1, 9, width), by_item), whole(wup.shape), whole(wdn.shape)],
        (table, second, cot, mod, wup, wdn),
        [shard, row, pl.BlockSpec((1, 3, width), by_item)]
        + [pl.BlockSpec((FIN, nf, depth, PACK), lambda t, s: (jnp.maximum(t - total, 0), 0, 0, 0))],
        [struct(cot.shape, BF), struct(second.shape, BF), struct((items, 3, width), F32)]
        + [struct((ni, nf, depth + 5 * width * width // (nf * ni * PACK), PACK), BF)],
        scratch=[pltpu.VMEM((width, ff), F32), pltpu.VMEM((ff, width), F32)],
        deps=deps,
        work=cost(12 * items * count * width * ff, items * count * width * 16, items * count * ff * 2),
    )


def cross_back_call(
    table, g2, bb, cr, cq, att, ba, first, mod, kv, lse, text, wo, wq, wco, wkv, blocks_all, score_scale, block, nf, ni, deps
):
    items, count, width = g2.shape
    slots = kv.shape[1]
    short = slots // nf
    blocks, total, by_item, by_row = back_grid(items, count, block)
    row = pl.BlockSpec((1, block, width), by_row)
    by_slot = pl.BlockSpec((nf, 1, short, width), lambda t, s: (0, by_item(t, s)[0], 0, 0))
    depth = 5 * width * width // (nf * ni * PACK)
    lse_spec = pl.BlockSpec((1, H // 2, 2, block), lambda t, s: (by_row(t, s)[0], 0, 0, by_row(t, s)[1]))
    return run(
        partial(
            cross_back_kernel,
            blocks=blocks,
            total=total,
            score_scale=score_scale,
            nf=nf,
            ni=ni,
            length_at=2 + 2 * items,
        ),
        "cross_bwd",
        (total + ni // FIN,),
        [row] * 7
        + [pl.BlockSpec((1, 9, width), by_item), pl.BlockSpec((1, slots, 2 * width), by_item), lse_spec]
        + [pl.BlockSpec((1, slots, width), by_item)]
        + [whole(weight.shape) for weight in (wo, wq, wco, wkv)]
        + any_spec(1),
        (table, g2, bb, cr, cq, att, ba, first, mod, kv, lse, text, wo, wq, wco, wkv, blocks_all),
        [row, row, by_slot, pl.BlockSpec((1, 4, width), by_item)] + any_spec(1),
        [struct(g2.shape, BF)] * 2
        + [struct((nf, items, short, width), BF), struct((items, 4, width), F32), struct(blocks_all.shape, BF)],
        scratch=[pltpu.VMEM((width, width), F32)] * 3
        + [pltpu.VMEM((width, 2 * width), F32), pltpu.VMEM((slots, 2 * width), F32)]
        + [pltpu.VMEM((2, FIN, nf, depth, PACK), BF), pltpu.SemaphoreType.DMA((2,))],
        aliases={16: 4},
        deps=deps,
        work=cost(
            items * count * (12 * width * width + 40 * slots * width), items * count * width * 24, items * H * count * slots
        ),
    )


def deal_call(table, jobs, per, name, deps=(), group=2):
    nf, _, _, width = jobs[0][0][0].shape
    items = nf * per
    at = 2 + 3 * per
    specs, args, counts = [], [], []
    for got, block, skip, _ in jobs:
        counts.append(len(got) * group)
        args += list(got) * group
        for part in range(group):
            if len(got) == 1:
                specs.append(
                    pl.BlockSpec(
                        (1, 1, block, width),
                        lambda t, s, part=part, skip=skip: (
                            s[at + t * group + part], 0, skip + s[at + items + t * group + part], 0
                        ),
                    )
                )
            else:
                specs += [
                    pl.BlockSpec((1, 1, block, width), lambda t, s, part=part: (s[at + t * group + part], 0, 0, 0))
                ] * len(got)

    def body(table, *refs):
        outs = refs[sum(counts) :]
        first = 0
        for count, out in zip(counts, outs):
            deal_kernel(table, *refs[first : first + count], out, at=at, items=items, group=group)
            first += count

    return run(
        body,
        name,
        (items // group,),
        specs,
        (table, *args),
        [pl.BlockSpec((group, job[1], width), lambda t, s: (t, 0, 0)) for job in jobs],
        [struct((items, job[1], width), job[3]) for job in jobs],
        deps=deps,
        work=cost(0, items * jobs[0][1] * width * 6),
    )


def small_call(kernel, name, args, out_shape, deps=()):
    return pl.pallas_call(
        kernel,
        in_specs=[pl.BlockSpec(arg.shape, lambda: (0,) * arg.ndim) for arg in args] + any_spec(len(deps)),
        out_specs=[pl.BlockSpec(out.shape, lambda: (0,) * len(out.shape)) for out in out_shape],
        out_shape=out_shape,
        compiler_params=params(),
        name=name,
    )(*args, *deps)


def exchange(blocks):
    return lax.all_to_all(blocks, "frames", 0, 0, tiled=True)


def swap(block, offset, nf):
    if offset == 0:
        return block
    return lax.ppermute(block, "frames", [(i, i ^ offset) for i in range(nf)])


def bits_of(count):
    return count.bit_length() - 1


class Sum:
    def __init__(self, keep, send, order, sizes):
        self.sizes = sizes
        ni, nf = sizes["items"], sizes["frames"]
        self.dims = [("items", bit) for bit in reversed(range(bits_of(ni)))]
        self.dims += [("frames", bit) for bit in reversed(range(1, bits_of(nf)))]
        shape = (2,) * len(self.dims) + keep.shape[2:]
        self.keep, self.send = keep.reshape(shape), send
        self.shape = shape
        self.steps = [("frames", 0)] + list(order)
        self.got = None

    def launch(self):
        name, bit = self.steps.pop(0)
        self.got = lax.ppermute(self.send, name, [(i, i ^ (1 << bit)) for i in range(self.sizes[name])])

    def land(self, deps=()):
        got = self.got.reshape(self.keep.shape)
        if not self.steps:
            return self.keep, got
        dim = self.dims.index(self.steps[0])
        self.dims.remove(self.steps[0])
        shape = self.keep.shape
        outer, inner = 2**dim, 2 ** (len(shape) - 3 - dim)
        view = (outer, 2, inner) + shape[-2:]
        out = struct((outer, inner) + shape[-2:], BF)
        source = pl.BlockSpec((1,) + view[1:], lambda t: (t, 0, 0, 0, 0))
        target = pl.BlockSpec((1,) + out.shape[1:], lambda t: (t, 0, 0, 0))
        self.keep, self.send = pl.pallas_call(
            land_kernel,
            grid=(outer,),
            in_specs=[source] * 2 + any_spec(len(deps)),
            out_specs=[target] * 2,
            out_shape=[out] * 2,
            compiler_params=params(),
            name="land",
        )(self.keep.reshape(view), got.reshape(view), *deps)
        left = shape[:dim] + shape[dim + 1 :]
        self.keep = self.keep.reshape(left)
        return None


def collect_items(rows, ni):
    for bit in range(bits_of(ni)):
        rows = jnp.concatenate([rows, lax.ppermute(rows, "items", [(i, i ^ (1 << bit)) for i in range(ni)])], 0)
    return rows


def total_here(blocks):
    flat = blocks.reshape((-1,) + blocks.shape[2:])
    return lax.psum_scatter(flat, ("items", "frames"), scatter_dimension=0, tiled=True)[0]


def items_whole(
    ni, nf, frames_in, cond, text, item_lengths, text_lengths, ada_weight, qkv_weight, out_weight,
    cross_q_weight, cross_kv_weight, cross_out_weight, up_weight, down_weight, cotangent,
):
    items, block, width = frames_in.shape
    per = items // nf
    ff = up_weight.shape[1]
    sizes = {"items": ni, "frames": nf}
    score_scale = (width // H) ** (-0.5)
    me = lax.axis_index("frames")
    row_item = lax.axis_index("items")
    x_first = [("items", bit) for bit in range(bits_of(ni))] + [("frames", bit) for bit in range(1, bits_of(nf))]

    table = start_call(jnp.stack([me, row_item]), item_lengths, text_lengths, items, nf)
    rows_first = exchange(gather_first_call(table, frames_in, nf))
    mixed_send, cot_send = gather_call(table, frames_in, text, cotangent, nf)

    cond_f = cond.astype(F32)
    low_cond = jax.nn.silu(cond_f).astype(BF)
    modulation = nn(low_cond, ada_weight)
    pick = table[2 : 2 + per, None] == jnp.arange(items, dtype=jnp.int32)[None, :]
    mod = jnp.sum(jnp.where(pick[:, :, None], modulation[None], 0.0), 1).reshape(per, 9, width)

    (mixed_send,) = gate_call([mixed_send], [rows_first, mod])
    mixed = exchange(mixed_send)
    kept = self_fwd_call(table, 0, rows_first, mod, qkv_weight, (), per, block, 1024, score_scale, [mixed_send])
    (cot_send,) = gate_call([cot_send], [mixed])
    cot = exchange(cot_send)
    kept = self_fwd_call(table, 1, mixed, mod, qkv_weight, kept, per, block, 1024, score_scale, [cot_send])
    rows, qkv, attended, self_lse = kept
    text_kv, text_rows, first, second, branch_a, branch_b, cross_q, crossed, cross_lse = cross_call(
        table, attended, rows, mod, mixed, text.shape[1], cross_kv_weight, out_weight, cross_q_weight, cross_out_weight,
        score_scale, 2 * block, [],
    )
    layer_send, g2, dmod_c, g_mlp = mlp_call(
        table, second, cot, mod, up_weight, down_weight, block, 768, nf, ni, []
    )
    layer_got = exchange(layer_send)
    g1, d_att, text_back, dmod_b, g_all = cross_back_call(
        table, g2, branch_b, crossed, cross_q, attended, branch_a, first, mod, text_kv, cross_lse, text_rows,
        out_weight, cross_q_weight, cross_out_weight, cross_kv_weight, g_mlp, score_scale, 2 * block, nf, ni, [],
    )
    sum_all = total_here(g_all)
    made_0, dmod_0, early = self_bwd_call(
        table, 0, qkv, attended, d_att, self_lse, rows, g1, mod, qkv_weight, None, text_back, 1024, score_scale, block, nf, ni,
        [],
    )
    got_0 = exchange(made_0)
    made_1, dmod_1, grad_keep, grad_send = self_bwd_call(
        table, 1, qkv, attended, d_att, self_lse, rows, g1, mod, qkv_weight, early, None, 1024, score_scale, block, nf, ni,
        [layer_got],
    )
    made_1, grad_send = gate_call([made_1, grad_send], [got_0])
    grad = Sum(grad_keep, grad_send, x_first, sizes)
    grad.launch()
    d_mod = jnp.concatenate([jnp.concatenate([dmod_0, dmod_1], 0), dmod_b, dmod_c], 1).reshape(per, 9 * width)
    ada_rows, ada_cols, cond_cols = width // ni, 9 * width // nf, width // nf
    high = d_mod.astype(BF)
    rest = (d_mod - high.astype(F32)).astype(BF)
    parts = nt(jnp.concatenate([high, rest], 0), ada_weight)
    parts = jnp.concatenate(
        [d_mod.reshape(per, nf, ada_cols), (parts[:per] + parts[per:]).reshape(per, nf, cond_cols)], 2
    ).transpose(1, 0, 2)
    parts = exchange(parts)
    grad.land([parts])
    grad.launch()
    (made_1,) = gate_call([made_1], [grad.send])
    got_1 = exchange(made_1)
    layer_out, text_grad = deal_call(
        table,
        [
            ([layer_got.reshape(nf, 1, per * block, width)], block, 0, BF),
            ([got_0[:, None]], text.shape[1], block // text.shape[1], F32),
        ],
        per,
        "deal_out",
        [grad.send],
    )
    grad.land([layer_out])
    grad.launch()
    (input_grad,) = deal_call(
        table, [([got_0[:, None], got_1[:, None]], block, 0, F32)], per, "deal_in", [grad.send]
    )
    grad.land([input_grad])
    grad.launch()
    (parts,) = gate_call([parts], [grad.send])
    parts = parts.reshape(items, ada_cols + cond_cols)
    at = 2 + 3 * per
    spot = table[at : at + items] * per + table[at + items : at + 2 * items]
    pick_row = spot[:, None] == jnp.arange(items, dtype=jnp.int32)[None, :]
    parts = jnp.sum(jnp.where(pick_row[:, :, None], parts[None], 0.0), 1)
    every = collect_items(jnp.concatenate([parts[:, :ada_cols].astype(BF), low_cond], 1), ni)
    grad_ada = lax.dot_general(
        lax.dynamic_slice(every, (0, ada_cols + row_item * ada_rows), (items * ni, ada_rows), allow_negative_indices=False),
        every[:, :ada_cols],
        (((0,), (0,)), ((), ())),
        preferred_element_type=F32,
    )
    cond_mine = lax.dynamic_slice(cond_f, (0, me * cond_cols), (items, cond_cols), allow_negative_indices=False)
    sigmoid_c = jax.nn.sigmoid(cond_mine)
    cond_grad = parts[:, ada_cols:] * (sigmoid_c * (1.0 + cond_mine * (1.0 - sigmoid_c)))

    while grad.steps:
        grad.land()
        grad.launch()
    square = struct((ada_rows, cond_cols), F32)
    grad_up, grad_down, grad_out, grad_cross_q, grad_cross_out, grad_cross_kv = small_call(
        finish_kernel,
        "finish",
        [sum_all],
        [struct((ada_rows, ff // nf), F32), struct((cond_cols, ff // ni), F32)]
        + [square] * 3
        + [struct((ada_rows, 2 * cond_cols), F32)],
    )
    (grad_qkv,) = small_call(
        finish_qkv_kernel, "finish_qkv", grad.land(), [struct((ada_rows, 3 * cond_cols), F32)], [grad_up]
    )
    return (
        layer_out,
        input_grad,
        text_grad,
        cond_grad,
        grad_ada,
        grad_qkv,
        grad_out,
        grad_cross_q,
        grad_cross_kv,
        grad_cross_out,
        grad_up,
        grad_down.T,
    )


def on_device(mesh, *args):
    ni, nf = mesh.shape["items"], mesh.shape["frames"]
    if nf == 4 and args[0].shape[0] == 2 * nf and args[0].shape[-1] == 768 and 768 % (32 * ni) == 0:
        return items_whole(ni, nf, *args)
    return frames_split(*args)


def solution(mesh):
    in_specs = (
        P("items", "frames", None),
        P("items", None),
        P("items", "frames", None),
        P("items"),
        P("items"),
        P(),
        P(),
        P(),
        P(),
        P(),
        P(),
        P(),
        P(),
        P("items", "frames", None),
    )
    out_specs = (
        P("items", "frames", None),
        P("items", "frames", None),
        P("items", "frames", None),
        P("items", "frames"),
        P("items", "frames"),
        P("items", "frames"),
        P("items", "frames"),
        P("items", "frames"),
        P("items", "frames"),
        P("items", "frames"),
        P("items", "frames"),
        P("items", "frames"),
    )
    return jax.shard_map(
        partial(on_device, mesh), mesh=mesh, in_specs=in_specs, out_specs=out_specs, check_vma=False
    )
```
